32 devices in a mesh: mode: 4 (over y, core), cell: 8 (over z, x).
Axes of the slice: x: 2, y: 2, z: 4, core: 2. Of those that a mesh axis runs over, the one named last changes fastest.
Arguments:
- adjoint: float32 [256, 4608], P('cell', 'mode'), may hold values from -6 to 6
- source: float32 [256, 4608], P('cell', 'mode'), may hold values from -6 to 6
- collision: bfloat16 [4, 8, 144, 4608], P(None, 'cell', None, 'mode'), may hold values from -0.033570226 to 1.0335702
- speed: float32 [4608], P('mode'), may hold values from 0.2 to 1
- direction: int32 [96], P('mode'), may hold values from 0 to 1
- labels: int32 [256], P('cell'), may hold values from 0 to 7
- conductance: float32 [8], replicated, may hold values from 0.3 to 1
Outputs:
- adjoint_out: float32 [256, 4608], P('cell', 'mode')
The draws below stay inside these ranges and needn't reach their ends.
All inputs are finite; a program needn't handle non-finite values.
Results may differ from the reference program's by a relative error of at most 0.005.
Values may be sent and summed in bfloat16 or wider, within the bound.
No kernel may reach another device: no remote copies, remote signals or barrier semaphores. Data moves between devices by JAX's collectives and lax.ppermute only.
A program may use at most 64 MiB of HBM per device.

```python
import math
import jax
import jax.numpy as jnp
from jax import lax

BRANCH = 48
ITERS = 2
NMAT = 8
SUBW = 144
MODES = 4608
MBLK = 1152
QPTS = 96
CELLS = 256
N_MODE = 4
N_CELL = 8


def draw_collision(key, part):
    first, second = jax.random.split(jax.random.fold_in(key, 11), 2)
    spread = jax.random.normal(first, (MODES, MODES), jnp.float32)
    limit = 1.6 / math.sqrt(MODES)
    spread = jnp.clip(spread * (0.4 / math.sqrt(MODES)), -limit, limit)
    rates = jnp.exp(jax.random.uniform(second, (MODES,), jnp.float32, math.log(0.3), math.log(1.0)))
    diag_index = jnp.arange(MODES, dtype=jnp.int32)
    spread = spread.at[diag_index, diag_index].add(rates)
    return spread.reshape(MODES // MBLK, MBLK // SUBW, SUBW, MODES).astype(jnp.bfloat16)


def with_ends(entries, own_key, least, largest):
    shape = entries.shape
    spot = [jax.random.randint(jax.random.fold_in(own_key, axis), (), 0, shape[axis]) for axis in range(len(shape))]
    entries = entries.at[tuple(spot)].set(least)
    longest = shape.index(max(shape))
    spot[longest] = (spot[longest] + 1) % shape[longest]
    return entries.at[tuple(spot)].set(largest)


def block_scale(key, shape, cuts, smallest, high):
    gain, own = 1.0, jax.random.fold_in(key, 6)
    for position, parts in cuts:
        draws = jnp.exp(jax.random.uniform(jax.random.fold_in(own, position), (parts,), jnp.float32, smallest / len(cuts), high / len(cuts)))
        gain = gain * jnp.repeat(draws, shape[position] // parts).reshape([-1 if axis == position else 1 for axis in range(len(shape))])
    return gain


def noise(key, dims, scale, bound, cuts=(), kind=jnp.bfloat16):
    loudness = block_scale(key, dims, cuts, -0.22, 0.18) if cuts else 1.0
    result = jax.random.normal(key, dims, jnp.float32) * scale * loudness
    return jnp.minimum(jnp.maximum(result, -bound), bound).astype(kind)


def setup_inputs(seed: int = 0) -> dict:
    arg_keys = jax.random.split(jax.random.key(seed), 8)
    return {
        "adjoint": noise(arg_keys[0], (CELLS, MODES), 1.0, 6.0, ((0, 8), (1, 4)), jnp.float32),
        "source": noise(arg_keys[1], (CELLS, MODES), 1.0, 6.0, ((0, 8), (1, 4)), jnp.float32),
        "collision": draw_collision(jax.random.fold_in(arg_keys[7], 71), 0),
        "speed": jnp.clip(jnp.exp(math.log(1.0) - 1.609438 * jax.random.uniform(arg_keys[3], (MODES,), jnp.float32) ** block_scale(arg_keys[3], (MODES,), ((0, 4),), -0.2, 0.2)), 0.2, 1.0),
        "direction": with_ends(jax.random.randint(arg_keys[4], (QPTS,), 0, 2), jax.random.fold_in(arg_keys[4], 1), 0, 1).astype(jnp.int32),
        "labels": with_ends(jax.random.randint(arg_keys[5], (CELLS,), 0, NMAT), jax.random.fold_in(arg_keys[5], 1), 0, NMAT - 1).astype(jnp.int32),
        "conductance": jnp.clip(jax.random.uniform(arg_keys[6], (NMAT,), jnp.float32, 0.3, 1.0), 0.3, 1.0),
    }


relax_factor = 0.5


def material_scale(labels, conductance):
    matches = labels[:, None] == jnp.arange(conductance.shape[0], dtype=jnp.int32)[None, :]
    return jnp.sum(jnp.where(matches, conductance[None, :], 0.0), axis=1)


def upwind_pick(padded, sign_mode):
    return jnp.where(sign_mode[None, :] > 0, padded[2:], padded[:-2])


def reference(adjoint, source, collision, speed, direction, labels, conductance):
    conduct = material_scale(labels, conductance)
    sign_mode = jnp.repeat(2 * direction - 1, BRANCH)
    transport_rate = speed[None, :] * conduct[:, None]
    state = adjoint
    for sweep in range(ITERS):
        rounded = state.astype(jnp.bfloat16).reshape(CELLS, N_MODE, N_CELL, SUBW)

        def add_group(running, group):
            kernel_rows = lax.dynamic_index_in_dim(collision, group, 1, keepdims=False).reshape(N_MODE * SUBW, MODES)
            columns = lax.dynamic_index_in_dim(rounded, group, 2, keepdims=False).reshape(CELLS, N_MODE * SUBW)
            partial_value = jnp.dot(columns, kernel_rows, preferred_element_type=jnp.float32).astype(jnp.bfloat16)
            partial_value = lax.optimization_barrier(partial_value)
            return running + partial_value.astype(jnp.float32), None

        scattering, _ = lax.scan(add_group, jnp.zeros((CELLS, MODES), jnp.float32), jnp.arange(N_CELL, dtype=jnp.int32))
        padded = jnp.pad(state, ((1, 1), (0, 0)))
        transport = transport_rate * (state - upwind_pick(padded, sign_mode))
        state = state + relax_factor * (source - transport - scattering)
    return state
```

```python
import jax
import jax.numpy as jnp
from jax import lax
from jax.sharding import PartitionSpec as P

BRANCH = 48
ITERS = 2


relax_factor = 0.5


def material_scale(labels, conductance):
    matches = labels[:, None] == jnp.arange(conductance.shape[0], dtype=jnp.int32)[None, :]
    return jnp.sum(jnp.where(matches, conductance[None, :], 0.0), axis=1)


def pieces(array, count):
    found = []
    for _ in range(count):
        head = lax.reduce_precision(array, exponent_bits=8, mantissa_bits=7)
        found.append(head.astype(jnp.bfloat16))
        array = array - head
    return found


def upwind_change(state, sign_mode):
    edge = jnp.zeros((state.shape[0], 1), state.dtype)
    after = jnp.concatenate([state[:, 1:], edge], axis=1)
    before = jnp.concatenate([edge, state[:, :-1]], axis=1)
    return state - jnp.where(sign_mode[:, None] > 0, after, before)


def contract(lhs, rhs):
    return lax.dot_general(
        lhs, rhs, (((0,), (0,)), ((), ())), preferred_element_type=jnp.float32
    )


def one_hot_rows(rows, columns, first):
    row = lax.broadcasted_iota(jnp.int32, (rows, columns), 0)
    column = lax.broadcasted_iota(jnp.int32, (rows, columns), 1)
    return (column == row + first).astype(jnp.bfloat16)


def shards(adjoint, source, collision, speed, direction, labels, conductance):
    rows, width = adjoint.shape
    groups = lax.axis_size("cell")
    part = width // groups
    cells = rows * groups
    me = lax.axis_index("cell")
    kernel = collision.reshape(-1, width)

    scale = jnp.stack(pieces(material_scale(labels, conductance), 3), axis=1)
    blocks = adjoint.astype(jnp.bfloat16).reshape(rows, groups, part).transpose(1, 0, 2)
    sent = jnp.concatenate(
        [blocks, jnp.broadcast_to(scale[None], (groups,) + scale.shape)], axis=2
    )
    got = lax.all_to_all(sent, "cell", split_axis=0, concat_axis=0, tiled=True)
    got = got.reshape(cells, part + 3)
    kappa = jnp.sum(got[:, part:].astype(jnp.float32), axis=1)
    start = got[:, :part].T

    sign_mode = jnp.repeat(2 * direction - 1, BRANCH)
    sign_mode = lax.dynamic_slice_in_dim(sign_mode, me * part, part)
    own_speed = lax.dynamic_slice_in_dim(speed, me * part, part)
    half_rate = relax_factor * own_speed[:, None] * kappa[None, :]

    full = lax.all_gather(start, "mode", axis=0, tiled=True)
    base = pieces(adjoint + relax_factor * source, 2)
    place = one_hot_rows(rows, cells, me * rows)
    terms = contract(kernel, full * jnp.bfloat16(-relax_factor))
    terms = terms + contract(jnp.concatenate(base, axis=0), jnp.concatenate([place, place], axis=0))
    moved = lax.all_to_all(
        terms.astype(jnp.bfloat16).reshape(groups, part, cells), "cell", split_axis=0, concat_axis=0, tiled=True
    )
    start = start.astype(jnp.float32)
    state = jnp.sum(moved.astype(jnp.float32), axis=0) - half_rate * upwind_change(start, sign_mode)

    full = lax.all_gather(state.astype(jnp.bfloat16), "mode", axis=0, tiled=True)
    kept = pieces(state - half_rate * upwind_change(state, sign_mode), 2)
    place = one_hot_rows(part, width, me * part)
    terms = contract(full * jnp.bfloat16(-relax_factor), kernel)
    terms = terms + contract(jnp.concatenate(kept, axis=0), jnp.concatenate([place, place], axis=0))
    moved = lax.all_to_all(
        terms.astype(jnp.bfloat16).reshape(groups, rows, width), "cell", split_axis=0, concat_axis=0, tiled=True
    )
    return jnp.sum(moved.astype(jnp.float32), axis=0) + relax_factor * source


def solution(mesh):
    in_specs = (
        P("cell", "mode"),
        P("cell", "mode"),
        P(None, "cell", None, "mode"),
        P("mode"),
        P("mode"),
        P("cell"),
        P(),
    )
    out_specs = P("cell", "mode")
    return jax.shard_map(shards, mesh=mesh, in_specs=in_specs, out_specs=out_specs, check_vma=False)
```

```python
import jax
import jax.numpy as jnp
from jax import lax
from jax.sharding import Mesh, PartitionSpec as P

BRANCH = 48
ITERS = 2


relax_factor = 0.5


def material_scale(labels, conductance):
    matches = labels[:, None] == jnp.arange(conductance.shape[0], dtype=jnp.int32)[None, :]
    return jnp.sum(jnp.where(matches, conductance[None, :], 0.0), axis=1)


def pieces(array, count):
    found = []
    for _ in range(count):
        head = lax.reduce_precision(array, exponent_bits=8, mantissa_bits=7)
        found.append(head.astype(jnp.bfloat16))
        array = array - head
    return found


def contract(lhs, rhs):
    return lax.dot_general(
        lhs, rhs, (((0,), (0,)), ((), ())), preferred_element_type=jnp.float32
    )


def one_hot_rows(rows, columns, first):
    row = lax.broadcasted_iota(jnp.int32, (rows, columns), 0)
    column = lax.broadcasted_iota(jnp.int32, (rows, columns), 1)
    return (column == row + first).astype(jnp.bfloat16)


def cell_of(place, lines, rows):
    half = lines * rows
    pair, line, row = place // half, (place % half) // rows, place % rows
    return (2 * line + pair) * rows + row


def neighbours(state, sign_mode, lines, rows, first, count):
    cells = state.shape[1]
    source = cell_of(lax.broadcasted_iota(jnp.int32, (cells, count), 0), lines, rows)
    target = cell_of(first + lax.broadcasted_iota(jnp.int32, (cells, count), 1), lines, rows)
    after = jnp.dot(state, (source == target + 1).astype(jnp.bfloat16), preferred_element_type=jnp.float32)
    before = jnp.dot(state, (source == target - 1).astype(jnp.bfloat16), preferred_element_type=jnp.float32)
    return jnp.where(sign_mode[:, None] > 0, after, before)


def shards(adjoint, source, collision, speed, direction, labels, conductance):
    rows, width = adjoint.shape
    lines, pairs = lax.axis_size("line"), lax.axis_size("pair")
    modes = lax.axis_size("mode")
    groups = lines * pairs
    part = width // groups
    cells = rows * groups
    half = rows * lines
    line, pair = lax.axis_index("line"), lax.axis_index("pair")
    me = line * pairs + pair
    kernel = collision.reshape(-1, width)
    other_kernel = lax.ppermute(kernel, "pair", [(0, 1), (1, 0)])

    scale = jnp.stack(pieces(material_scale(labels, conductance), 3), axis=1)
    blocks = adjoint.astype(jnp.bfloat16).reshape(rows, groups, part).transpose(1, 0, 2)
    sent = jnp.concatenate(
        [blocks, jnp.broadcast_to(scale[None], (groups,) + scale.shape)], axis=2
    )
    got = lax.all_to_all(sent, ("line", "pair"), split_axis=0, concat_axis=0, tiled=True)
    got = got.reshape(lines, pairs, rows, part + 3).transpose(1, 0, 2, 3).reshape(cells, part + 3)
    kappa = jnp.sum(got[:, part:].astype(jnp.float32), axis=1)
    start = got[:, :part].T

    sign_mode = jnp.repeat(2 * direction - 1, BRANCH)
    own_sign = lax.dynamic_slice_in_dim(sign_mode, me * part, part)
    own_speed = lax.dynamic_slice_in_dim(speed, me * part, part)
    half_rate = relax_factor * own_speed[:, None] * kappa[None, :]

    full = lax.all_gather(start, "mode", axis=0, tiled=True)
    base = pieces(adjoint + relax_factor * source, 2)
    place = one_hot_rows(rows, cells, (pair * lines + line) * rows)
    terms = contract(kernel, full * jnp.bfloat16(-relax_factor))
    terms = terms + contract(jnp.concatenate(base, axis=0), jnp.concatenate([place, place], axis=0))
    moved = lax.all_to_all(
        terms.astype(jnp.bfloat16).reshape(groups, part, cells), ("line", "pair"), split_axis=0, concat_axis=0, tiled=True
    )
    change = start.astype(jnp.float32) - neighbours(start, own_sign, lines, rows, 0, cells)
    state = jnp.sum(moved.astype(jnp.float32), axis=0) - half_rate * change

    full = lax.all_gather(state.astype(jnp.bfloat16), ("pair", "mode"), axis=0, tiled=True)
    full = full.reshape(pairs, modes, part, cells)
    both = lax.dynamic_index_in_dim(full, lax.axis_index("mode"), 1, keepdims=False).reshape(pairs * part, cells)
    sign_mode = lax.dynamic_slice_in_dim(sign_mode, line * pairs * part, pairs * part)
    speed = lax.dynamic_slice_in_dim(speed, line * pairs * part, pairs * part)
    kappa = lax.dynamic_slice_in_dim(kappa, pair * half, half)
    mine = lax.dynamic_slice_in_dim(both, pair * half, half, axis=1).astype(jnp.float32)
    change = mine - neighbours(both, sign_mode, lines, rows, pair * half, half)
    kept = pieces(mine - relax_factor * speed[:, None] * kappa[None, :] * change, 2)
    place = one_hot_rows(pairs * part, width, line * pairs * part)
    full = lax.dynamic_slice_in_dim(full, pair * half, half, axis=3) * jnp.bfloat16(-relax_factor)
    full = full.reshape(pairs, modes * part, half)
    terms = contract(lax.dynamic_index_in_dim(full, pair, 0, keepdims=False), kernel)
    terms = terms + contract(lax.dynamic_index_in_dim(full, 1 - pair, 0, keepdims=False), other_kernel)
    terms = terms + contract(jnp.concatenate(kept, axis=0), jnp.concatenate([place, place], axis=0))
    moved = lax.all_to_all(
        terms.astype(jnp.bfloat16).reshape(lines, rows, width), "line", split_axis=0, concat_axis=0, tiled=True
    )
    return jnp.sum(moved.astype(jnp.float32), axis=0) + relax_factor * source


def solution(mesh):
    modes, groups = mesh.shape["mode"], mesh.shape["cell"]
    mesh = Mesh(mesh.devices.reshape(modes, groups // 2, 2), ("mode", "line", "pair"))
    cell = ("line", "pair")
    in_specs = (
        P(cell, "mode"),
        P(cell, "mode"),
        P(None, cell, None, "mode"),
        P("mode"),
        P("mode"),
        P(cell),
        P(),
    )
    out_specs = P(cell, "mode")
    return jax.shard_map(shards, mesh=mesh, in_specs=in_specs, out_specs=out_specs, check_vma=False)
```

```python
import jax
import jax.numpy as jnp
from jax import lax
from jax.sharding import PartitionSpec as P

BRANCH = 48
ITERS = 2


relax_factor = 0.5


def material_scale(labels, conductance):
    matches = labels[:, None] == jnp.arange(conductance.shape[0], dtype=jnp.int32)[None, :]
    return jnp.sum(jnp.where(matches, conductance[None, :], 0.0), axis=1)


def pieces(array, count):
    found = []
    for _ in range(count):
        head = lax.reduce_precision(array, exponent_bits=8, mantissa_bits=7)
        found.append(head.astype(jnp.bfloat16))
        array = array - head
    return found


def upwind_change(state, sign_mode):
    edge = jnp.zeros((state.shape[0], 1), state.dtype)
    after = jnp.concatenate([state[:, 1:], edge], axis=1)
    before = jnp.concatenate([edge, state[:, :-1]], axis=1)
    return state - jnp.where(sign_mode[:, None] > 0, after, before)


def contract(lhs, rhs):
    return lax.dot_general(
        lhs, rhs, (((0,), (0,)), ((), ())), preferred_element_type=jnp.float32
    )


def one_hot_rows(rows, columns, first):
    row = lax.broadcasted_iota(jnp.int32, (rows, columns), 0)
    column = lax.broadcasted_iota(jnp.int32, (rows, columns), 1)
    return (column == row + first).astype(jnp.bfloat16)


def exchange_sum(terms, axis):
    count = terms.shape[0]
    me = lax.axis_index(axis)
    blocks = terms.astype(jnp.bfloat16)
    arrived = []
    for step in range(count - 1, 0, -1):
        if count & (count - 1):
            target = (me + step) % count
            pairs = [(i, (i + step) % count) for i in range(count)]
        else:
            target = me ^ step
            pairs = [(i, i ^ step) for i in range(count)]
        block = lax.dynamic_index_in_dim(blocks, target, 0, keepdims=False)
        arrived.append(lax.ppermute(block, axis, pairs))
    total = lax.dynamic_index_in_dim(blocks, me, 0, keepdims=False).astype(jnp.float32)
    for block in arrived:
        total = total + block.astype(jnp.float32)
    return total


def shards(adjoint, source, collision, speed, direction, labels, conductance):
    rows, width = adjoint.shape
    groups = lax.axis_size("cell")
    part = width // groups
    cells = rows * groups
    me = lax.axis_index("cell")
    kernel = collision.reshape(-1, width)

    scale = jnp.stack(pieces(material_scale(labels, conductance), 3), axis=1)
    blocks = adjoint.astype(jnp.bfloat16).reshape(rows, groups, part).transpose(1, 0, 2)
    sent = jnp.concatenate(
        [blocks, jnp.broadcast_to(scale[None], (groups,) + scale.shape)], axis=2
    )
    got = lax.all_to_all(sent, "cell", split_axis=0, concat_axis=0, tiled=True)
    got = got.reshape(cells, part + 3)
    kappa = jnp.sum(got[:, part:].astype(jnp.float32), axis=1)
    start = got[:, :part].T

    base = pieces(adjoint + relax_factor * source, 2)
    flipped = jnp.concatenate([kernel, *base], axis=0).T
    place = one_hot_rows(rows, cells, me * rows)

    sign_mode = jnp.repeat(2 * direction - 1, BRANCH)
    sign_mode = lax.dynamic_slice_in_dim(sign_mode, me * part, part)
    own_speed = lax.dynamic_slice_in_dim(speed, me * part, part)
    half_rate = relax_factor * own_speed[:, None] * kappa[None, :]

    full = lax.all_gather(start, "mode", axis=0, tiled=True)
    inputs = jnp.concatenate([full * jnp.bfloat16(-relax_factor), place, place], axis=0)
    terms = jnp.dot(flipped, inputs, preferred_element_type=jnp.float32)
    moved = exchange_sum(terms.reshape(groups, part, cells), "cell")
    state = moved - half_rate * upwind_change(start.astype(jnp.float32), sign_mode)

    full = lax.all_gather(state.astype(jnp.bfloat16), "mode", axis=0, tiled=True)
    kept = pieces(state - half_rate * upwind_change(state, sign_mode), 2)
    place = one_hot_rows(part, width, me * part)
    terms = contract(full * jnp.bfloat16(-relax_factor), kernel)
    terms = terms + contract(jnp.concatenate(kept, axis=0), jnp.concatenate([place, place], axis=0))
    return exchange_sum(terms.reshape(groups, rows, width), "cell") + relax_factor * source


def solution(mesh):
    in_specs = (
        P("cell", "mode"),
        P("cell", "mode"),
        P(None, "cell", None, "mode"),
        P("mode"),
        P("mode"),
        P("cell"),
        P(),
    )
    out_specs = P("cell", "mode")
    return jax.shard_map(shards, mesh=mesh, in_specs=in_specs, out_specs=out_specs, check_vma=False)
```

```python
import functools

import jax
import jax.numpy as jnp
from jax import lax
from jax.experimental import pallas as pl
from jax.experimental.pallas import tpu as pltpu
from jax.sharding import Mesh, PartitionSpec as P

BRANCH = 48
ITERS = 2


relax_factor = 0.5
VMEM = pl.BlockSpec(memory_space=pltpu.VMEM)
SMEM = pl.BlockSpec(memory_space=pltpu.SMEM)
bf16, f32 = jnp.bfloat16, jnp.float32


def split(array):
    head = array.astype(bf16)
    return head, (array - head.astype(f32)).astype(bf16)


def call(body, out, in_specs, scratch=(), flops=0, bytes_accessed=0):
    return pl.pallas_call(
        body,
        out_shape=out,
        in_specs=in_specs,
        out_specs=jax.tree.map(lambda _: VMEM, out),
        scratch_shapes=list(scratch),
        compiler_params=pltpu.CompilerParams(vmem_limit_bytes=56 * 2**20),
        cost_estimate=pl.CostEstimate(flops=flops, bytes_accessed=bytes_accessed, transcendentals=0),
    )


def pack_kernel(labels, conductance, adjoint, out):
    groups, rows, span = out.shape
    part = span - 3
    row = lax.broadcasted_iota(jnp.int32, (rows, 1), 0)
    kappa = jnp.zeros((rows, 1), f32)
    for cell in range(rows):
        kappa = jnp.where(row == cell, conductance[labels[cell]], kappa)
    first, rest = split(kappa)
    second, third = split(kappa - first.astype(f32))
    del rest
    for group in range(groups):
        out[group, :, :part] = adjoint[:, group * part : (group + 1) * part].astype(bf16)
        out[group, :, part : part + 1] = first
        out[group, :, part + 1 : part + 2] = second
        out[group, :, part + 2 :] = third


def first_kernel(index, flipped, base, full, place, start, rate, sign, kappa, out, terms):
    groups, span, half = out.shape
    part, cells = start.shape
    rows = place.shape[0] // 2
    terms[...] = jnp.dot(flipped[...], full[...] * bf16(-relax_factor), preferred_element_type=f32)
    terms[...] += jnp.dot(base[...], place[...], preferred_element_type=f32)
    lam = start[...].astype(f32)
    spot = lax.broadcasted_iota(jnp.int32, (1, cells), 1)
    inner = lax.rem(spot, rows)
    early = spot < half
    step = pltpu.roll(lam, cells - 1, 1)
    skip = pltpu.roll(lam, half + rows - 1, 1)
    back = pltpu.roll(lam, half - 1, 1)
    after = jnp.where(inner < rows - 1, step, jnp.where(early, skip, jnp.where(spot == cells - 1, 0.0, back)))
    step = pltpu.roll(lam, 1, 1)
    skip = pltpu.roll(lam, half + 1, 1)
    back = pltpu.roll(lam, cells - (half + rows - 1), 1)
    before = jnp.where(inner > 0, step, jnp.where(early, jnp.where(spot == 0, 0.0, skip), back))
    change = lam - jnp.where(sign[...] > 0, after, before)
    own = pl.ds(pl.multiple_of(index[0] * part, 16), part)
    terms[own, :] -= rate[...] * kappa[...] * change
    for line in range(groups // 2):
        for pair in range(2):
            block = terms[line * span : (line + 1) * span, pair * half : (pair + 1) * half]
            out[2 * line + pair] = block.astype(bf16)


def second_kernel(index, flipped, other, full, lam, beyond, rate, sign, kappa, out, inputs, terms):
    lines, rows, width = out.shape
    modes, span, half = full.shape
    part = span // 2
    line, pair = index[1], index[2]
    for mode in range(modes):
        mine = pl.ds(pl.multiple_of(pair * part, 16), part)
        inputs[0, mode * part : (mode + 1) * part, :] = full[mode, mine, :] * bf16(-relax_factor)
        theirs = pl.ds(pl.multiple_of((1 - pair) * part, 16), part)
        inputs[1, mode * part : (mode + 1) * part, :] = full[mode, theirs, :] * bf16(-relax_factor)
    terms[...] = jnp.dot(flipped[...], inputs[0], preferred_element_type=f32)
    terms[...] += jnp.dot(other[...], inputs[1], preferred_element_type=f32)
    state = lam[...]
    far = beyond[...].astype(f32)
    spot = lax.broadcasted_iota(jnp.int32, (1, half), 1)
    inner = lax.rem(spot, rows)
    close = pltpu.roll(far, rows - 1, 1)
    away = jnp.where(spot == half - 1, 0.0, pltpu.roll(far, half - 1, 1))
    after = jnp.where(inner < rows - 1, pltpu.roll(state, half - 1, 1), jnp.where(pair == 0, close, away))
    close = pltpu.roll(far, half - (rows - 1), 1)
    away = jnp.where(spot == 0, 0.0, pltpu.roll(far, 1, 1))
    before = jnp.where(inner > 0, pltpu.roll(state, 1, 1), jnp.where(pair == 0, away, close))
    change = state - jnp.where(sign[...] > 0, after, before)
    own = pl.ds(pl.multiple_of(line * span, 16), span)
    terms[own, :] += state - rate[...] * kappa[...] * change
    result = terms[...].T.astype(bf16)
    for target in range(lines):
        out[target] = result[target * rows : (target + 1) * rows, :]


def shards(adjoint, source, collision, speed, direction, labels, conductance):
    rows, width = adjoint.shape
    lines, pairs, modes = lax.axis_size("line"), lax.axis_size("pair"), lax.axis_size("mode")
    groups = lines * pairs
    part = width // groups
    span = part * pairs
    cells = rows * groups
    half = rows * lines
    depth = modes * part
    line, pair = lax.axis_index("line"), lax.axis_index("pair")
    me = line * pairs + pair
    index = jnp.stack([me, line, pair]).astype(jnp.int32)
    kernel = collision.reshape(depth, width)

    sent = call(pack_kernel, jax.ShapeDtypeStruct((groups, rows, part + 3), bf16), [SMEM, SMEM, VMEM])(
        labels, conductance, adjoint
    )
    got = lax.all_to_all(sent, ("line", "pair"), split_axis=0, concat_axis=0, tiled=True)
    got = got.reshape(lines, pairs, rows, part + 3).transpose(1, 0, 2, 3).reshape(cells, part + 3)
    kappa = jnp.sum(got[:, part:].astype(f32), axis=1)
    start = got[:, :part].T

    adjoint, source, kernel, sent = lax.optimization_barrier((adjoint, source, kernel, sent))
    base = adjoint + relax_factor * source
    head = lax.reduce_precision(base, exponent_bits=8, mantissa_bits=7)
    base = jnp.concatenate([head.astype(bf16), (base - head).astype(bf16)], axis=0).T
    flipped = lax.optimization_barrier(kernel.T)
    other = lax.ppermute(flipped, "pair", [(0, 1), (1, 0)])
    row = lax.broadcasted_iota(jnp.int32, (rows, cells), 0)
    column = lax.broadcasted_iota(jnp.int32, (rows, cells), 1)
    place = (column == row + (pair * lines + line) * rows).astype(bf16)
    place = jnp.concatenate([place, place], axis=0)
    sign_mode = jnp.broadcast_to((2 * direction - 1)[:, None], (direction.shape[0], BRANCH)).reshape(-1, 1)
    half_speed = (relax_factor * speed)[:, None]
    own_sign = lax.dynamic_slice_in_dim(sign_mode, me * part, part)
    own_speed = lax.dynamic_slice_in_dim(half_speed, me * part, part)
    line_sign = lax.dynamic_slice_in_dim(sign_mode, line * span, span)
    line_speed = lax.dynamic_slice_in_dim(half_speed, line * span, span)

    full = lax.all_gather(start, "mode", axis=0, tiled=True)
    terms = call(
        first_kernel,
        jax.ShapeDtypeStruct((groups, span, half), bf16),
        [SMEM] + [VMEM] * 8,
        [pltpu.VMEM((width, cells), f32)],
    )(index, flipped, base, full, place, start, own_speed, own_sign, kappa[None, :])
    moved = lax.all_to_all(terms, ("line", "pair"), split_axis=0, concat_axis=0, tiled=True)
    state = jnp.sum(moved.astype(f32), axis=0)

    rounded = state.astype(bf16)
    beyond = lax.ppermute(rounded, "pair", [(0, 1), (1, 0)])
    full = lax.all_gather(rounded, "mode", axis=0, tiled=False)
    kappa = lax.dynamic_slice_in_dim(kappa, pair * half, half)[None, :]
    terms = call(
        second_kernel,
        jax.ShapeDtypeStruct((lines, rows, width), bf16),
        [SMEM] + [VMEM] * 8,
        [pltpu.VMEM((2, depth, half), bf16), pltpu.VMEM((width, half), f32)],
    )(index, flipped, other, full, state, beyond, line_speed, line_sign, kappa)
    moved = lax.all_to_all(terms, "line", split_axis=0, concat_axis=0, tiled=True)
    return jnp.sum(moved.astype(f32), axis=0) + relax_factor * source


def solution(mesh):
    modes, groups = mesh.shape["mode"], mesh.shape["cell"]
    mesh = Mesh(mesh.devices.reshape(modes, groups // 2, 2), ("mode", "line", "pair"))
    cell = ("line", "pair")
    in_specs = (
        P(cell, "mode"),
        P(cell, "mode"),
        P(None, cell, None, "mode"),
        P("mode"),
        P("mode"),
        P(cell),
        P(),
    )
    out_specs = P(cell, "mode")
    return jax.shard_map(shards, mesh=mesh, in_specs=in_specs, out_specs=out_specs, check_vma=False)
```

```python
import math

import jax
import jax.numpy as jnp
from jax import lax
from jax.experimental import pallas as pl
from jax.experimental.pallas import tpu as pltpu
from jax.sharding import Mesh, PartitionSpec as P

BRANCH = 48
ITERS = 2


relax_factor = 0.5
VMEM = pl.BlockSpec(memory_space=pltpu.VMEM)
SMEM = pl.BlockSpec(memory_space=pltpu.SMEM)
bf16, f32 = jnp.bfloat16, jnp.float32
EXTRA = 16


def split(array):
    head = array.astype(bf16)
    return head, (array - head.astype(f32)).astype(bf16)


def padded_bytes(shape, dtype):
    size = jnp.dtype(dtype).itemsize
    if len(shape) < 2:
        return 4096
    sublanes = 8 * 4 // size
    rows, lanes = -(-shape[-2] // sublanes) * sublanes, -(-shape[-1] // 128) * 128
    return math.prod(shape[:-2]) * rows * lanes * size


def call(body, out, scalars, arrays, scratch=(), flops=0):
    outs = jax.tree.leaves(out)
    bytes_ = sum(padded_bytes(a.shape, a.dtype) for a in (*arrays, *outs))
    held = sum(padded_bytes(shape, dtype) for shape, dtype in scratch)
    return pl.pallas_call(
        body,
        out_shape=out,
        in_specs=[SMEM] * len(scalars) + [VMEM] * len(arrays),
        out_specs=jax.tree.map(lambda _: VMEM, out),
        scratch_shapes=[pltpu.VMEM(shape, dtype) for shape, dtype in scratch],
        compiler_params=pltpu.CompilerParams(vmem_limit_bytes=int(1.5 * (bytes_ + held)) + 4 * 2**20),
        cost_estimate=pl.CostEstimate(flops=flops, bytes_accessed=bytes_, transcendentals=0),
    )(*scalars, *arrays)


def pack_kernel(labels, conductance, adjoint, out):
    lines, rows, columns = out.shape
    span = columns - EXTRA
    row = lax.broadcasted_iota(jnp.int32, (rows, EXTRA), 0)
    column = lax.broadcasted_iota(jnp.int32, (rows, EXTRA), 1)
    kappa = jnp.zeros((rows, EXTRA), f32)
    for cell in range(rows):
        kappa = jnp.where(row == cell, conductance[labels[cell]], kappa)
    first, _ = split(kappa)
    rest = kappa - first.astype(f32)
    second, third = split(rest)
    scale = jnp.where(column == 0, first.astype(f32), 0.0) + jnp.where(column == 1, second.astype(f32), 0.0)
    scale = (scale + jnp.where(column == 2, third.astype(f32), 0.0)).astype(bf16)
    for line in range(lines):
        out[line, :, :span] = adjoint[:, line * span : (line + 1) * span].astype(bf16)
        out[line, :, span:] = scale


def flip_kernel(index, collision, adjoint, source, keep, send):
    modes, part, width = collision.shape
    pair = index[1]
    base = split(adjoint[...] + relax_factor * source[...])
    rows = jnp.concatenate([collision[...].reshape(modes * part, width), *base], axis=0).T
    for line in range(width // (2 * part)):
        first = rows[2 * line * part : (2 * line + 1) * part]
        second = rows[(2 * line + 1) * part : (2 * line + 2) * part]
        spot = slice(line * part, (line + 1) * part)
        keep[spot, :] = jnp.where(pair == 0, first, second)
        send[spot, :] = jnp.where(pair == 0, second, first)


def first_kernel(index, keep, other, full, out, inputs):
    lines, part, cells = out.shape
    _, modes, _, half = full.shape
    line, pair = index[0], index[1]
    depth = modes * part
    rows = half // lines
    row = lax.broadcasted_iota(jnp.int32, (rows, cells), 0)
    column = lax.broadcasted_iota(jnp.int32, (rows, cells), 1)
    for group in range(2):
        for mode in range(modes):
            for side in range(2):
                block = full[side, mode, group * part : (group + 1) * part, :] * bf16(-relax_factor)
                inputs[group, mode * part : (mode + 1) * part, side * half : (side + 1) * half] = block
        place = (column == row + (group * half + line * rows)).astype(f32).astype(bf16)
        inputs[group, depth : depth + rows, :] = place
        inputs[group, depth + rows :, :] = place
    terms = jnp.dot(keep[...], inputs[pair], preferred_element_type=f32)
    terms += jnp.dot(other[...], inputs[1 - pair], preferred_element_type=f32)
    for target in range(lines):
        out[target] = terms[target * part : (target + 1) * part].astype(bf16)


def shifted(own, far, pair, rows):
    half = own.shape[1]
    spot = lax.broadcasted_iota(jnp.int32, (1, half), 1)
    inner = lax.rem(spot, rows)
    close = pltpu.roll(far, rows - 1, 1)
    away = jnp.where(spot == half - 1, 0.0, pltpu.roll(far, half - 1, 1))
    after = jnp.where(inner < rows - 1, pltpu.roll(own, half - 1, 1), jnp.where(pair == 0, close, away))
    close = pltpu.roll(far, half - (rows - 1), 1)
    away = jnp.where(spot == 0, 0.0, pltpu.roll(far, 1, 1))
    before = jnp.where(inner > 0, pltpu.roll(own, 1, 1), jnp.where(pair == 0, away, close))
    return after, before


def transport_kernel(index, full, rate, sign, out, kappa_out):
    part, cells = out.shape
    _, _, span, half = full.shape
    span -= EXTRA
    mode, pair = index[2], index[1]
    lines = kappa_out.shape[0]
    mine = pl.ds(pl.multiple_of(pair * part, 16), part)
    lam = [full[side, mode, mine, :].astype(f32) for side in range(2)]
    kappa = [jnp.sum(full[side, 0, span:, :].astype(f32), axis=0, keepdims=True) for side in range(2)]
    for side in range(2):
        after, before = shifted(lam[side], lam[1 - side], side, half // lines)
        change = lam[side] - jnp.where(sign[...] > 0, after, before)
        out[:, side * half : (side + 1) * half] = rate[...] * kappa[side] * change
    kappa_out[...] = jnp.broadcast_to(jnp.where(pair == 0, kappa[0], kappa[1]), kappa_out.shape)


def second_kernel(index, keep, send, near, rest, full, rate, sign, kappa, out, inputs, terms):
    lines, rows, width = out.shape
    _, modes, part, _ = full.shape
    half = lines * rows
    depth = modes * part
    line, pair, own_mode = index[0], index[1], index[2]
    mine = pl.ds(pl.multiple_of(pair * half, 128), half)
    theirs = pl.ds(pl.multiple_of((1 - pair) * half, 128), half)
    for group in range(2):
        for mode in range(modes):
            inputs[group, mode * part : (mode + 1) * part, :] = full[group, mode, :, mine] * bf16(-relax_factor)
    own, other = inputs[pair], inputs[1 - pair]
    same = jnp.dot(keep[:, :depth], own, preferred_element_type=f32)
    same += jnp.dot(near[:, :depth], other, preferred_element_type=f32)
    cross = jnp.dot(send[:, :depth], own, preferred_element_type=f32)
    cross += jnp.dot(rest[:, :depth], other, preferred_element_type=f32)
    for target in range(lines):
        spot = slice(target * part, (target + 1) * part)
        terms[target, pair] = same[spot]
        terms[target, 1 - pair] = cross[spot]
    for group in range(2):
        state = full[group, own_mode, :, mine].astype(f32)
        far = full[group, own_mode, :, theirs].astype(f32)
        after, before = shifted(state, far, pair, rows)
        spot = slice(group * part, (group + 1) * part)
        change = state - jnp.where(sign[spot, :] > 0, after, before)
        terms[line, group] += state - rate[spot, :] * kappa[:1, :] * change
    result = terms[...].reshape(width, half).T.astype(bf16)
    for target in range(lines):
        out[target] = result[target * rows : (target + 1) * rows, :]


def shards(adjoint, source, collision, speed, direction, labels, conductance):
    rows, width = adjoint.shape
    lines, pairs, modes = lax.axis_size("line"), lax.axis_size("pair"), lax.axis_size("mode")
    part = width // (lines * pairs)
    span = part * pairs
    half = rows * lines
    cells = half * pairs
    depth = modes * part
    line, pair, mode = lax.axis_index("line"), lax.axis_index("pair"), lax.axis_index("mode")
    index = jnp.stack([line, pair, mode]).astype(jnp.int32)
    swap = [(0, 1), (1, 0)]
    shape = jax.ShapeDtypeStruct

    sent = call(pack_kernel, shape((lines, rows, span + EXTRA), bf16), [labels, conductance], [adjoint])
    got = lax.all_to_all(sent, "line", split_axis=0, concat_axis=0, tiled=True)

    adjoint, collision, sent = lax.optimization_barrier((adjoint, collision, sent))
    half_block = shape((width // 2, depth + 2 * rows), bf16)
    keep, send = call(
        flip_kernel, (half_block, half_block), [index], [collision.reshape(modes, part, width), adjoint, source]
    )
    near = lax.ppermute(send, "pair", swap)

    full = lax.all_gather(got.reshape(half, span + EXTRA).T, ("pair", "mode"), axis=0, tiled=False)
    full = full.reshape(pairs, modes, span + EXTRA, half)
    terms = call(
        first_kernel,
        shape((lines, part, cells), bf16),
        [index],
        [keep, near, full],
        [((2, depth + 2 * rows, cells), bf16)],
        flops=2 * width * depth * cells,
    )
    moved = lax.all_to_all(terms, "line", split_axis=0, concat_axis=0, tiled=True)

    keep_late, speed, direction, terms = lax.optimization_barrier((keep, speed, direction, terms))
    rest = lax.ppermute(keep_late, "pair", swap)
    sign = jnp.broadcast_to((2 * direction - 1)[:, None], (direction.shape[0], BRANCH)).reshape(-1, 1)
    rate = (relax_factor * speed)[:, None]
    line_sign = lax.dynamic_slice_in_dim(sign, line * span, span)
    line_rate = lax.dynamic_slice_in_dim(rate, line * span, span)
    own_sign = lax.dynamic_slice_in_dim(line_sign, pair * part, part)
    own_rate = lax.dynamic_slice_in_dim(line_rate, pair * part, part)
    transport, kappa = call(
        transport_kernel, (shape((part, cells), f32), shape((lines, half), f32)), [index], [full, own_rate, own_sign]
    )
    state = (jnp.sum(moved.astype(f32), axis=0) - transport).astype(bf16)

    full = lax.all_gather(state, ("pair", "mode"), axis=0, tiled=False).reshape(pairs, modes, part, cells)
    terms = call(
        second_kernel,
        shape((lines, rows, width), bf16),
        [index],
        [keep, send, near, rest, full, line_rate, line_sign, kappa],
        [((2, depth, half), bf16), ((lines, 2, part, half), f32)],
        flops=2 * 2 * width * depth * half,
    )
    moved = lax.all_to_all(terms, "line", split_axis=0, concat_axis=0, tiled=True)
    return jnp.sum(moved.astype(f32), axis=0) + relax_factor * source


def solution(mesh):
    modes, groups = mesh.shape["mode"], mesh.shape["cell"]
    mesh = Mesh(mesh.devices.reshape(modes, groups // 2, 2), ("mode", "line", "pair"))
    cell = ("line", "pair")
    in_specs = (
        P(cell, "mode"),
        P(cell, "mode"),
        P(None, cell, None, "mode"),
        P("mode"),
        P("mode"),
        P(cell),
        P(),
    )
    out_specs = P(cell, "mode")
    return jax.shard_map(shards, mesh=mesh, in_specs=in_specs, out_specs=out_specs, check_vma=False)
```

```python
import math

import jax
import jax.numpy as jnp
from jax import lax
from jax.experimental import pallas as pl
from jax.experimental.pallas import tpu as pltpu
from jax.sharding import Mesh, PartitionSpec as P

BRANCH = 48
ITERS = 2


relax_factor = 0.5
VMEM = pl.BlockSpec(memory_space=pltpu.VMEM)
SMEM = pl.BlockSpec(memory_space=pltpu.SMEM)
bf16, f32 = jnp.bfloat16, jnp.float32
EXTRA = 16
TARGETS = 3


def split(array):
    head = array.astype(bf16)
    return head, (array - head.astype(f32)).astype(bf16)


def padded_bytes(shape, dtype):
    size = jnp.dtype(dtype).itemsize
    if len(shape) < 2:
        return 4096
    sublanes = 8 * 4 // size
    rows, lanes = -(-shape[-2] // sublanes) * sublanes, -(-shape[-1] // 128) * 128
    return math.prod(shape[:-2]) * rows * lanes * size


def call(body, out, scalars, arrays, scratch=(), flops=0, own_copies=False):
    outs = jax.tree.leaves(out)
    bytes_ = sum(padded_bytes(a.shape, a.dtype) for a in (*arrays, *outs))
    held = sum(padded_bytes(shape, dtype) for shape, dtype in scratch)
    scratch = [pltpu.VMEM(shape, dtype) for shape, dtype in scratch]
    if own_copies:
        scratch += [pltpu.VMEM(a.shape, a.dtype) for a in arrays] + [pltpu.SemaphoreType.DMA((len(arrays),))]
    return pl.pallas_call(
        body,
        out_shape=out,
        in_specs=[SMEM] * len(scalars) + [pl.BlockSpec(memory_space=pl.ANY) if own_copies else VMEM] * len(arrays),
        out_specs=jax.tree.map(lambda _: VMEM, out),
        scratch_shapes=scratch,
        compiler_params=pltpu.CompilerParams(vmem_limit_bytes=int(1.5 * (bytes_ + held)) + 4 * 2**20),
        cost_estimate=pl.CostEstimate(flops=flops, bytes_accessed=bytes_, transcendentals=0),
    )(*scalars, *arrays)


def fetch(sources, targets, semaphores):
    copies = [
        pltpu.make_async_copy(source, target, semaphores.at[k])
        for k, (source, target) in enumerate(zip(sources, targets))
    ]
    for copy in copies:
        copy.start()
    for copy in copies:
        copy.wait()


def column_of(row, first, count, each=1):
    wide = row.shape[1]
    place = first + lax.broadcasted_iota(jnp.int32, (count, wide), 0)
    start = lax.broadcasted_iota(jnp.int32, (count, wide), 1) * each
    hit = jnp.logical_and(place >= start, place < start + each)
    return jnp.sum(jnp.where(hit, row, 0.0), axis=1, keepdims=True)


def pack_kernel(index, adjoint_, labels_, conductance_, *refs):
    lines = len(refs) - 5
    outs, (blocks, adjoint, labels, conductance, semaphores) = refs[:lines], refs[lines:]
    fetch((adjoint_, labels_, conductance_), (adjoint, labels, conductance), semaphores)
    rows, columns = outs[0].shape
    span = adjoint.shape[1] // lines
    label = column_of(labels[...].astype(f32), 0, rows)
    kinds = lax.broadcasted_iota(jnp.int32, (rows, conductance.shape[1]), 1).astype(f32)
    kappa = jnp.sum(jnp.where(kinds == label, conductance[...], 0.0), axis=1, keepdims=True)
    first, _ = split(kappa)
    second, third = split(kappa - first.astype(f32))
    column = lax.broadcasted_iota(jnp.int32, (rows, columns - span), 1)
    scale = jnp.where(column == 0, first.astype(f32), 0.0) + jnp.where(column == 1, second.astype(f32), 0.0)
    scale = (scale + jnp.where(column == 2, third.astype(f32), 0.0)).astype(bf16)
    for line in range(lines):
        blocks[line, :, :span] = adjoint[:, line * span : (line + 1) * span].astype(bf16)
        blocks[line, :, span:] = scale
    for step in range(lines):
        outs[step][...] = blocks[index[TARGETS + step]]


def turn_kernel(index, *refs):
    *arrived, out, blocks = refs
    for step, block in enumerate(arrived):
        blocks[index[TARGETS + len(arrived) + step]] = block[...]
    lines, rows, columns = blocks.shape
    out[...] = blocks[...].reshape(lines * rows, columns).T[: out.shape[0]]


def flip_kernel(index, collision_, adjoint_, source_, keep, send, collision, adjoint, source, semaphores):
    fetch((collision_, adjoint_, source_), (collision, adjoint, source), semaphores)
    modes, part, width = collision.shape
    pair = index[1]
    base = split(adjoint[...] + relax_factor * source[...])
    rows = jnp.concatenate([collision[...].reshape(modes * part, width), *base], axis=0).T
    for line in range(width // (2 * part)):
        first = rows[2 * line * part : (2 * line + 1) * part]
        second = rows[(2 * line + 1) * part : (2 * line + 2) * part]
        spot = slice(line * part, (line + 1) * part)
        keep[spot, :] = jnp.where(pair == 0, first, second)
        send[spot, :] = jnp.where(pair == 0, second, first)


def first_kernel(index, keep, other, full, *refs):
    *outs, inputs, terms = refs
    lines = len(outs)
    part, cells = outs[0].shape
    _, modes, _, half = full.shape
    line, pair = index[0], index[1]
    depth = modes * part
    rows = half // lines
    row = lax.broadcasted_iota(jnp.int32, (rows, cells), 0)
    column = lax.broadcasted_iota(jnp.int32, (rows, cells), 1)
    for group in range(2):
        for mode in range(modes):
            for side in range(2):
                block = full[side, mode, group * part : (group + 1) * part, :] * bf16(-relax_factor)
                inputs[group, mode * part : (mode + 1) * part, side * half : (side + 1) * half] = block
        place = (column == row + (group * half + line * rows)).astype(f32).astype(bf16)
        inputs[group, depth : depth + rows, :] = place
        inputs[group, depth + rows :, :] = place
    result = jnp.dot(keep[...], inputs[pair], preferred_element_type=f32)
    result += jnp.dot(other[...], inputs[1 - pair], preferred_element_type=f32)
    terms[...] = result.reshape(terms.shape)
    for step, out in enumerate(outs):
        out[...] = terms[index[TARGETS + step]].astype(out.dtype)


def shifted(own, far, pair, rows):
    half = own.shape[1]
    spot = lax.broadcasted_iota(jnp.int32, (1, half), 1)
    inner = lax.rem(spot, rows)
    close = pltpu.roll(far, rows - 1, 1)
    away = jnp.where(spot == half - 1, 0.0, pltpu.roll(far, half - 1, 1))
    after = jnp.where(inner < rows - 1, pltpu.roll(own, half - 1, 1), jnp.where(pair == 0, close, away))
    close = pltpu.roll(far, half - (rows - 1), 1)
    away = jnp.where(spot == 0, 0.0, pltpu.roll(far, 1, 1))
    before = jnp.where(inner > 0, pltpu.roll(own, 1, 1), jnp.where(pair == 0, away, close))
    return after, before


def transport_kernel(index, full, speed, direction, out, kappa_out, rate_out, sign_out):
    part, cells = out.shape
    _, _, span, half = full.shape
    span -= EXTRA
    lines = kappa_out.shape[0]
    line, pair, mode = index[0], index[1], index[2]
    rate_out[...] = relax_factor * column_of(speed[...], line * span, span)
    sign_out[...] = 2.0 * column_of(direction[...].astype(f32), line * span, span, BRANCH) - 1.0
    mine = pl.ds(pl.multiple_of(pair * part, 16), part)
    rate, sign = rate_out[mine, :], sign_out[mine, :]
    lam = [full[side, mode, mine, :].astype(f32) for side in range(2)]
    kappa = [jnp.sum(full[side, 0, span:, :].astype(f32), axis=0, keepdims=True) for side in range(2)]
    for side in range(2):
        after, before = shifted(lam[side], lam[1 - side], side, half // lines)
        change = lam[side] - jnp.where(sign > 0, after, before)
        out[:, side * half : (side + 1) * half] = rate * kappa[side] * change
    kappa_out[...] = jnp.broadcast_to(jnp.where(pair == 0, kappa[0], kappa[1]), kappa_out.shape)


def second_kernel(index, keep, send, near, rest, full, rate, sign, kappa, *refs):
    *outs, inputs, terms, flat = refs
    lines = len(outs)
    rows, width = outs[0].shape
    _, modes, part, _ = full.shape
    half = lines * rows
    depth = modes * part
    line, pair, own_mode = index[0], index[1], index[2]
    mine = pl.ds(pl.multiple_of(pair * half, 128), half)
    theirs = pl.ds(pl.multiple_of((1 - pair) * half, 128), half)
    for group in range(2):
        for mode in range(modes):
            inputs[group, mode * part : (mode + 1) * part, :] = full[group, mode, :, mine] * bf16(-relax_factor)
    own, other = inputs[pair], inputs[1 - pair]
    same = jnp.dot(keep[:, :depth], own, preferred_element_type=f32)
    same += jnp.dot(near[:, :depth], other, preferred_element_type=f32)
    cross = jnp.dot(send[:, :depth], own, preferred_element_type=f32)
    cross += jnp.dot(rest[:, :depth], other, preferred_element_type=f32)
    for target in range(lines):
        spot = slice(target * part, (target + 1) * part)
        terms[target, pair] = same[spot]
        terms[target, 1 - pair] = cross[spot]
    for group in range(2):
        state = full[group, own_mode, :, mine].astype(f32)
        far = full[group, own_mode, :, theirs].astype(f32)
        after, before = shifted(state, far, pair, rows)
        spot = slice(group * part, (group + 1) * part)
        change = state - jnp.where(sign[spot, :] > 0, after, before)
        terms[line, group] += state - rate[spot, :] * kappa[:1, :] * change
    flat[...] = terms[...].reshape(width, half).T
    for step, out in enumerate(outs):
        start = pl.multiple_of(index[TARGETS + step] * rows, 16)
        out[...] = flat[pl.ds(start, rows), :].astype(out.dtype)


def line_steps(lines):
    if lines & (lines - 1):
        return [[(i, (i + step) % lines) for i in range(lines)] for step in range(lines)]
    return [[(i, i ^ step) for i in range(lines)] for step in range(lines)]


def exchange(blocks, steps):
    return [blocks[0]] + [lax.ppermute(block, "line", pairs) for block, pairs in zip(blocks[1:], steps[1:])]


def total(blocks):
    result = blocks[0].astype(f32)
    for block in blocks[1:]:
        result = result + block.astype(f32)
    return result


def shards(adjoint, source, collision, speed, direction, labels, conductance):
    rows, width = adjoint.shape
    lines, pairs, modes = lax.axis_size("line"), lax.axis_size("pair"), lax.axis_size("mode")
    part = width // (lines * pairs)
    span = part * pairs
    half = rows * lines
    cells = half * pairs
    depth = modes * part
    line, pair, mode = lax.axis_index("line"), lax.axis_index("pair"), lax.axis_index("mode")
    steps = line_steps(lines)
    targets = [line] + [jnp.array([t for _, t in pairs], jnp.int32)[line] for pairs in steps[1:]]
    origins = [line] + [jnp.array([o for o, _ in sorted(pairs, key=lambda p: p[1])], jnp.int32)[line] for pairs in steps[1:]]
    if lines & (lines - 1) == 0:
        targets = origins = [line ^ step for step in range(lines)]
    index = jnp.stack([line, pair, mode, *targets, *origins]).astype(jnp.int32)
    swap = [(0, 1), (1, 0)]
    shape = jax.ShapeDtypeStruct

    columns = -(-(span + EXTRA) // 128) * 128
    sent = call(
        pack_kernel,
        [shape((rows, columns), bf16)] * lines,
        [index],
        [adjoint, labels[None, :], conductance[None, :]],
        [((lines, rows, columns), bf16)],
        own_copies=True,
    )
    got = exchange(sent, steps)

    collision, sent = lax.optimization_barrier((collision, sent))
    half_block = shape((width // 2, depth + 2 * rows), bf16)
    keep, send = call(
        flip_kernel,
        [half_block, half_block],
        [index],
        [collision.reshape(modes, part, width), adjoint, source],
        own_copies=True,
    )
    near = lax.ppermute(send, "pair", swap)

    start = call(turn_kernel, shape((span + EXTRA, half), bf16), [index], got, [((lines, rows, columns), bf16)])
    full = lax.all_gather(start, ("pair", "mode"), axis=0, tiled=False).reshape(pairs, modes, span + EXTRA, half)
    terms = call(
        first_kernel,
        [shape((part, cells), f32)] + [shape((part, cells), bf16)] * (lines - 1),
        [index],
        [keep, near, full],
        [((2, depth + 2 * rows, cells), bf16), ((lines, part, cells), f32)],
        flops=2 * width * depth * cells,
    )
    moved = exchange(terms, steps)

    keep_late, full, terms = lax.optimization_barrier((keep, full, terms))
    rest = lax.ppermute(keep_late, "pair", swap)
    transport, kappa, rate, sign = call(
        transport_kernel,
        [shape((part, cells), f32), shape((lines, half), f32), shape((span, 1), f32), shape((span, 1), f32)],
        [index],
        [full, speed[None, :], direction[None, :]],
    )
    state = (total(moved) - transport).astype(bf16)

    full = lax.all_gather(state, ("pair", "mode"), axis=0, tiled=False).reshape(pairs, modes, part, cells)
    terms = call(
        second_kernel,
        [shape((rows, width), f32)] + [shape((rows, width), bf16)] * (lines - 1),
        [index],
        [keep, send, near, rest, full, rate, sign, kappa],
        [((2, depth, half), bf16), ((lines, 2, part, half), f32), ((half, width), f32)],
        flops=2 * 2 * width * depth * half,
    )
    return total(exchange(terms, steps)) + relax_factor * source


def solution(mesh):
    modes, groups = mesh.shape["mode"], mesh.shape["cell"]
    mesh = Mesh(mesh.devices.reshape(modes, groups // 2, 2), ("mode", "line", "pair"))
    cell = ("line", "pair")
    in_specs = (
        P(cell, "mode"),
        P(cell, "mode"),
        P(None, cell, None, "mode"),
        P("mode"),
        P("mode"),
        P(cell),
        P(),
    )
    out_specs = P(cell, "mode")
    return jax.shard_map(shards, mesh=mesh, in_specs=in_specs, out_specs=out_specs, check_vma=False)
```

```python
import math

import jax
import jax.numpy as jnp
from jax import lax
from jax.experimental import pallas as pl
from jax.experimental.pallas import tpu as pltpu
from jax.sharding import Mesh, PartitionSpec as P

BRANCH = 48
ITERS = 2


relax_factor = 0.5
VMEM = pl.BlockSpec(memory_space=pltpu.VMEM)
SMEM = pl.BlockSpec(memory_space=pltpu.SMEM)
HBM = pl.BlockSpec(memory_space=pltpu.HBM)
bf16, f32 = jnp.bfloat16, jnp.float32
EXTRA = 16


def split(array):
    head = array.astype(bf16)
    return head, (array - head.astype(f32)).astype(bf16)


def padded_bytes(shape, dtype):
    size = jnp.dtype(dtype).itemsize
    if len(shape) < 2:
        return 4096
    sublanes = 8 * 4 // size
    rows, lanes = -(-shape[-2] // sublanes) * sublanes, -(-shape[-1] // 128) * 128
    return math.prod(shape[:-2]) * rows * lanes * size


def call(body, out, scalars, arrays, scratch=(), flops=0, own_copies=False):
    outs = jax.tree.leaves(out)
    bytes_ = sum(padded_bytes(a.shape, a.dtype) for a in (*arrays, *outs))
    held = sum(padded_bytes(shape, dtype) for shape, dtype in scratch)
    scratch = [pltpu.VMEM(shape, dtype) for shape, dtype in scratch]
    if own_copies:
        scratch += [pltpu.VMEM(a.shape, a.dtype) for a in arrays] + [pltpu.SemaphoreType.DMA((len(arrays),))]
    return pl.pallas_call(
        body,
        out_shape=out,
        in_specs=[SMEM] * len(scalars) + [HBM if own_copies else VMEM] * len(arrays),
        out_specs=jax.tree.map(lambda _: VMEM, out),
        scratch_shapes=scratch,
        compiler_params=pltpu.CompilerParams(vmem_limit_bytes=int(1.5 * (bytes_ + held)) + 4 * 2**20),
        cost_estimate=pl.CostEstimate(flops=flops, bytes_accessed=bytes_, transcendentals=0),
    )(*scalars, *arrays)


def fetch(sources, targets, semaphores):
    copies = [
        pltpu.make_async_copy(source, target, semaphores.at[k])
        for k, (source, target) in enumerate(zip(sources, targets))
    ]
    for copy in copies:
        copy.start()
    for copy in copies:
        copy.wait()


def column_of(row, first, count, each=1):
    wide = row.shape[1]
    place = first + lax.broadcasted_iota(jnp.int32, (count, wide), 0)
    start = lax.broadcasted_iota(jnp.int32, (count, wide), 1) * each
    hit = jnp.logical_and(place >= start, place < start + each)
    return jnp.sum(jnp.where(hit, row, 0.0), axis=1, keepdims=True)


def upwind_change(state, sign):
    cells = state.shape[1]
    spot = lax.broadcasted_iota(jnp.int32, (1, cells), 1)
    after = jnp.where(spot == cells - 1, 0.0, pltpu.roll(state, cells - 1, 1))
    before = jnp.where(spot == 0, 0.0, pltpu.roll(state, 1, 1))
    return state - jnp.where(sign > 0, after, before)


def pack_kernel(index, adjoint_, labels_, conductance_, *refs):
    groups = len(refs) - 5
    outs, (blocks, adjoint, labels, conductance, semaphores) = refs[:groups], refs[groups:]
    fetch((adjoint_, labels_, conductance_), (adjoint, labels, conductance), semaphores)
    rows, columns = outs[0].shape
    part = adjoint.shape[1] // groups
    label = column_of(labels[...].astype(f32), 0, rows)
    kinds = lax.broadcasted_iota(jnp.int32, (rows, conductance.shape[1]), 1).astype(f32)
    kappa = jnp.sum(jnp.where(kinds == label, conductance[...], 0.0), axis=1, keepdims=True)
    first, _ = split(kappa)
    second, third = split(kappa - first.astype(f32))
    column = lax.broadcasted_iota(jnp.int32, (rows, columns - part), 1)
    scale = jnp.where(column == 0, first.astype(f32), 0.0) + jnp.where(column == 1, second.astype(f32), 0.0)
    scale = (scale + jnp.where(column == 2, third.astype(f32), 0.0)).astype(bf16)
    for group in range(groups):
        blocks[group, :, :part] = adjoint[:, group * part : (group + 1) * part].astype(bf16)
        blocks[group, :, part:] = scale
    for step in range(groups):
        outs[step][...] = blocks[index[step]]


def turn_kernel(index, *refs):
    *arrived, out, kappa, blocks = refs
    groups = len(arrived)
    for step, block in enumerate(arrived):
        blocks[index[groups + step]] = block[...]
    _, rows, columns = blocks.shape
    part = out.shape[0]
    turned = blocks[...].reshape(groups * rows, columns).T
    out[...] = turned[:part]
    scale = jnp.sum(turned[part:].astype(f32), axis=0, keepdims=True)
    kappa[...] = jnp.broadcast_to(scale, kappa.shape)


def flip_kernel(collision_, adjoint_, source_, out, collision, adjoint, source, semaphores):
    fetch((collision_, adjoint_, source_), (collision, adjoint, source), semaphores)
    base = split(adjoint[...] + relax_factor * source[...])
    out[...] = jnp.concatenate([collision[...], *base], axis=0).T


def first_kernel(index, flipped, full, *refs):
    *outs, inputs, terms = refs
    lines = len(outs) // 2
    groups, part, cells = terms.shape
    depth = full.shape[0]
    pair = index[2 * groups + lines + 1]
    rows = cells // groups
    inputs[:depth, :] = full[...] * bf16(-relax_factor)
    row = lax.broadcasted_iota(jnp.int32, (rows, cells), 0)
    column = lax.broadcasted_iota(jnp.int32, (rows, cells), 1)
    place = (column == row + index[0] * rows).astype(f32).astype(bf16)
    inputs[depth : depth + rows, :] = place
    inputs[depth + rows :, :] = place
    terms[...] = jnp.dot(flipped[...], inputs[...], preferred_element_type=f32).reshape(terms.shape)
    for step in range(lines):
        target = index[2 * groups + step]
        outs[step][...] = terms[2 * target + pair]
        outs[lines + step][...] = terms[2 * target + 1 - pair].astype(bf16)


def transport_kernel(index, start, kappa, speed, direction, out, rate_out, sign_out):
    part, _ = out.shape
    first = index[0] * part
    rate_out[...] = relax_factor * column_of(speed[...], first, part) * kappa[:1, :]
    sign_out[...] = 2.0 * column_of(direction[...].astype(f32), first, part, BRANCH) - 1.0
    out[...] = rate_out[...] * upwind_change(start[...].astype(f32), sign_out[...])


def second_kernel(index, flipped, full, state, rate, sign, *refs):
    *outs, terms, blocks = refs
    lines = len(outs) // 2
    groups, part, cells = terms.shape
    depth = full.shape[0]
    pair = index[2 * groups + lines + 1]
    inputs = full[...] * bf16(-relax_factor)
    terms[...] = jnp.dot(flipped[:, :depth], inputs, preferred_element_type=f32).reshape(terms.shape)
    terms[index[0]] += state[...] - rate[...] * upwind_change(state[...], sign[...])
    blocks[...] = terms[...].reshape(groups * part, cells).T.reshape(blocks.shape)
    for step in range(lines):
        target = index[2 * groups + step]
        outs[step][...] = blocks[2 * target + pair]
        outs[lines + step][...] = blocks[2 * target + 1 - pair].astype(bf16)


def steps_of(count):
    if count & (count - 1):
        return [[(i, (i + step) % count) for i in range(count)] for step in range(count)]
    return [[(i, i ^ step) for i in range(count)] for step in range(count)]


def partners(pairs, me):
    to = jnp.array([target for _, target in sorted(pairs)], jnp.int32)
    origin = jnp.array([source for source, _ in sorted(pairs, key=lambda pair: pair[1])], jnp.int32)
    return to[me], origin[me]


def reduce_over_cells(blocks, steps):
    lines = len(steps)
    near = [None] * lines
    for step in reversed(range(lines)):
        near[step] = lax.ppermute(blocks[lines + step], "pair", [(0, 1), (1, 0)])
    sums = [blocks[step] + near[step].astype(f32) for step in range(lines)]
    result = sums[0]
    for step in reversed(range(1, lines)):
        result = result + lax.ppermute(sums[step].astype(bf16), "line", steps[step]).astype(f32)
    return result


def shards(adjoint, source, collision, speed, direction, labels, conductance):
    rows, width = adjoint.shape
    lines, pairs, modes = lax.axis_size("line"), lax.axis_size("pair"), lax.axis_size("mode")
    groups = lines * pairs
    part = width // groups
    cells = rows * groups
    depth = modes * part
    line, pair = lax.axis_index("line"), lax.axis_index("pair")
    me = line * pairs + pair
    line_steps, group_steps = steps_of(lines), steps_of(groups)
    if groups & (groups - 1):
        found = [partners(step, me) for step in group_steps]
        near = [partners(step, line)[0] for step in line_steps]
    else:
        found = [(me ^ step, me ^ step) for step in range(groups)]
        near = [line ^ step for step in range(lines)]
    index = jnp.stack([to for to, _ in found] + [origin for _, origin in found] + near + [line, pair])
    index = index.astype(jnp.int32)
    shape = jax.ShapeDtypeStruct

    columns = -(-(part + EXTRA) // 128) * 128
    sent = call(
        pack_kernel,
        [shape((rows, columns), bf16)] * groups,
        [index],
        [adjoint, labels[None, :], conductance[None, :]],
        [((groups, rows, columns), bf16)],
        own_copies=True,
    )
    got = [sent[0]] + [
        lax.ppermute(block, ("line", "pair"), step) for block, step in zip(sent[1:], group_steps[1:])
    ]

    collision, sent = lax.optimization_barrier((collision, sent))
    flipped = call(
        flip_kernel,
        shape((width, depth + 2 * rows), bf16),
        [],
        [collision.reshape(depth, width), adjoint, source],
        own_copies=True,
    )

    start, kappa = call(
        turn_kernel, [shape((part, cells), bf16), shape((8, cells), f32)], [index], got, [((groups, rows, columns), bf16)]
    )
    full = lax.all_gather(start, "mode", axis=0, tiled=True)
    terms = call(
        first_kernel,
        [shape((part, cells), f32)] * lines + [shape((part, cells), bf16)] * lines,
        [index],
        [flipped, full],
        [((depth + 2 * rows, cells), bf16), ((groups, part, cells), f32)],
        flops=2 * width * depth * cells,
    )
    start, kappa, terms = lax.optimization_barrier((start, kappa, terms))
    transport, rate, sign = call(
        transport_kernel,
        [shape((part, cells), f32), shape((part, cells), f32), shape((part, 1), f32)],
        [index],
        [start, kappa, speed[None, :], direction[None, :]],
    )
    state = reduce_over_cells(terms, line_steps) - transport

    full = lax.all_gather(state.astype(bf16), "mode", axis=0, tiled=True)
    terms = call(
        second_kernel,
        [shape((rows, width), f32)] * lines + [shape((rows, width), bf16)] * lines,
        [index],
        [flipped, full, state, rate, sign],
        [((groups, part, cells), f32), ((groups, rows, width), f32)],
        flops=2 * width * depth * cells,
    )
    return reduce_over_cells(terms, line_steps) + relax_factor * source


def solution(mesh):
    modes, groups = mesh.shape["mode"], mesh.shape["cell"]
    mesh = Mesh(mesh.devices.reshape(modes, groups // 2, 2), ("mode", "line", "pair"))
    cell = ("line", "pair")
    in_specs = (
        P(cell, "mode"),
        P(cell, "mode"),
        P(None, cell, None, "mode"),
        P("mode"),
        P("mode"),
        P(cell),
        P(),
    )
    out_specs = P(cell, "mode")
    return jax.shard_map(shards, mesh=mesh, in_specs=in_specs, out_specs=out_specs, check_vma=False)
```

```python
import math

import jax
import jax.numpy as jnp
from jax import lax
from jax.experimental import pallas as pl
from jax.experimental.pallas import tpu as pltpu
from jax.sharding import Mesh, PartitionSpec as P

BRANCH = 48
ITERS = 2


relax_factor = 0.5
VMEM = pl.BlockSpec(memory_space=pltpu.VMEM)
SMEM = pl.BlockSpec(memory_space=pltpu.SMEM)
HBM = pl.BlockSpec(memory_space=pltpu.HBM)
bf16, f32 = jnp.bfloat16, jnp.float32
EXTRA = 16
ME, PAIR, TARGETS = 0, 1, 2


def split(array):
    head = array.astype(bf16)
    return head, (array - head.astype(f32)).astype(bf16)


def padded_bytes(shape, dtype):
    size = jnp.dtype(dtype).itemsize
    if len(shape) < 2:
        return 4096
    sublanes = 8 * 4 // size
    rows, lanes = -(-shape[-2] // sublanes) * sublanes, -(-shape[-1] // 128) * 128
    return math.prod(shape[:-2]) * rows * lanes * size


def call(body, out, scalars, arrays, scratch=(), flops=0, own_copies=False):
    outs = jax.tree.leaves(out)
    bytes_ = sum(padded_bytes(a.shape, a.dtype) for a in (*arrays, *outs))
    held = sum(padded_bytes(shape, dtype) for shape, dtype in scratch)
    scratch = [pltpu.VMEM(shape, dtype) for shape, dtype in scratch]
    if own_copies:
        scratch += [pltpu.VMEM(a.shape, a.dtype) for a in arrays] + [pltpu.SemaphoreType.DMA((len(arrays),))]
    return pl.pallas_call(
        body,
        out_shape=out,
        in_specs=[SMEM] * len(scalars) + [HBM if own_copies else VMEM] * len(arrays),
        out_specs=jax.tree.map(lambda _: VMEM, out),
        scratch_shapes=scratch,
        compiler_params=pltpu.CompilerParams(
            vmem_limit_bytes=56 * 2**20 if own_copies else int(1.5 * (bytes_ + held)) + 4 * 2**20
        ),
        cost_estimate=pl.CostEstimate(flops=flops, bytes_accessed=bytes_, transcendentals=0),
    )(*scalars, *arrays)


def fetch(sources, targets, semaphores):
    copies = [
        pltpu.make_async_copy(source, target, semaphores.at[k])
        for k, (source, target) in enumerate(zip(sources, targets))
    ]
    for copy in copies:
        copy.start()
    for copy in copies:
        copy.wait()


def column_of(row, first, count, each=1):
    wide = row.shape[1]
    place = first + lax.broadcasted_iota(jnp.int32, (count, wide), 0)
    start = lax.broadcasted_iota(jnp.int32, (count, wide), 1) * each
    hit = jnp.logical_and(place >= start, place < start + each)
    return jnp.sum(jnp.where(hit, row, 0.0), axis=1, keepdims=True)


def upwind_change(state, sign):
    cells = state.shape[1]
    spot = lax.broadcasted_iota(jnp.int32, (1, cells), 1)
    after = jnp.where(spot == cells - 1, 0.0, pltpu.roll(state, cells - 1, 1))
    before = jnp.where(spot == 0, 0.0, pltpu.roll(state, 1, 1))
    return state - jnp.where(sign > 0, after, before)


def pack_kernel(adjoint_, labels_, conductance_, out, adjoint, labels, conductance, semaphores):
    fetch((adjoint_, labels_, conductance_), (adjoint, labels, conductance), semaphores)
    groups, rows, columns = out.shape
    part = adjoint.shape[1] // groups
    label = column_of(labels[...].astype(f32), 0, rows)
    kinds = lax.broadcasted_iota(jnp.int32, (rows, conductance.shape[1]), 1).astype(f32)
    kappa = jnp.sum(jnp.where(kinds == label, conductance[...], 0.0), axis=1, keepdims=True)
    first, _ = split(kappa)
    second, third = split(kappa - first.astype(f32))
    column = lax.broadcasted_iota(jnp.int32, (rows, columns - part), 1)
    scale = jnp.where(column == 0, first.astype(f32), 0.0) + jnp.where(column == 1, second.astype(f32), 0.0)
    scale = (scale + jnp.where(column == 2, third.astype(f32), 0.0)).astype(bf16)
    for group in range(groups):
        out[group, :, :part] = adjoint[:, group * part : (group + 1) * part].astype(bf16)
        out[group, :, part:] = scale


def flip_kernel(collision_, adjoint_, source_, out, collision, adjoint, source, semaphores):
    fetch((collision_, adjoint_, source_), (collision, adjoint, source), semaphores)
    base = split(adjoint[...] + relax_factor * source[...])
    out[...] = jnp.concatenate([collision[...], *base], axis=0).T


def pieces_of(lines):
    return [(step,) for step in range(lines - 1, 1, -1)] + [(1, 0) if lines > 1 else (0,)]


def hand_out(index, blocks, outs, lines):
    for step in range(lines):
        outs[step][...] = blocks[2 * index[TARGETS + step] + index[PAIR]]
    for piece, out in zip(pieces_of(lines), outs[lines:]):
        for spot, step in enumerate(piece):
            out[spot] = blocks[2 * index[TARGETS + step] + 1 - index[PAIR]].astype(bf16)


def handed_out(lines, block):
    kept = [jax.ShapeDtypeStruct(block, f32)] * lines
    return kept + [jax.ShapeDtypeStruct((len(piece), *block), bf16) for piece in pieces_of(lines)]


def first_kernel(index, flipped, full, *refs):
    *outs, inputs, terms = refs
    groups, part, cells = terms.shape
    lines = groups // 2
    depth = full.shape[0]
    rows = cells // groups
    inputs[:depth, :] = full[...] * bf16(-relax_factor)
    row = lax.broadcasted_iota(jnp.int32, (rows, cells), 0)
    column = lax.broadcasted_iota(jnp.int32, (rows, cells), 1)
    place = (column == row + index[ME] * rows).astype(f32).astype(bf16)
    inputs[depth : depth + rows, :] = place
    inputs[depth + rows :, :] = place
    terms[...] = jnp.dot(flipped[...], inputs[...], preferred_element_type=f32).reshape(terms.shape)
    hand_out(index, terms, outs, lines)


def transport_kernel(index, start, kappa, speed, direction, out, rate_out, sign_out):
    part, _ = out.shape
    first = index[ME] * part
    rate_out[...] = relax_factor * column_of(speed[...], first, part) * kappa[:1, :]
    sign_out[...] = 2.0 * column_of(direction[...].astype(f32), first, part, BRANCH) - 1.0
    out[...] = rate_out[...] * upwind_change(start[...].astype(f32), sign_out[...])


def second_kernel(index, flipped, full, state, rate, sign, *refs):
    *outs, terms, blocks = refs
    groups, part, cells = terms.shape
    lines = groups // 2
    depth = full.shape[0]
    inputs = full[...] * bf16(-relax_factor)
    terms[...] = jnp.dot(flipped[:, :depth], inputs, preferred_element_type=f32).reshape(terms.shape)
    terms[index[ME]] += state[...] - rate[...] * upwind_change(state[...], sign[...])
    blocks[...] = terms[...].reshape(groups * part, cells).T.reshape(blocks.shape)
    hand_out(index, blocks, outs, lines)


def steps_of(count):
    if count & (count - 1):
        return [[(i, (i + step) % count) for i in range(count)] for step in range(count)]
    return [[(i, i ^ step) for i in range(count)] for step in range(count)]


def reduce_over_cells(blocks, steps):
    lines = len(steps)
    kept, pieces = blocks[:lines], list(blocks[lines:])
    near, sums = [], {}
    for k, steps_in in enumerate(pieces_of(lines)):
        if k >= 2:
            near[k - 2], pieces[k] = lax.optimization_barrier((near[k - 2], pieces[k]))
        near.append(lax.ppermute(pieces[k], "pair", [(0, 1), (1, 0)]))
    for arrived, steps_in in zip(near, pieces_of(lines)):
        for spot, step in enumerate(steps_in):
            sums[step] = kept[step] + arrived[spot].astype(f32)
    result = sums[0]
    for step in reversed(range(1, lines)):
        result = result + lax.ppermute(sums[step].astype(bf16), "line", steps[step]).astype(f32)
    return result


def shards(adjoint, source, collision, speed, direction, labels, conductance):
    rows, width = adjoint.shape
    lines, pairs, modes = lax.axis_size("line"), lax.axis_size("pair"), lax.axis_size("mode")
    groups = lines * pairs
    part = width // groups
    cells = rows * groups
    depth = modes * part
    line, pair = lax.axis_index("line"), lax.axis_index("pair")
    me = line * pairs + pair
    steps = steps_of(lines)
    targets = [line]
    for step in range(1, lines):
        targets.append(lax.rem(line + step, lines) if lines & (lines - 1) else line ^ step)
    index = jnp.stack([me, pair, *targets]).astype(jnp.int32)
    shape = jax.ShapeDtypeStruct

    columns = -(-(part + EXTRA) // 128) * 128
    sent = call(
        pack_kernel,
        shape((groups, rows, columns), bf16),
        [],
        [adjoint, labels[None, :], conductance[None, :]],
        own_copies=True,
    )
    got = lax.all_to_all(sent, ("line", "pair"), split_axis=0, concat_axis=0, tiled=True).reshape(cells, columns)

    collision, sent = lax.optimization_barrier((collision, sent))
    flipped = call(
        flip_kernel,
        shape((width, depth + 2 * rows), bf16),
        [],
        [collision.reshape(depth, width), adjoint, source],
        own_copies=True,
    )

    start = got[:, :part].T
    full = lax.all_gather(start, "mode", axis=0, tiled=True)
    terms = call(
        first_kernel,
        handed_out(lines, (part, cells)),
        [index],
        [flipped, full],
        [((depth + 2 * rows, cells), bf16), ((groups, part, cells), f32)],
        flops=2 * width * depth * cells,
    )
    start, got, terms = lax.optimization_barrier((start, got, terms))
    transport, rate, sign = call(
        transport_kernel,
        [shape((part, cells), f32), shape((part, cells), f32), shape((part, 1), f32)],
        [index],
        [start, jnp.sum(got[:, part:].astype(f32), axis=1)[None, :], speed[None, :], direction[None, :]],
    )
    state = reduce_over_cells(terms, steps) - transport

    full = lax.all_gather(state.astype(bf16), "mode", axis=0, tiled=True)
    terms = call(
        second_kernel,
        handed_out(lines, (rows, width)),
        [index],
        [flipped, full, state, rate, sign],
        [((groups, part, cells), f32), ((groups, rows, width), f32)],
        flops=2 * width * depth * cells,
    )
    return reduce_over_cells(terms, steps) + relax_factor * source


def solution(mesh):
    modes, groups = mesh.shape["mode"], mesh.shape["cell"]
    mesh = Mesh(mesh.devices.reshape(modes, groups // 2, 2), ("mode", "line", "pair"))
    cell = ("line", "pair")
    in_specs = (
        P(cell, "mode"),
        P(cell, "mode"),
        P(None, cell, None, "mode"),
        P("mode"),
        P("mode"),
        P(cell),
        P(),
    )
    out_specs = P(cell, "mode")
    return jax.shard_map(shards, mesh=mesh, in_specs=in_specs, out_specs=out_specs, check_vma=False)
```

```python
import math

import jax
import jax.numpy as jnp
from jax import lax
from jax.experimental import pallas as pl
from jax.experimental.pallas import tpu as pltpu
from jax.sharding import Mesh, PartitionSpec as P

BRANCH = 48
ITERS = 2


relax_factor = 0.5
VMEM = pl.BlockSpec(memory_space=pltpu.VMEM)
SMEM = pl.BlockSpec(memory_space=pltpu.SMEM)
HBM = pl.BlockSpec(memory_space=pltpu.HBM)
bf16, f32 = jnp.bfloat16, jnp.float32
EXTRA = 16
TARGETS = 3


def split(array):
    head = array.astype(bf16)
    return head, (array - head.astype(f32)).astype(bf16)


def padded_bytes(shape, dtype):
    size = jnp.dtype(dtype).itemsize
    if len(shape) < 2:
        return 4096
    sublanes = 8 * 4 // size
    rows, lanes = -(-shape[-2] // sublanes) * sublanes, -(-shape[-1] // 128) * 128
    return math.prod(shape[:-2]) * rows * lanes * size


def call(body, out, scalars, arrays, scratch=(), flops=0, own_copies=False):
    outs = jax.tree.leaves(out)
    bytes_ = sum(padded_bytes(a.shape, a.dtype) for a in (*arrays, *outs))
    held = sum(padded_bytes(shape, dtype) for shape, dtype in scratch)
    scratch = [pltpu.VMEM(shape, dtype) for shape, dtype in scratch]
    if own_copies:
        scratch += [pltpu.VMEM(a.shape, a.dtype) for a in arrays] + [pltpu.SemaphoreType.DMA((len(arrays),))]
    return pl.pallas_call(
        body,
        out_shape=out,
        in_specs=[SMEM] * len(scalars) + [HBM if own_copies else VMEM] * len(arrays),
        out_specs=jax.tree.map(lambda _: VMEM, out),
        scratch_shapes=scratch,
        compiler_params=pltpu.CompilerParams(vmem_limit_bytes=(56 * 2**20 if own_copies else int(1.5 * (bytes_ + held)) + 4 * 2**20)),
        cost_estimate=pl.CostEstimate(flops=flops, bytes_accessed=0 if own_copies else bytes_, transcendentals=0),
    )(*scalars, *arrays)


def fetch(sources, targets, semaphores):
    copies = [
        pltpu.make_async_copy(source, target, semaphores.at[k])
        for k, (source, target) in enumerate(zip(sources, targets))
    ]
    for copy in copies:
        copy.start()
    return copies


def column_of(row, first, count, each=1):
    wide = row.shape[1]
    place = first + lax.broadcasted_iota(jnp.int32, (count, wide), 0)
    start = lax.broadcasted_iota(jnp.int32, (count, wide), 1) * each
    hit = jnp.logical_and(place >= start, place < start + each)
    return jnp.sum(jnp.where(hit, row, 0.0), axis=1, keepdims=True)


def open_kernel(index, adjoint_, labels_, conductance_, collision_, source_, *refs):
    *outs, keep, send, blocks, adjoint, labels, conductance, collision, source, semaphores = refs
    lines, pair = len(outs), index[1]
    copies = fetch(
        (adjoint_, labels_, conductance_, collision_, source_),
        (adjoint, labels, conductance, collision, source),
        semaphores,
    )
    for copy in copies[:3]:
        copy.wait()
    rows, columns = outs[0].shape
    span = adjoint.shape[1] // lines
    label = column_of(labels[...].astype(f32), 0, rows)
    kinds = lax.broadcasted_iota(jnp.int32, (rows, conductance.shape[1]), 1).astype(f32)
    kappa = jnp.sum(jnp.where(kinds == label, conductance[...], 0.0), axis=1, keepdims=True)
    first, _ = split(kappa)
    second, third = split(kappa - first.astype(f32))
    column = lax.broadcasted_iota(jnp.int32, (rows, columns - span), 1)
    scale = jnp.where(column == 0, first.astype(f32), 0.0) + jnp.where(column == 1, second.astype(f32), 0.0)
    scale = (scale + jnp.where(column == 2, third.astype(f32), 0.0)).astype(bf16)
    for line in range(lines):
        blocks[line, :, :span] = adjoint[:, line * span : (line + 1) * span].astype(bf16)
        blocks[line, :, span:] = scale
    for step in range(lines):
        outs[step][...] = blocks[index[TARGETS + step]]

    for copy in copies[3:]:
        copy.wait()
    part = span // 2
    base = split(adjoint[...] + relax_factor * source[...])
    turned = jnp.concatenate([collision[...], *base], axis=0).T
    for line in range(lines):
        first = turned[2 * line * part : (2 * line + 1) * part]
        second = turned[(2 * line + 1) * part : (2 * line + 2) * part]
        spot = slice(line * part, (line + 1) * part)
        keep[spot, :] = jnp.where(pair == 0, first, second)
        send[spot, :] = jnp.where(pair == 0, second, first)


def turn_kernel(index, *refs):
    *arrived, out, blocks = refs
    for step, block in enumerate(arrived):
        blocks[index[TARGETS + len(arrived) + step]] = block[...]
    lines, rows, columns = blocks.shape
    out[...] = blocks[...].reshape(lines * rows, columns).T[: out.shape[0]]


def first_kernel(index, keep, other, full, *refs):
    *outs, inputs, terms = refs
    lines = len(outs)
    part, cells = outs[0].shape
    _, modes, _, half = full.shape
    line, pair = index[0], index[1]
    depth = modes * part
    rows = half // lines
    row = lax.broadcasted_iota(jnp.int32, (rows, cells), 0)
    column = lax.broadcasted_iota(jnp.int32, (rows, cells), 1)
    for group in range(2):
        for mode in range(modes):
            for side in range(2):
                block = full[side, mode, group * part : (group + 1) * part, :] * bf16(-relax_factor)
                inputs[group, mode * part : (mode + 1) * part, side * half : (side + 1) * half] = block
        place = (column == row + (group * half + line * rows)).astype(f32).astype(bf16)
        inputs[group, depth : depth + rows, :] = place
        inputs[group, depth + rows :, :] = place
    result = jnp.dot(keep[...], inputs[pair], preferred_element_type=f32)
    result += jnp.dot(other[...], inputs[1 - pair], preferred_element_type=f32)
    terms[...] = result.reshape(terms.shape)
    for step, out in enumerate(outs):
        out[...] = terms[index[TARGETS + step]].astype(out.dtype)


def shifted(own, far, pair, rows):
    half = own.shape[1]
    spot = lax.broadcasted_iota(jnp.int32, (1, half), 1)
    inner = lax.rem(spot, rows)
    close = pltpu.roll(far, rows - 1, 1)
    away = jnp.where(spot == half - 1, 0.0, pltpu.roll(far, half - 1, 1))
    after = jnp.where(inner < rows - 1, pltpu.roll(own, half - 1, 1), jnp.where(pair == 0, close, away))
    close = pltpu.roll(far, half - (rows - 1), 1)
    away = jnp.where(spot == 0, 0.0, pltpu.roll(far, 1, 1))
    before = jnp.where(inner > 0, pltpu.roll(own, 1, 1), jnp.where(pair == 0, away, close))
    return after, before


def transport_kernel(index, full, speed, direction, out, kappa_out, rate_out, sign_out):
    part, cells = out.shape
    _, _, span, half = full.shape
    span -= EXTRA
    lines = kappa_out.shape[0]
    line, pair, mode = index[0], index[1], index[2]
    rate_out[...] = relax_factor * column_of(speed[...], line * span, span)
    sign_out[...] = 2.0 * column_of(direction[...].astype(f32), line * span, span, BRANCH) - 1.0
    mine = pl.ds(pl.multiple_of(pair * part, 16), part)
    rate, sign = rate_out[mine, :], sign_out[mine, :]
    lam = [full[side, mode, mine, :].astype(f32) for side in range(2)]
    kappa = [jnp.sum(full[side, 0, span:, :].astype(f32), axis=0, keepdims=True) for side in range(2)]
    for side in range(2):
        after, before = shifted(lam[side], lam[1 - side], side, half // lines)
        change = lam[side] - jnp.where(sign > 0, after, before)
        out[:, side * half : (side + 1) * half] = rate * kappa[side] * change
    kappa_out[...] = jnp.broadcast_to(jnp.where(pair == 0, kappa[0], kappa[1]), kappa_out.shape)


def second_kernel(index, keep, send, near, rest, full, state, beyond, rate, sign, kappa, *refs):
    *outs, inputs, terms, flat = refs
    lines = len(outs)
    rows, width = outs[0].shape
    modes, _, part, half = full.shape
    depth = modes * part
    line, pair = index[0], index[1]
    for group in range(2):
        for mode in range(modes):
            inputs[group, mode * part : (mode + 1) * part, :] = full[mode, group] * bf16(-relax_factor)
    same = jnp.dot(keep[:, :depth], inputs[0], preferred_element_type=f32)
    same += jnp.dot(near[:, :depth], inputs[1], preferred_element_type=f32)
    cross = jnp.dot(send[:, :depth], inputs[0], preferred_element_type=f32)
    cross += jnp.dot(rest[:, :depth], inputs[1], preferred_element_type=f32)
    for target in range(lines):
        spot = slice(target * part, (target + 1) * part)
        terms[target, pair] = same[spot]
        terms[target, 1 - pair] = cross[spot]
    mine = pl.ds(pl.multiple_of(pair * half, 128), half)
    theirs = pl.ds(pl.multiple_of((1 - pair) * half, 128), half)
    for values, group in ((state, pair), (beyond, 1 - pair)):
        lam = values[:, mine].astype(f32)
        after, before = shifted(lam, values[:, theirs].astype(f32), pair, rows)
        spot = pl.ds(pl.multiple_of(group * part, 16), part)
        change = lam - jnp.where(sign[spot, :] > 0, after, before)
        terms[line, group] += lam - rate[spot, :] * kappa[:1, :] * change
    flat[...] = terms[...].reshape(width, half).T
    for step, out in enumerate(outs):
        start = pl.multiple_of(index[TARGETS + step] * rows, 16)
        out[...] = flat[pl.ds(start, rows), :].astype(out.dtype)


def line_steps(lines):
    if lines & (lines - 1):
        return [[(i, (i + step) % lines) for i in range(lines)] for step in range(lines)]
    return [[(i, i ^ step) for i in range(lines)] for step in range(lines)]


def exchange(blocks, steps):
    arrived = [lax.ppermute(blocks[step], "line", steps[step]) for step in reversed(range(1, len(steps)))]
    return [blocks[0]] + arrived[::-1]


def total(blocks):
    result = blocks[0].astype(f32)
    for block in blocks[1:]:
        result = result + block.astype(f32)
    return result


def shards(adjoint, source, collision, speed, direction, labels, conductance):
    rows, width = adjoint.shape
    lines, pairs, modes = lax.axis_size("line"), lax.axis_size("pair"), lax.axis_size("mode")
    part = width // (lines * pairs)
    span = part * pairs
    half = rows * lines
    cells = half * pairs
    depth = modes * part
    line, pair, mode = lax.axis_index("line"), lax.axis_index("pair"), lax.axis_index("mode")
    steps = line_steps(lines)
    targets = [line] + [jnp.array([t for _, t in pairs], jnp.int32)[line] for pairs in steps[1:]]
    origins = [line] + [jnp.array([o for o, _ in sorted(pairs, key=lambda p: p[1])], jnp.int32)[line] for pairs in steps[1:]]
    if lines & (lines - 1) == 0:
        targets = origins = [line ^ step for step in range(lines)]
    index = jnp.stack([line, pair, mode, *targets, *origins]).astype(jnp.int32)
    swap = [(0, 1), (1, 0)]
    shape = jax.ShapeDtypeStruct

    columns = -(-(span + EXTRA) // 128) * 128
    half_block = shape((width // 2, depth + 2 * rows), bf16)
    *sent, keep, send = call(
        open_kernel,
        [shape((rows, columns), bf16)] * lines + [half_block, half_block],
        [index],
        [adjoint, labels[None, :], conductance[None, :], collision.reshape(depth, width), source],
        [((lines, rows, columns), bf16)],
        flops=10**9,
        own_copies=True,
    )
    got = exchange(sent, steps)
    near = lax.ppermute(send, "pair", swap)

    start = call(turn_kernel, shape((span + EXTRA, half), bf16), [index], got, [((lines, rows, columns), bf16)])
    full = lax.all_gather(start, ("pair", "mode"), axis=0, tiled=False).reshape(pairs, modes, span + EXTRA, half)
    terms = call(
        first_kernel,
        [shape((part, cells), f32)] + [shape((part, cells), bf16)] * (lines - 1),
        [index],
        [keep, near, full],
        [((2, depth + 2 * rows, cells), bf16), ((lines, part, cells), f32)],
        flops=2 * width * depth * cells,
    )
    moved = exchange(terms, steps)

    keep_late, full, terms = lax.optimization_barrier((keep, full, terms))
    rest = lax.ppermute(keep_late, "pair", swap)
    transport, kappa, rate, sign = call(
        transport_kernel,
        [shape((part, cells), f32), shape((lines, half), f32), shape((span, 1), f32), shape((span, 1), f32)],
        [index],
        [full, speed[None, :], direction[None, :]],
    )
    state = total(moved) - transport
    rounded = state.astype(bf16)
    beyond = lax.ppermute(rounded, "pair", swap)

    both = [lax.dynamic_slice_in_dim(values, pair * half, half, axis=1) for values in (rounded, beyond)]
    full = lax.all_gather(jnp.concatenate(both, axis=0), "mode", axis=0, tiled=False).reshape(modes, 2, part, half)
    terms = call(
        second_kernel,
        [shape((rows, width), f32)] + [shape((rows, width), bf16)] * (lines - 1),
        [index],
        [keep, send, near, rest, full, state, beyond, rate, sign, kappa],
        [((2, depth, half), bf16), ((lines, 2, part, half), f32), ((half, width), f32)],
        flops=2 * 2 * width * depth * half,
    )
    return total(exchange(terms, steps)) + relax_factor * source


def solution(mesh):
    modes, groups = mesh.shape["mode"], mesh.shape["cell"]
    mesh = Mesh(mesh.devices.reshape(modes, groups // 2, 2), ("mode", "line", "pair"))
    cell = ("line", "pair")
    in_specs = (
        P(cell, "mode"),
        P(cell, "mode"),
        P(None, cell, None, "mode"),
        P("mode"),
        P("mode"),
        P(cell),
        P(),
    )
    out_specs = P(cell, "mode")
    return jax.shard_map(shards, mesh=mesh, in_specs=in_specs, out_specs=out_specs, check_vma=False)
```

```python
import math

import jax
import jax.numpy as jnp
from jax import lax
from jax.experimental import pallas as pl
from jax.experimental.pallas import tpu as pltpu
from jax.sharding import Mesh, PartitionSpec as P

BRANCH = 48
ITERS = 2


relax_factor = 0.5
VMEM = pl.BlockSpec(memory_space=pltpu.VMEM)
SMEM = pl.BlockSpec(memory_space=pltpu.SMEM)
HBM = pl.BlockSpec(memory_space=pltpu.HBM)
bf16, f32 = jnp.bfloat16, jnp.float32
EXTRA = 16
ME, PAIR, TARGETS = 0, 1, 2


def split(array):
    head = array.astype(bf16)
    return head, (array - head.astype(f32)).astype(bf16)


def padded_bytes(shape, dtype):
    size = jnp.dtype(dtype).itemsize
    if len(shape) < 2:
        return 4096
    sublanes = 8 * 4 // size
    rows, lanes = -(-shape[-2] // sublanes) * sublanes, -(-shape[-1] // 128) * 128
    return math.prod(shape[:-2]) * rows * lanes * size


def call(body, out, scalars, arrays, scratch=(), flops=0, own_copies=False):
    outs = jax.tree.leaves(out)
    bytes_ = sum(padded_bytes(a.shape, a.dtype) for a in (*arrays, *outs))
    held = sum(padded_bytes(shape, dtype) for shape, dtype in scratch)
    scratch = [pltpu.VMEM(shape, dtype) for shape, dtype in scratch]
    if own_copies:
        scratch += [pltpu.VMEM(a.shape, a.dtype) for a in arrays] + [pltpu.SemaphoreType.DMA((len(arrays),))]
    return pl.pallas_call(
        body,
        out_shape=out,
        in_specs=[SMEM] * len(scalars) + [HBM if own_copies else VMEM] * len(arrays),
        out_specs=jax.tree.map(lambda _: VMEM, out),
        scratch_shapes=scratch,
        compiler_params=pltpu.CompilerParams(
            vmem_limit_bytes=56 * 2**20 if own_copies else int(1.5 * (bytes_ + held)) + 4 * 2**20
        ),
        cost_estimate=pl.CostEstimate(flops=flops, bytes_accessed=bytes_, transcendentals=0),
    )(*scalars, *arrays)


def fetch(sources, targets, semaphores):
    copies = [
        pltpu.make_async_copy(source, target, semaphores.at[k])
        for k, (source, target) in enumerate(zip(sources, targets))
    ]
    for copy in copies:
        copy.start()
    for copy in copies:
        copy.wait()


def column_of(row, first, count, each=1):
    wide = row.shape[1]
    place = first + lax.broadcasted_iota(jnp.int32, (count, wide), 0)
    start = lax.broadcasted_iota(jnp.int32, (count, wide), 1) * each
    hit = jnp.logical_and(place >= start, place < start + each)
    return jnp.sum(jnp.where(hit, row, 0.0), axis=1, keepdims=True)


def upwind_change(state, sign):
    cells = state.shape[1]
    spot = lax.broadcasted_iota(jnp.int32, (1, cells), 1)
    after = jnp.where(spot == cells - 1, 0.0, pltpu.roll(state, cells - 1, 1))
    before = jnp.where(spot == 0, 0.0, pltpu.roll(state, 1, 1))
    return state - jnp.where(sign > 0, after, before)


def pack_kernel(adjoint_, labels_, conductance_, out, adjoint, labels, conductance, semaphores):
    fetch((adjoint_, labels_, conductance_), (adjoint, labels, conductance), semaphores)
    groups, rows, columns = out.shape
    part = adjoint.shape[1] // groups
    label = column_of(labels[...].astype(f32), 0, rows)
    kinds = lax.broadcasted_iota(jnp.int32, (rows, conductance.shape[1]), 1).astype(f32)
    kappa = jnp.sum(jnp.where(kinds == label, conductance[...], 0.0), axis=1, keepdims=True)
    first, _ = split(kappa)
    second, third = split(kappa - first.astype(f32))
    column = lax.broadcasted_iota(jnp.int32, (rows, columns - part), 1)
    scale = jnp.where(column == 0, first.astype(f32), 0.0) + jnp.where(column == 1, second.astype(f32), 0.0)
    scale = (scale + jnp.where(column == 2, third.astype(f32), 0.0)).astype(bf16)
    for group in range(groups):
        out[group, :, :part] = adjoint[:, group * part : (group + 1) * part].astype(bf16)
        out[group, :, part:] = scale


def flip_kernel(collision, adjoint, source, out):
    base = split(adjoint[...] + relax_factor * source[...])
    out[...] = jnp.concatenate([collision[...], *base], axis=0).T


def relayed(step, lines):
    return lines // 2 <= step < lines - 1


def hand_out(index, blocks, outs, lines):
    for step in range(lines):
        own, other = outs[2 * step], outs[2 * step + 1]
        own[...] = blocks[2 * index[TARGETS + step] + index[PAIR]].astype(own.dtype)
        other[...] = blocks[2 * index[TARGETS + step] + 1 - index[PAIR]].astype(other.dtype)


def handed_out(lines, block):
    shapes = []
    for step in range(lines):
        local = step == 0 or relayed(step, lines)
        shapes += [jax.ShapeDtypeStruct(block, f32 if local else bf16), jax.ShapeDtypeStruct(block, bf16)]
    return shapes


def first_kernel(index, flipped, full, *refs):
    *outs, inputs, terms = refs
    groups, part, cells = terms.shape
    lines = groups // 2
    depth = full.shape[0]
    rows = cells // groups
    inputs[:depth, :] = full[...] * bf16(-relax_factor)
    row = lax.broadcasted_iota(jnp.int32, (rows, cells), 0)
    column = lax.broadcasted_iota(jnp.int32, (rows, cells), 1)
    place = (column == row + index[ME] * rows).astype(f32).astype(bf16)
    inputs[depth : depth + rows, :] = place
    inputs[depth + rows :, :] = place
    terms[...] = jnp.dot(flipped[...], inputs[...], preferred_element_type=f32).reshape(terms.shape)
    hand_out(index, terms, outs, lines)


def transport_kernel(index, start, kappa, speed, direction, out, rate_out, sign_out):
    part, _ = out.shape
    first = index[ME] * part
    rate_out[...] = relax_factor * column_of(speed[...], first, part) * kappa[:1, :]
    sign_out[...] = 2.0 * column_of(direction[...].astype(f32), first, part, BRANCH) - 1.0
    out[...] = rate_out[...] * upwind_change(start[...].astype(f32), sign_out[...])


def second_kernel(index, flipped, full, state, rate, sign, *refs):
    *outs, terms, blocks = refs
    groups, part, cells = terms.shape
    lines = groups // 2
    depth = full.shape[0]
    inputs = full[...] * bf16(-relax_factor)
    terms[...] = jnp.dot(flipped[:, :depth], inputs, preferred_element_type=f32).reshape(terms.shape)
    terms[index[ME]] += state[...] - rate[...] * upwind_change(state[...], sign[...])
    blocks[...] = terms[...].reshape(groups * part, cells).T.reshape(blocks.shape)
    hand_out(index, blocks, outs, lines)


def steps_of(count):
    if count & (count - 1):
        return [[(i, (i + step) % count) for i in range(count)] for step in range(count)]
    return [[(i, i ^ step) for i in range(count)] for step in range(count)]


def reduce_over_cells(blocks, steps):
    lines = len(steps)
    swap = [(0, 1), (1, 0)]
    order = sorted(range(lines), key=lambda step: (not relayed(step, lines), -step))
    across = {}
    for step in order:
        if step == 0 or relayed(step, lines):
            across[step] = lax.ppermute(blocks[2 * step + 1], "pair", swap)
        else:
            pairs = [(2 * i + p, 2 * j + 1 - p) for i, j in steps[step] for p in range(2)]
            across[step] = lax.ppermute(blocks[2 * step + 1], ("line", "pair"), pairs)
    result = blocks[0] + across[0].astype(f32)
    for step in range(1, lines):
        own = blocks[2 * step]
        if relayed(step, lines):
            own = (own + across[step].astype(f32)).astype(bf16)
        else:
            result = result + across[step].astype(f32)
        result = result + lax.ppermute(own, "line", steps[step]).astype(f32)
    return result


def shards(adjoint, source, collision, speed, direction, labels, conductance):
    rows, width = adjoint.shape
    lines, pairs, modes = lax.axis_size("line"), lax.axis_size("pair"), lax.axis_size("mode")
    groups = lines * pairs
    part = width // groups
    cells = rows * groups
    depth = modes * part
    line, pair = lax.axis_index("line"), lax.axis_index("pair")
    me = line * pairs + pair
    steps = steps_of(lines)
    targets = [line]
    for step in range(1, lines):
        targets.append(lax.rem(line + step, lines) if lines & (lines - 1) else line ^ step)
    index = jnp.stack([me, pair, *targets]).astype(jnp.int32)
    shape = jax.ShapeDtypeStruct

    columns = -(-(part + EXTRA) // 128) * 128
    sent = call(
        pack_kernel,
        shape((groups, rows, columns), bf16),
        [],
        [adjoint, labels[None, :], conductance[None, :]],
        own_copies=True,
    )
    got = lax.all_to_all(sent, ("line", "pair"), split_axis=0, concat_axis=0, tiled=True).reshape(cells, columns)

    collision, sent = lax.optimization_barrier((collision, sent))
    flipped = call(
        flip_kernel,
        shape((width, depth + 2 * rows), bf16),
        [],
        [collision.reshape(depth, width), adjoint, source],
    )

    start = got[:, :part].T
    full = lax.all_gather(start, "mode", axis=0, tiled=True)
    terms = call(
        first_kernel,
        handed_out(lines, (part, cells)),
        [index],
        [flipped, full],
        [((depth + 2 * rows, cells), bf16), ((groups, part, cells), f32)],
        flops=2 * width * depth * cells,
    )
    start, got, terms = lax.optimization_barrier((start, got, terms))
    transport, rate, sign = call(
        transport_kernel,
        [shape((part, cells), f32), shape((part, cells), f32), shape((part, 1), f32)],
        [index],
        [start, jnp.sum(got[:, part:].astype(f32), axis=1)[None, :], speed[None, :], direction[None, :]],
    )
    state = reduce_over_cells(terms, steps) - transport

    full = lax.all_gather(state.astype(bf16), "mode", axis=0, tiled=True)
    terms = call(
        second_kernel,
        handed_out(lines, (rows, width)),
        [index],
        [flipped, full, state, rate, sign],
        [((groups, part, cells), f32), ((groups, rows, width), f32)],
        flops=2 * width * depth * cells,
    )
    return reduce_over_cells(terms, steps) + relax_factor * source


def solution(mesh):
    modes, groups = mesh.shape["mode"], mesh.shape["cell"]
    mesh = Mesh(mesh.devices.reshape(modes, groups // 2, 2), ("mode", "line", "pair"))
    cell = ("line", "pair")
    in_specs = (
        P(cell, "mode"),
        P(cell, "mode"),
        P(None, cell, None, "mode"),
        P("mode"),
        P("mode"),
        P(cell),
        P(),
    )
    out_specs = P(cell, "mode")
    return jax.shard_map(shards, mesh=mesh, in_specs=in_specs, out_specs=out_specs, check_vma=False)
```

```python
import math

import jax
import jax.numpy as jnp
from jax import lax
from jax.experimental import pallas as pl
from jax.experimental.pallas import tpu as pltpu
from jax.sharding import Mesh, PartitionSpec as P

BRANCH = 48
ITERS = 2


relax_factor = 0.5
VMEM = pl.BlockSpec(memory_space=pltpu.VMEM)
SMEM = pl.BlockSpec(memory_space=pltpu.SMEM)
HBM = pl.BlockSpec(memory_space=pltpu.HBM)
bf16, f32 = jnp.bfloat16, jnp.float32
EXTRA = 16
ME, PAIR, TARGETS = 0, 1, 2


def split(array):
    head = array.astype(bf16)
    return head, (array - head.astype(f32)).astype(bf16)


def padded_bytes(shape, dtype):
    size = jnp.dtype(dtype).itemsize
    if len(shape) < 2:
        return 4096
    sublanes = 8 * 4 // size
    rows, lanes = -(-shape[-2] // sublanes) * sublanes, -(-shape[-1] // 128) * 128
    return math.prod(shape[:-2]) * rows * lanes * size


def call(body, out, scalars, arrays, scratch=(), flops=0, own_copies=False):
    outs = jax.tree.leaves(out)
    bytes_ = sum(padded_bytes(a.shape, a.dtype) for a in (*arrays, *outs))
    held = sum(padded_bytes(shape, dtype) for shape, dtype in scratch)
    scratch = [pltpu.VMEM(shape, dtype) for shape, dtype in scratch]
    if own_copies:
        scratch += [pltpu.VMEM(a.shape, a.dtype) for a in arrays] + [pltpu.SemaphoreType.DMA((len(arrays),))]
    return pl.pallas_call(
        body,
        out_shape=out,
        in_specs=[SMEM] * len(scalars) + [HBM if own_copies else VMEM] * len(arrays),
        out_specs=jax.tree.map(lambda _: VMEM, out),
        scratch_shapes=scratch,
        compiler_params=pltpu.CompilerParams(
            vmem_limit_bytes=56 * 2**20 if own_copies else int(1.5 * (bytes_ + held)) + 4 * 2**20
        ),
        cost_estimate=pl.CostEstimate(flops=flops, bytes_accessed=bytes_, transcendentals=0),
    )(*scalars, *arrays)


def fetch(sources, targets, semaphores):
    copies = [
        pltpu.make_async_copy(source, target, semaphores.at[k])
        for k, (source, target) in enumerate(zip(sources, targets))
    ]
    for copy in copies:
        copy.start()
    for copy in copies:
        copy.wait()


def column_of(row, first, count, each=1):
    wide = row.shape[1]
    place = first + lax.broadcasted_iota(jnp.int32, (count, wide), 0)
    start = lax.broadcasted_iota(jnp.int32, (count, wide), 1) * each
    hit = jnp.logical_and(place >= start, place < start + each)
    return jnp.sum(jnp.where(hit, row, 0.0), axis=1, keepdims=True)


def upwind_change(state, sign):
    cells = state.shape[1]
    spot = lax.broadcasted_iota(jnp.int32, (1, cells), 1)
    after = jnp.where(spot == cells - 1, 0.0, pltpu.roll(state, cells - 1, 1))
    before = jnp.where(spot == 0, 0.0, pltpu.roll(state, 1, 1))
    return state - jnp.where(sign > 0, after, before)


def pack_kernel(adjoint_, labels_, conductance_, out, adjoint, labels, conductance, semaphores):
    fetch((adjoint_, labels_, conductance_), (adjoint, labels, conductance), semaphores)
    groups, rows, columns = out.shape
    part = adjoint.shape[1] // groups
    label = column_of(labels[...].astype(f32), 0, rows)
    kinds = lax.broadcasted_iota(jnp.int32, (rows, conductance.shape[1]), 1).astype(f32)
    kappa = jnp.sum(jnp.where(kinds == label, conductance[...], 0.0), axis=1, keepdims=True)
    first, _ = split(kappa)
    second, third = split(kappa - first.astype(f32))
    column = lax.broadcasted_iota(jnp.int32, (rows, columns - part), 1)
    scale = jnp.where(column == 0, first.astype(f32), 0.0) + jnp.where(column == 1, second.astype(f32), 0.0)
    scale = (scale + jnp.where(column == 2, third.astype(f32), 0.0)).astype(bf16)
    for group in range(groups):
        out[group, :, :part] = adjoint[:, group * part : (group + 1) * part].astype(bf16)
        out[group, :, part:] = scale


def flip_kernel(collision, adjoint, source, out):
    base = split(adjoint[...] + relax_factor * source[...])
    out[...] = jnp.concatenate([collision[...], *base], axis=0).T


def relayed(step, lines):
    return lines // 2 <= step < lines - 1


def pieces_of(lines):
    near = [step for step in range(lines) if relayed(step, lines)]
    return [(step,) for step in near[:0:-1]] + [(*near[:1], 0)]


def straight(lines):
    return [step for step in range(lines - 1, 0, -1) if not relayed(step, lines)]


def hand_out(index, blocks, outs, lines):
    outs = iter(outs)
    own, other = index[PAIR], 1 - index[PAIR]
    for piece in pieces_of(lines):
        for step in piece:
            next(outs)[...] = blocks[2 * index[TARGETS + step] + own]
        out = next(outs)
        for spot, step in enumerate(piece):
            out[spot] = blocks[2 * index[TARGETS + step] + other].astype(bf16)
    for step in straight(lines):
        for pair in (other, own):
            next(outs)[...] = blocks[2 * index[TARGETS + step] + pair].astype(bf16)


def handed_out(lines, block):
    shapes = []
    for piece in pieces_of(lines):
        shapes += [jax.ShapeDtypeStruct(block, f32)] * len(piece)
        shapes += [jax.ShapeDtypeStruct((len(piece), *block), bf16)]
    return shapes + [jax.ShapeDtypeStruct(block, bf16)] * (2 * len(straight(lines)))


def first_kernel(index, flipped, full, *refs):
    *outs, inputs, terms = refs
    groups, part, cells = terms.shape
    lines = groups // 2
    depth = full.shape[0]
    rows = cells // groups
    inputs[:depth, :] = full[...] * bf16(-relax_factor)
    row = lax.broadcasted_iota(jnp.int32, (rows, cells), 0)
    column = lax.broadcasted_iota(jnp.int32, (rows, cells), 1)
    place = (column == row + index[ME] * rows).astype(f32).astype(bf16)
    inputs[depth : depth + rows, :] = place
    inputs[depth + rows :, :] = place
    terms[...] = jnp.dot(flipped[...], inputs[...], preferred_element_type=f32).reshape(terms.shape)
    hand_out(index, terms, outs, lines)


def transport_kernel(index, start, kappa, speed, direction, out, rate_out, sign_out):
    part, _ = out.shape
    first = index[ME] * part
    rate_out[...] = relax_factor * column_of(speed[...], first, part) * kappa[:1, :]
    sign_out[...] = 2.0 * column_of(direction[...].astype(f32), first, part, BRANCH) - 1.0
    out[...] = rate_out[...] * upwind_change(start[...].astype(f32), sign_out[...])


def second_kernel(index, flipped, full, state, rate, sign, *refs):
    *outs, terms, blocks = refs
    groups, part, cells = terms.shape
    lines = groups // 2
    depth = full.shape[0]
    inputs = full[...] * bf16(-relax_factor)
    terms[...] = jnp.dot(flipped[:, :depth], inputs, preferred_element_type=f32).reshape(terms.shape)
    terms[index[ME]] += state[...] - rate[...] * upwind_change(state[...], sign[...])
    blocks[...] = terms[...].reshape(groups * part, cells).T.reshape(blocks.shape)
    hand_out(index, blocks, outs, lines)


def steps_of(count):
    if count & (count - 1):
        return [[(i, (i + step) % count) for i in range(count)] for step in range(count)]
    return [[(i, i ^ step) for i in range(count)] for step in range(count)]


def reduce_over_cells(blocks, steps):
    lines, blocks = len(steps), iter(blocks)
    terms = []
    for piece in pieces_of(lines):
        kept = [next(blocks) for _ in piece]
        across = lax.ppermute(next(blocks), "pair", [(0, 1), (1, 0)])
        for spot, step in enumerate(piece):
            block = kept[spot] + across[spot].astype(f32)
            terms.append(lax.ppermute(block.astype(bf16), "line", steps[step]) if step else block)
    for step in straight(lines):
        diagonal = [(2 * i + pair, 2 * j + 1 - pair) for i, j in steps[step] for pair in range(2)]
        terms.append(lax.ppermute(next(blocks), ("line", "pair"), diagonal))
        terms.append(lax.ppermute(next(blocks), "line", steps[step]))
    result = terms[0].astype(f32)
    for term in terms[1:]:
        result = result + term.astype(f32)
    return result


def shards(adjoint, source, collision, speed, direction, labels, conductance):
    rows, width = adjoint.shape
    lines, pairs, modes = lax.axis_size("line"), lax.axis_size("pair"), lax.axis_size("mode")
    groups = lines * pairs
    part = width // groups
    cells = rows * groups
    depth = modes * part
    line, pair = lax.axis_index("line"), lax.axis_index("pair")
    me = line * pairs + pair
    steps = steps_of(lines)
    targets = [line]
    for step in range(1, lines):
        targets.append(lax.rem(line + step, lines) if lines & (lines - 1) else line ^ step)
    index = jnp.stack([me, pair, *targets]).astype(jnp.int32)
    shape = jax.ShapeDtypeStruct

    columns = -(-(part + EXTRA) // 128) * 128
    sent = call(
        pack_kernel,
        shape((groups, rows, columns), bf16),
        [],
        [adjoint, labels[None, :], conductance[None, :]],
        own_copies=True,
    )
    got = lax.all_to_all(sent, ("line", "pair"), split_axis=0, concat_axis=0, tiled=True).reshape(cells, columns)

    collision, sent = lax.optimization_barrier((collision, sent))
    flipped = call(
        flip_kernel,
        shape((width, depth + 2 * rows), bf16),
        [],
        [collision.reshape(depth, width), adjoint, source],
    )

    start = got[:, :part].T
    full = lax.all_gather(start, "mode", axis=0, tiled=True)
    terms = call(
        first_kernel,
        handed_out(lines, (part, cells)),
        [index],
        [flipped, full],
        [((depth + 2 * rows, cells), bf16), ((groups, part, cells), f32)],
        flops=2 * width * depth * cells,
    )
    start, got, terms = lax.optimization_barrier((start, got, terms))
    transport, rate, sign = call(
        transport_kernel,
        [shape((part, cells), f32), shape((part, cells), f32), shape((part, 1), f32)],
        [index],
        [start, jnp.sum(got[:, part:].astype(f32), axis=1)[None, :], speed[None, :], direction[None, :]],
    )
    state = reduce_over_cells(terms, steps) - transport

    full = lax.all_gather(state.astype(bf16), "mode", axis=0, tiled=True)
    terms = call(
        second_kernel,
        handed_out(lines, (rows, width)),
        [index],
        [flipped, full, state, rate, sign],
        [((groups, part, cells), f32), ((groups, rows, width), f32)],
        flops=2 * width * depth * cells,
    )
    return reduce_over_cells(terms, steps) + relax_factor * source


def solution(mesh):
    modes, groups = mesh.shape["mode"], mesh.shape["cell"]
    mesh = Mesh(mesh.devices.reshape(modes, groups // 2, 2), ("mode", "line", "pair"))
    cell = ("line", "pair")
    in_specs = (
        P(cell, "mode"),
        P(cell, "mode"),
        P(None, cell, None, "mode"),
        P("mode"),
        P("mode"),
        P(cell),
        P(),
    )
    out_specs = P(cell, "mode")
    return jax.shard_map(shards, mesh=mesh, in_specs=in_specs, out_specs=out_specs, check_vma=False)
```

```python
import math

import jax
import jax.numpy as jnp
from jax import lax
from jax.experimental import pallas as pl
from jax.experimental.pallas import tpu as pltpu
from jax.sharding import Mesh, PartitionSpec as P

BRANCH = 48
ITERS = 2


relax_factor = 0.5
VMEM = pl.BlockSpec(memory_space=pltpu.VMEM)
SMEM = pl.BlockSpec(memory_space=pltpu.SMEM)
HBM = pl.BlockSpec(memory_space=pltpu.HBM)
bf16, f32 = jnp.bfloat16, jnp.float32
EXTRA = 16
ME, PAIR, TARGETS = 0, 1, 2


def split(array):
    head = array.astype(bf16)
    return head, (array - head.astype(f32)).astype(bf16)


def padded_bytes(shape, dtype):
    size = jnp.dtype(dtype).itemsize
    if len(shape) < 2:
        return 4096
    sublanes = 8 * 4 // size
    rows, lanes = -(-shape[-2] // sublanes) * sublanes, -(-shape[-1] // 128) * 128
    return math.prod(shape[:-2]) * rows * lanes * size


def call(body, out, scalars, arrays, scratch=(), flops=0, own_copies=False):
    outs = jax.tree.leaves(out)
    bytes_ = sum(padded_bytes(a.shape, a.dtype) for a in (*arrays, *outs))
    held = sum(padded_bytes(shape, dtype) for shape, dtype in scratch)
    scratch = [pltpu.VMEM(shape, dtype) for shape, dtype in scratch]
    if own_copies:
        scratch += [pltpu.VMEM(a.shape, a.dtype) for a in arrays] + [pltpu.SemaphoreType.DMA((len(arrays),))]
    return pl.pallas_call(
        body,
        out_shape=out,
        in_specs=[SMEM] * len(scalars) + [HBM if own_copies else VMEM] * len(arrays),
        out_specs=jax.tree.map(lambda _: VMEM, out),
        scratch_shapes=scratch,
        compiler_params=pltpu.CompilerParams(
            vmem_limit_bytes=56 * 2**20 if own_copies else int(1.5 * (bytes_ + held)) + 4 * 2**20
        ),
        cost_estimate=pl.CostEstimate(flops=flops, bytes_accessed=bytes_, transcendentals=0),
    )(*scalars, *arrays)


def fetch(sources, targets, semaphores):
    copies = [
        pltpu.make_async_copy(source, target, semaphores.at[k])
        for k, (source, target) in enumerate(zip(sources, targets))
    ]
    for copy in copies:
        copy.start()
    for copy in copies:
        copy.wait()


def column_of(row, first, count, each=1):
    wide = row.shape[1]
    place = first + lax.broadcasted_iota(jnp.int32, (count, wide), 0)
    start = lax.broadcasted_iota(jnp.int32, (count, wide), 1) * each
    hit = jnp.logical_and(place >= start, place < start + each)
    return jnp.sum(jnp.where(hit, row, 0.0), axis=1, keepdims=True)


def upwind_change(state, sign):
    cells = state.shape[1]
    spot = lax.broadcasted_iota(jnp.int32, (1, cells), 1)
    after = jnp.where(spot == cells - 1, 0.0, pltpu.roll(state, cells - 1, 1))
    before = jnp.where(spot == 0, 0.0, pltpu.roll(state, 1, 1))
    return state - jnp.where(sign > 0, after, before)


def pack_kernel(adjoint_, labels_, conductance_, out, adjoint, labels, conductance, semaphores):
    fetch((adjoint_, labels_, conductance_), (adjoint, labels, conductance), semaphores)
    groups, rows, columns = out.shape
    part = adjoint.shape[1] // groups
    label = column_of(labels[...].astype(f32), 0, rows)
    kinds = lax.broadcasted_iota(jnp.int32, (rows, conductance.shape[1]), 1).astype(f32)
    kappa = jnp.sum(jnp.where(kinds == label, conductance[...], 0.0), axis=1, keepdims=True)
    first, _ = split(kappa)
    second, third = split(kappa - first.astype(f32))
    column = lax.broadcasted_iota(jnp.int32, (rows, columns - part), 1)
    scale = jnp.where(column == 0, first.astype(f32), 0.0) + jnp.where(column == 1, second.astype(f32), 0.0)
    scale = (scale + jnp.where(column == 2, third.astype(f32), 0.0)).astype(bf16)
    for group in range(groups):
        out[group, :, :part] = adjoint[:, group * part : (group + 1) * part].astype(bf16)
        out[group, :, part:] = scale


def flip_kernel(collision, adjoint, source, out):
    base = split(adjoint[...] + relax_factor * source[...])
    out[...] = jnp.concatenate([collision[...], *base], axis=0).T


def relayed(step, lines):
    return lines // 2 <= step < lines - 1


def pieces_of(lines):
    near = [step for step in range(lines) if relayed(step, lines)]
    return [(step,) for step in near[:0:-1]] + [(*near[:1], 0)]


def straight(lines):
    return [step for step in range(lines - 1, 0, -1) if not relayed(step, lines)]


def hand_out(index, blocks, outs, lines):
    outs = iter(outs)
    own, other = index[PAIR], 1 - index[PAIR]
    for piece in pieces_of(lines):
        for step in piece:
            next(outs)[...] = blocks[2 * index[TARGETS + step] + own]
        out = next(outs)
        for spot, step in enumerate(piece):
            out[spot] = blocks[2 * index[TARGETS + step] + other].astype(bf16)
    for step in straight(lines):
        for pair in (other, own):
            next(outs)[...] = blocks[2 * index[TARGETS + step] + pair].astype(bf16)


def handed_out(lines, block):
    shapes = []
    for piece in pieces_of(lines):
        shapes += [jax.ShapeDtypeStruct(block, f32)] * len(piece)
        shapes += [jax.ShapeDtypeStruct((len(piece), *block), bf16)]
    return shapes + [jax.ShapeDtypeStruct(block, bf16)] * (2 * len(straight(lines)))


def first_kernel(index, flipped, full, *refs):
    *outs, inputs, terms = refs
    groups, part, cells = terms.shape
    lines = groups // 2
    depth = full.shape[0]
    rows = cells // groups
    inputs[:depth, :] = full[...] * bf16(-relax_factor)
    row = lax.broadcasted_iota(jnp.int32, (rows, cells), 0)
    column = lax.broadcasted_iota(jnp.int32, (rows, cells), 1)
    place = (column == row + index[ME] * rows).astype(f32).astype(bf16)
    inputs[depth : depth + rows, :] = place
    inputs[depth + rows :, :] = place
    terms[...] = jnp.dot(flipped[...], inputs[...], preferred_element_type=f32).reshape(terms.shape)
    hand_out(index, terms, outs, lines)


def transport_kernel(index, start, kappa, speed, direction, out, rate_out, sign_out):
    part, _ = out.shape
    first = index[ME] * part
    rate_out[...] = relax_factor * column_of(speed[...], first, part) * kappa[:1, :]
    sign_out[...] = 2.0 * column_of(direction[...].astype(f32), first, part, BRANCH) - 1.0
    out[...] = rate_out[...] * upwind_change(start[...].astype(f32), sign_out[...])


def second_kernel(index, flipped, full, state, rate, sign, *refs):
    *outs, terms, blocks = refs
    groups, part, cells = terms.shape
    lines = groups // 2
    depth = full.shape[0]
    inputs = full[...] * bf16(-relax_factor)
    terms[...] = jnp.dot(flipped[:, :depth], inputs, preferred_element_type=f32).reshape(terms.shape)
    terms[index[ME]] += state[...] - rate[...] * upwind_change(state[...], sign[...])
    blocks[...] = terms[...].reshape(groups * part, cells).T.reshape(blocks.shape)
    hand_out(index, blocks, outs, lines)


def steps_of(count):
    if count & (count - 1):
        return [[(i, (i + step) % count) for i in range(count)] for step in range(count)]
    return [[(i, i ^ step) for i in range(count)] for step in range(count)]


def reduce_over_cells(blocks, steps):
    lines, blocks = len(steps), list(blocks)
    far = [step for step in straight(lines) if step >= lines // 2]
    near = blocks[len(blocks) - 2 * (len(straight(lines)) - len(far)) :]
    blocks, terms = iter(blocks), []
    for piece in pieces_of(lines):
        kept = [next(blocks) for _ in piece]
        arrived = lax.ppermute(next(blocks), "pair", [(0, 1), (1, 0)])
        for spot, step in enumerate(piece):
            block = kept[spot] + arrived[spot].astype(f32)
            if step:
                block, near = lax.optimization_barrier((block.astype(bf16), near))
                block = lax.ppermute(block, "line", steps[step])
            terms.append(block)
    near = iter(near)
    for step in straight(lines):
        diagonal = [(2 * i + pair, 2 * j + 1 - pair) for i, j in steps[step] for pair in range(2)]
        source = blocks if step in far else near
        terms.append(lax.ppermute(next(source), ("line", "pair"), diagonal))
        terms.append(lax.ppermute(next(source), "line", steps[step]))
    result = terms[0].astype(f32)
    for term in terms[1:]:
        result = result + term.astype(f32)
    return result


def shards(adjoint, source, collision, speed, direction, labels, conductance):
    rows, width = adjoint.shape
    lines, pairs, modes = lax.axis_size("line"), lax.axis_size("pair"), lax.axis_size("mode")
    groups = lines * pairs
    part = width // groups
    cells = rows * groups
    depth = modes * part
    line, pair = lax.axis_index("line"), lax.axis_index("pair")
    me = line * pairs + pair
    steps = steps_of(lines)
    targets = [line]
    for step in range(1, lines):
        targets.append(lax.rem(line + step, lines) if lines & (lines - 1) else line ^ step)
    index = jnp.stack([me, pair, *targets]).astype(jnp.int32)
    shape = jax.ShapeDtypeStruct

    columns = -(-(part + EXTRA) // 128) * 128
    sent = call(
        pack_kernel,
        shape((groups, rows, columns), bf16),
        [],
        [adjoint, labels[None, :], conductance[None, :]],
        own_copies=True,
    )
    got = lax.all_to_all(sent, ("line", "pair"), split_axis=0, concat_axis=0, tiled=True).reshape(cells, columns)

    collision, sent = lax.optimization_barrier((collision, sent))
    flipped = call(
        flip_kernel,
        shape((width, depth + 2 * rows), bf16),
        [],
        [collision.reshape(depth, width), adjoint, source],
    )

    start = got[:, :part].T
    full = lax.all_gather(start, "mode", axis=0, tiled=True)
    terms = call(
        first_kernel,
        handed_out(lines, (part, cells)),
        [index],
        [flipped, full],
        [((depth + 2 * rows, cells), bf16), ((groups, part, cells), f32)],
        flops=2 * width * depth * cells,
    )
    start, got, terms = lax.optimization_barrier((start, got, terms))
    transport, rate, sign = call(
        transport_kernel,
        [shape((part, cells), f32), shape((part, cells), f32), shape((part, 1), f32)],
        [index],
        [start, jnp.sum(got[:, part:].astype(f32), axis=1)[None, :], speed[None, :], direction[None, :]],
    )
    state = reduce_over_cells(terms, steps) - transport

    full = lax.all_gather(state.astype(bf16), "mode", axis=0, tiled=True)
    terms = call(
        second_kernel,
        handed_out(lines, (rows, width)),
        [index],
        [flipped, full, state, rate, sign],
        [((groups, part, cells), f32), ((groups, rows, width), f32)],
        flops=2 * width * depth * cells,
    )
    return reduce_over_cells(terms, steps) + relax_factor * source


def solution(mesh):
    modes, groups = mesh.shape["mode"], mesh.shape["cell"]
    mesh = Mesh(mesh.devices.reshape(modes, groups // 2, 2), ("mode", "line", "pair"))
    cell = ("line", "pair")
    in_specs = (
        P(cell, "mode"),
        P(cell, "mode"),
        P(None, cell, None, "mode"),
        P("mode"),
        P("mode"),
        P(cell),
        P(),
    )
    out_specs = P(cell, "mode")
    return jax.shard_map(shards, mesh=mesh, in_specs=in_specs, out_specs=out_specs, check_vma=False)
```

```python
import math

import jax
import jax.numpy as jnp
from jax import lax
from jax.experimental import pallas as pl
from jax.experimental.pallas import tpu as pltpu
from jax.sharding import Mesh, PartitionSpec as P

BRANCH = 48
ITERS = 2


relax_factor = 0.5
VMEM = pl.BlockSpec(memory_space=pltpu.VMEM)
SMEM = pl.BlockSpec(memory_space=pltpu.SMEM)
HBM = pl.BlockSpec(memory_space=pltpu.HBM)
bf16, f32 = jnp.bfloat16, jnp.float32
EXTRA = 16
ME, PAIR, TARGETS = 0, 1, 2


def split(array):
    head = array.astype(bf16)
    return head, (array - head.astype(f32)).astype(bf16)


def padded_bytes(shape, dtype):
    size = jnp.dtype(dtype).itemsize
    if len(shape) < 2:
        return 4096
    sublanes = 8 * 4 // size
    rows, lanes = -(-shape[-2] // sublanes) * sublanes, -(-shape[-1] // 128) * 128
    return math.prod(shape[:-2]) * rows * lanes * size


def call(body, out, scalars, arrays, scratch=(), flops=0, own_copies=False):
    outs = jax.tree.leaves(out)
    bytes_ = sum(padded_bytes(a.shape, a.dtype) for a in (*arrays, *outs))
    held = sum(padded_bytes(shape, dtype) for shape, dtype in scratch)
    scratch = [pltpu.VMEM(shape, dtype) for shape, dtype in scratch]
    if own_copies:
        scratch += [pltpu.VMEM(a.shape, a.dtype) for a in arrays] + [pltpu.SemaphoreType.DMA((len(arrays),))]
    return pl.pallas_call(
        body,
        out_shape=out,
        in_specs=[SMEM] * len(scalars) + [HBM if own_copies else VMEM] * len(arrays),
        out_specs=jax.tree.map(lambda _: VMEM, out),
        scratch_shapes=scratch,
        compiler_params=pltpu.CompilerParams(
            vmem_limit_bytes=56 * 2**20 if own_copies else int(1.5 * (bytes_ + held)) + 4 * 2**20
        ),
        cost_estimate=pl.CostEstimate(flops=flops, bytes_accessed=bytes_, transcendentals=0),
    )(*scalars, *arrays)


def fetch(sources, targets, semaphores):
    copies = [
        pltpu.make_async_copy(source, target, semaphores.at[k])
        for k, (source, target) in enumerate(zip(sources, targets))
    ]
    for copy in copies:
        copy.start()
    for copy in copies:
        copy.wait()


def column_of(row, first, count, each=1):
    wide = row.shape[1]
    place = first + lax.broadcasted_iota(jnp.int32, (count, wide), 0)
    start = lax.broadcasted_iota(jnp.int32, (count, wide), 1) * each
    hit = jnp.logical_and(place >= start, place < start + each)
    return jnp.sum(jnp.where(hit, row, 0.0), axis=1, keepdims=True)


def upwind_change(state, sign):
    cells = state.shape[1]
    spot = lax.broadcasted_iota(jnp.int32, (1, cells), 1)
    after = jnp.where(spot == cells - 1, 0.0, pltpu.roll(state, cells - 1, 1))
    before = jnp.where(spot == 0, 0.0, pltpu.roll(state, 1, 1))
    return state - jnp.where(sign > 0, after, before)


def pack_kernel(adjoint_, labels_, conductance_, out, adjoint, labels, conductance, semaphores):
    fetch((adjoint_, labels_, conductance_), (adjoint, labels, conductance), semaphores)
    groups, rows, columns = out.shape
    part = adjoint.shape[1] // groups
    label = column_of(labels[...].astype(f32), 0, rows)
    kinds = lax.broadcasted_iota(jnp.int32, (rows, conductance.shape[1]), 1).astype(f32)
    kappa = jnp.sum(jnp.where(kinds == label, conductance[...], 0.0), axis=1, keepdims=True)
    first, _ = split(kappa)
    second, third = split(kappa - first.astype(f32))
    column = lax.broadcasted_iota(jnp.int32, (rows, columns - part), 1)
    scale = jnp.where(column == 0, first.astype(f32), 0.0) + jnp.where(column == 1, second.astype(f32), 0.0)
    scale = (scale + jnp.where(column == 2, third.astype(f32), 0.0)).astype(bf16)
    for group in range(groups):
        out[group, :, :part] = adjoint[:, group * part : (group + 1) * part].astype(bf16)
        out[group, :, part:] = scale


def flip_kernel(collision, adjoint, source, out):
    base = split(adjoint[...] + relax_factor * source[...])
    out[...] = jnp.concatenate([collision[...], *base], axis=0).T


def relayed(step, lines):
    return lines // 2 <= step < lines - 1


def pieces_of(lines):
    near = [step for step in range(lines) if relayed(step, lines)]
    return [(step,) for step in near[:0:-1]] + [(*near[:1], 0)]


def straight(lines):
    return [step for step in range(lines - 1, 0, -1) if not relayed(step, lines)]


def hand_out(index, blocks, outs, lines):
    outs = iter(outs)
    own, other = index[PAIR], 1 - index[PAIR]
    for piece in pieces_of(lines):
        for step in piece:
            next(outs)[...] = blocks[2 * index[TARGETS + step] + own]
        out = next(outs)
        for spot, step in enumerate(piece):
            out[spot] = blocks[2 * index[TARGETS + step] + other].astype(bf16)
    for step in straight(lines):
        for pair in (other, own):
            next(outs)[...] = blocks[2 * index[TARGETS + step] + pair].astype(bf16)


def handed_out(lines, block):
    shapes = []
    for piece in pieces_of(lines):
        shapes += [jax.ShapeDtypeStruct(block, f32)] * len(piece)
        shapes += [jax.ShapeDtypeStruct((len(piece), *block), bf16)]
    return shapes + [jax.ShapeDtypeStruct(block, bf16)] * (2 * len(straight(lines)))


def first_kernel(index, flipped, full, *refs):
    *outs, inputs, terms = refs
    groups, part, cells = terms.shape
    lines = groups // 2
    depth = full.shape[0]
    rows = cells // groups
    inputs[:depth, :] = full[...] * bf16(-relax_factor)
    row = lax.broadcasted_iota(jnp.int32, (rows, cells), 0)
    column = lax.broadcasted_iota(jnp.int32, (rows, cells), 1)
    place = (column == row + index[ME] * rows).astype(f32).astype(bf16)
    inputs[depth : depth + rows, :] = place
    inputs[depth + rows :, :] = place
    terms[...] = jnp.dot(flipped[...], inputs[...], preferred_element_type=f32).reshape(terms.shape)
    hand_out(index, terms, outs, lines)


def transport_kernel(index, start, kappa, speed, direction, out, rate_out, sign_out):
    part, _ = out.shape
    first = index[ME] * part
    rate_out[...] = relax_factor * column_of(speed[...], first, part) * kappa[:1, :]
    sign_out[...] = 2.0 * column_of(direction[...].astype(f32), first, part, BRANCH) - 1.0
    out[...] = rate_out[...] * upwind_change(start[...].astype(f32), sign_out[...])


def second_kernel(index, flipped, full, state, rate, sign, *refs):
    *outs, terms, blocks = refs
    groups, part, cells = terms.shape
    lines = groups // 2
    depth = full.shape[0]
    inputs = full[...] * bf16(-relax_factor)
    terms[...] = jnp.dot(flipped[:, :depth], inputs, preferred_element_type=f32).reshape(terms.shape)
    terms[index[ME]] += state[...] - rate[...] * upwind_change(state[...], sign[...])
    blocks[...] = terms[...].reshape(groups * part, cells).T.reshape(blocks.shape)
    hand_out(index, blocks, outs, lines)


def steps_of(count):
    if count & (count - 1):
        return [[(i, (i + step) % count) for i in range(count)] for step in range(count)]
    return [[(i, i ^ step) for i in range(count)] for step in range(count)]


def reduce_over_cells(blocks, steps):
    lines, blocks = len(steps), iter(blocks)
    relays, direct = [], []
    for piece in pieces_of(lines):
        kept = [next(blocks) for _ in piece]
        across = lax.ppermute(next(blocks), "pair", [(0, 1), (1, 0)])
        for spot, step in enumerate(piece):
            block = kept[spot] + across[spot].astype(f32)
            relays.append(lax.ppermute(block.astype(bf16), "line", steps[step]) if step else block)
    for step in straight(lines):
        diagonal = [(2 * i + pair, 2 * j + 1 - pair) for i, j in steps[step] for pair in range(2)]
        across = lax.ppermute(next(blocks), ("line", "pair"), diagonal)
        direct += [lax.ppermute(next(blocks), "line", steps[step]), across]
    terms = direct[:1] + relays + direct[1:]
    result = terms[0].astype(f32)
    for term in terms[1:]:
        result = result + term.astype(f32)
    return result


def shards(adjoint, source, collision, speed, direction, labels, conductance):
    rows, width = adjoint.shape
    lines, pairs, modes = lax.axis_size("line"), lax.axis_size("pair"), lax.axis_size("mode")
    groups = lines * pairs
    part = width // groups
    cells = rows * groups
    depth = modes * part
    line, pair = lax.axis_index("line"), lax.axis_index("pair")
    me = line * pairs + pair
    steps = steps_of(lines)
    targets = [line]
    for step in range(1, lines):
        targets.append(lax.rem(line + step, lines) if lines & (lines - 1) else line ^ step)
    index = jnp.stack([me, pair, *targets]).astype(jnp.int32)
    shape = jax.ShapeDtypeStruct

    columns = -(-(part + EXTRA) // 128) * 128
    sent = call(
        pack_kernel,
        shape((groups, rows, columns), bf16),
        [],
        [adjoint, labels[None, :], conductance[None, :]],
        own_copies=True,
    )
    got = lax.all_to_all(sent, ("line", "pair"), split_axis=0, concat_axis=0, tiled=True).reshape(cells, columns)

    collision, sent = lax.optimization_barrier((collision, sent))
    flipped = call(
        flip_kernel,
        shape((width, depth + 2 * rows), bf16),
        [],
        [collision.reshape(depth, width), adjoint, source],
    )

    start = got[:, :part].T
    full = lax.all_gather(start, "mode", axis=0, tiled=True)
    terms = call(
        first_kernel,
        handed_out(lines, (part, cells)),
        [index],
        [flipped, full],
        [((depth + 2 * rows, cells), bf16), ((groups, part, cells), f32)],
        flops=2 * width * depth * cells,
    )
    start, got, terms = lax.optimization_barrier((start, got, terms))
    transport, rate, sign = call(
        transport_kernel,
        [shape((part, cells), f32), shape((part, cells), f32), shape((part, 1), f32)],
        [index],
        [start, jnp.sum(got[:, part:].astype(f32), axis=1)[None, :], speed[None, :], direction[None, :]],
    )
    state = reduce_over_cells(terms, steps) - transport

    full = lax.all_gather(state.astype(bf16), "mode", axis=0, tiled=True)
    terms = call(
        second_kernel,
        handed_out(lines, (rows, width)),
        [index],
        [flipped, full, state, rate, sign],
        [((groups, part, cells), f32), ((groups, rows, width), f32)],
        flops=2 * width * depth * cells,
    )
    return reduce_over_cells(terms, steps) + relax_factor * source


def solution(mesh):
    modes, groups = mesh.shape["mode"], mesh.shape["cell"]
    mesh = Mesh(mesh.devices.reshape(modes, groups // 2, 2), ("mode", "line", "pair"))
    cell = ("line", "pair")
    in_specs = (
        P(cell, "mode"),
        P(cell, "mode"),
        P(None, cell, None, "mode"),
        P("mode"),
        P("mode"),
        P(cell),
        P(),
    )
    out_specs = P(cell, "mode")
    return jax.shard_map(shards, mesh=mesh, in_specs=in_specs, out_specs=out_specs, check_vma=False)
```

```python
import math

import jax
import jax.numpy as jnp
from jax import lax
from jax.experimental import pallas as pl
from jax.experimental.pallas import tpu as pltpu
from jax.sharding import Mesh, PartitionSpec as P

BRANCH = 48
ITERS = 2


relax_factor = 0.5
VMEM = pl.BlockSpec(memory_space=pltpu.VMEM)
SMEM = pl.BlockSpec(memory_space=pltpu.SMEM)
HBM = pl.BlockSpec(memory_space=pltpu.HBM)
bf16, f32 = jnp.bfloat16, jnp.float32
EXTRA = 16
ME, PAIR, TARGETS = 0, 1, 2


def split(array):
    head = array.astype(bf16)
    return head, (array - head.astype(f32)).astype(bf16)


def padded_bytes(shape, dtype):
    size = jnp.dtype(dtype).itemsize
    if len(shape) < 2:
        return 4096
    sublanes = 8 * 4 // size
    rows, lanes = -(-shape[-2] // sublanes) * sublanes, -(-shape[-1] // 128) * 128
    return math.prod(shape[:-2]) * rows * lanes * size


def call(body, out, scalars, arrays, scratch=(), flops=0, own_copies=False):
    outs = jax.tree.leaves(out)
    bytes_ = sum(padded_bytes(a.shape, a.dtype) for a in (*arrays, *outs))
    held = sum(padded_bytes(shape, dtype) for shape, dtype in scratch)
    scratch = [pltpu.VMEM(shape, dtype) for shape, dtype in scratch]
    if own_copies:
        scratch += [pltpu.VMEM(a.shape, a.dtype) for a in arrays] + [pltpu.SemaphoreType.DMA((len(arrays),))]
    return pl.pallas_call(
        body,
        out_shape=out,
        in_specs=[SMEM] * len(scalars) + [HBM if own_copies else VMEM] * len(arrays),
        out_specs=jax.tree.map(lambda _: VMEM, out),
        scratch_shapes=scratch,
        compiler_params=pltpu.CompilerParams(
            vmem_limit_bytes=56 * 2**20 if own_copies else int(1.5 * (bytes_ + held)) + 4 * 2**20
        ),
        cost_estimate=pl.CostEstimate(flops=flops, bytes_accessed=bytes_, transcendentals=0),
    )(*scalars, *arrays)


def fetch(sources, targets, semaphores):
    copies = [
        pltpu.make_async_copy(source, target, semaphores.at[k])
        for k, (source, target) in enumerate(zip(sources, targets))
    ]
    for copy in copies:
        copy.start()
    for copy in copies:
        copy.wait()


def column_of(row, first, count, each=1):
    wide = row.shape[1]
    place = first + lax.broadcasted_iota(jnp.int32, (count, wide), 0)
    start = lax.broadcasted_iota(jnp.int32, (count, wide), 1) * each
    hit = jnp.logical_and(place >= start, place < start + each)
    return jnp.sum(jnp.where(hit, row, 0.0), axis=1, keepdims=True)


def upwind_change(state, sign):
    cells = state.shape[1]
    spot = lax.broadcasted_iota(jnp.int32, (1, cells), 1)
    after = jnp.where(spot == cells - 1, 0.0, pltpu.roll(state, cells - 1, 1))
    before = jnp.where(spot == 0, 0.0, pltpu.roll(state, 1, 1))
    return state - jnp.where(sign > 0, after, before)


def pack_kernel(adjoint_, labels_, conductance_, out, adjoint, labels, conductance, semaphores):
    fetch((adjoint_, labels_, conductance_), (adjoint, labels, conductance), semaphores)
    groups, rows, columns = out.shape
    part = adjoint.shape[1] // groups
    label = column_of(labels[...].astype(f32), 0, rows)
    kinds = lax.broadcasted_iota(jnp.int32, (rows, conductance.shape[1]), 1).astype(f32)
    kappa = jnp.sum(jnp.where(kinds == label, conductance[...], 0.0), axis=1, keepdims=True)
    first, _ = split(kappa)
    second, third = split(kappa - first.astype(f32))
    column = lax.broadcasted_iota(jnp.int32, (rows, columns - part), 1)
    scale = jnp.where(column == 0, first.astype(f32), 0.0) + jnp.where(column == 1, second.astype(f32), 0.0)
    scale = (scale + jnp.where(column == 2, third.astype(f32), 0.0)).astype(bf16)
    for group in range(groups):
        out[group, :, :part] = adjoint[:, group * part : (group + 1) * part].astype(bf16)
        out[group, :, part:] = scale


def flip_kernel(collision, adjoint, source, flipped, plain):
    base = split(adjoint[...] + relax_factor * source[...])
    flipped[...] = jnp.concatenate([collision[...], *base], axis=0).T
    plain[...] = collision[...]


def relayed(step, lines):
    return lines // 2 <= step < lines - 1


def pieces_of(lines):
    near = [step for step in range(lines) if relayed(step, lines)]
    return [(step,) for step in near[:0:-1]] + [(*near[:1], 0)]


def straight(lines):
    return [step for step in range(lines - 1, 0, -1) if not relayed(step, lines)]


def leaving_first(lines):
    blocks = [(step, False) for piece in pieces_of(lines) for step in piece]
    return blocks + [(step, own) for step in straight(lines) if 2 * step >= lines for own in (False, True)]


def leaving_later(lines):
    blocks = [(step, True) for piece in pieces_of(lines) for step in piece]
    return blocks + [(step, own) for step in straight(lines) if 2 * step < lines for own in (False, True)]


def group_of(index, block):
    step, own = block
    return 2 * index[TARGETS + step] + (index[PAIR] if own else 1 - index[PAIR])


def shapes_first(lines, block):
    pieces = [jax.ShapeDtypeStruct((len(piece), *block), bf16) for piece in pieces_of(lines)]
    return pieces + [jax.ShapeDtypeStruct(block, bf16)] * (len(leaving_first(lines)) - sum(p.shape[0] for p in pieces))


def shapes_later(lines, block):
    staying = sum(len(piece) for piece in pieces_of(lines))
    near = len(leaving_later(lines)) - staying
    return [jax.ShapeDtypeStruct(block, f32)] * staying + [jax.ShapeDtypeStruct(block, bf16)] * near


def hand_out(result, outs):
    first = 0
    for out in outs:
        rows = out.shape[-2]
        if len(out.shape) == 2:
            out[...] = result[first : first + rows].astype(out.dtype)
            first += rows
        else:
            for spot in range(out.shape[0]):
                out[spot] = result[first : first + rows].astype(out.dtype)
                first += rows


def collect(index, blocks, source, target):
    rows = target.shape[0] // len(blocks)
    for spot, block in enumerate(blocks):
        start = pl.multiple_of(group_of(index, block) * rows, 16)
        target[spot * rows : (spot + 1) * rows, :] = source[pl.ds(start, rows), :]


def first_kernel(index, flipped, full, *refs):
    *outs, inputs, chosen = refs
    lines = index.shape[0] - TARGETS
    depth, cells = full.shape
    rows = cells // (2 * lines)
    inputs[:depth, :] = full[...] * bf16(-relax_factor)
    row = lax.broadcasted_iota(jnp.int32, (rows, cells), 0)
    column = lax.broadcasted_iota(jnp.int32, (rows, cells), 1)
    place = (column == row + index[ME] * rows).astype(f32).astype(bf16)
    inputs[depth : depth + rows, :] = place
    inputs[depth + rows :, :] = place
    collect(index, leaving_first(lines), flipped, chosen)
    hand_out(jnp.dot(chosen[...], inputs[...], preferred_element_type=f32), outs)


def first_rest_kernel(index, flipped, inputs, *refs):
    *outs, chosen = refs
    collect(index, leaving_later(index.shape[0] - TARGETS), flipped, chosen)
    hand_out(jnp.dot(chosen[...], inputs[...], preferred_element_type=f32), outs)


def transport_kernel(index, start, kappa, speed, direction, out, rate_out, sign_out):
    part, _ = out.shape
    first = index[ME] * part
    rate_out[...] = relax_factor * column_of(speed[...], first, part) * kappa[:1, :]
    sign_out[...] = 2.0 * column_of(direction[...].astype(f32), first, part, BRANCH) - 1.0
    out[...] = rate_out[...] * upwind_change(start[...].astype(f32), sign_out[...])


def second_product(index, blocks, plain, inputs, kept, outs, chosen, chosen_kept, terms):
    part = kept.shape[1]
    collect(index, blocks, inputs, chosen)
    collect(index, blocks, kept, chosen_kept)
    terms[...] = jnp.dot(chosen[...], plain[...], preferred_element_type=f32)
    for group in range(terms.shape[1] // part):

        @pl.when(index[ME] == group)
        def _():
            terms[:, group * part : (group + 1) * part] += chosen_kept[...]

    hand_out(terms, outs)


def second_kernel(index, plain, full, state, rate, sign, *refs):
    *outs, inputs, kept, chosen, chosen_kept, terms = refs
    lines = index.shape[0] - TARGETS
    depth, cells = full.shape
    part = state.shape[0]
    filled = -(-depth // 128) * 128 - depth
    scaled = full[...] * bf16(-relax_factor)
    scaled = jnp.concatenate([scaled, jnp.zeros((filled, cells), bf16)], axis=0) if filled else scaled
    inputs[...] = scaled.T[:, :depth]
    left = state[...] - rate[...] * upwind_change(state[...], sign[...])
    filled = -(-part // 128) * 128 - part
    left = jnp.concatenate([left, jnp.zeros((filled, cells), f32)], axis=0) if filled else left
    kept[...] = left.T[:, :part]
    second_product(index, leaving_first(lines), plain, inputs, kept, outs, chosen, chosen_kept, terms)


def second_rest_kernel(index, plain, inputs, kept, *refs):
    *outs, chosen, chosen_kept, terms = refs
    blocks = leaving_later(index.shape[0] - TARGETS)
    second_product(index, blocks, plain, inputs, kept, outs, chosen, chosen_kept, terms)


def steps_of(count):
    if count & (count - 1):
        return [[(i, (i + step) % count) for i in range(count)] for step in range(count)]
    return [[(i, i ^ step) for i in range(count)] for step in range(count)]


def reduce_over_cells(first, later, steps):
    lines, first, later = len(steps), iter(first), iter(later)
    relays, direct = [], []
    for piece in pieces_of(lines):
        across = lax.ppermute(next(first), "pair", [(0, 1), (1, 0)])
        for spot, step in enumerate(piece):
            block = next(later) + across[spot].astype(f32)
            relays.append(lax.ppermute(block.astype(bf16), "line", steps[step]) if step else block)
    for step in straight(lines):
        blocks = first if 2 * step >= lines else later
        diagonal = [(2 * i + pair, 2 * j + 1 - pair) for i, j in steps[step] for pair in range(2)]
        across = lax.ppermute(next(blocks), ("line", "pair"), diagonal)
        direct += [lax.ppermute(next(blocks), "line", steps[step]), across]
    terms = direct[:1] + relays + direct[1:]
    result = terms[0].astype(f32)
    for term in terms[1:]:
        result = result + term.astype(f32)
    return result


def shards(adjoint, source, collision, speed, direction, labels, conductance):
    rows, width = adjoint.shape
    lines, pairs, modes = lax.axis_size("line"), lax.axis_size("pair"), lax.axis_size("mode")
    groups = lines * pairs
    part = width // groups
    cells = rows * groups
    depth = modes * part
    line, pair = lax.axis_index("line"), lax.axis_index("pair")
    me = line * pairs + pair
    steps = steps_of(lines)
    targets = [line]
    for step in range(1, lines):
        targets.append(lax.rem(line + step, lines) if lines & (lines - 1) else line ^ step)
    index = jnp.stack([me, pair, *targets]).astype(jnp.int32)
    shape = jax.ShapeDtypeStruct

    columns = -(-(part + EXTRA) // 128) * 128
    sent = call(
        pack_kernel,
        shape((groups, rows, columns), bf16),
        [],
        [adjoint, labels[None, :], conductance[None, :]],
        own_copies=True,
    )
    got = lax.all_to_all(sent, ("line", "pair"), split_axis=0, concat_axis=0, tiled=True).reshape(cells, columns)

    collision, sent = lax.optimization_barrier((collision, sent))
    flipped, plain = call(
        flip_kernel,
        [shape((width, depth + 2 * rows), bf16), shape((depth, width), bf16)],
        [],
        [collision.reshape(depth, width), adjoint, source],
    )

    start = got[:, :part].T
    full = lax.all_gather(start, "mode", axis=0, tiled=True)
    early, late = len(leaving_first(lines)), len(leaving_later(lines))
    *first, inputs = call(
        first_kernel,
        shapes_first(lines, (part, cells)) + [shape((depth + 2 * rows, cells), bf16)],
        [index],
        [flipped, full],
        [((early * part, depth + 2 * rows), bf16)],
        flops=2 * early * part * depth * cells,
    )
    later = call(
        first_rest_kernel,
        shapes_later(lines, (part, cells)),
        [index],
        [flipped, inputs],
        [((late * part, depth + 2 * rows), bf16)],
        flops=2 * late * part * depth * cells,
    )
    start, got, first = lax.optimization_barrier((start, got, first))
    transport, rate, sign = call(
        transport_kernel,
        [shape((part, cells), f32), shape((part, cells), f32), shape((part, 1), f32)],
        [index],
        [start, jnp.sum(got[:, part:].astype(f32), axis=1)[None, :], speed[None, :], direction[None, :]],
    )
    state = reduce_over_cells(first, later, steps) - transport

    full = lax.all_gather(state.astype(bf16), "mode", axis=0, tiled=True)
    scratch = [[((count * rows, depth), bf16), ((count * rows, part), f32), ((count * rows, width), f32)] for count in (early, late)]
    *first, inputs, kept = call(
        second_kernel,
        shapes_first(lines, (rows, width)) + [shape((cells, depth), bf16), shape((cells, part), f32)],
        [index],
        [plain, full, state, rate, sign],
        scratch[0],
        flops=2 * early * rows * depth * width,
    )
    later = call(
        second_rest_kernel,
        shapes_later(lines, (rows, width)),
        [index],
        [plain, inputs, kept],
        scratch[1],
        flops=2 * late * rows * depth * width,
    )
    source, first = lax.optimization_barrier((source, first))
    return reduce_over_cells(first, later, steps) + relax_factor * source


def solution(mesh):
    modes, groups = mesh.shape["mode"], mesh.shape["cell"]
    mesh = Mesh(mesh.devices.reshape(modes, groups // 2, 2), ("mode", "line", "pair"))
    cell = ("line", "pair")
    in_specs = (
        P(cell, "mode"),
        P(cell, "mode"),
        P(None, cell, None, "mode"),
        P("mode"),
        P("mode"),
        P(cell),
        P(),
    )
    out_specs = P(cell, "mode")
    return jax.shard_map(shards, mesh=mesh, in_specs=in_specs, out_specs=out_specs, check_vma=False)
```

```python
import math

import jax
import jax.numpy as jnp
from jax import lax
from jax.experimental import pallas as pl
from jax.experimental.pallas import tpu as pltpu
from jax.sharding import Mesh, PartitionSpec as P

BRANCH = 48
ITERS = 2


relax_factor = 0.5
VMEM = pl.BlockSpec(memory_space=pltpu.VMEM)
SMEM = pl.BlockSpec(memory_space=pltpu.SMEM)
HBM = pl.BlockSpec(memory_space=pltpu.HBM)
bf16, f32 = jnp.bfloat16, jnp.float32
EXTRA = 16
ME, PAIR, TARGETS = 0, 1, 2


def split(array):
    head = array.astype(bf16)
    return head, (array - head.astype(f32)).astype(bf16)


def padded_bytes(shape, dtype):
    size = jnp.dtype(dtype).itemsize
    if len(shape) < 2:
        return 4096
    sublanes = 8 * 4 // size
    rows, lanes = -(-shape[-2] // sublanes) * sublanes, -(-shape[-1] // 128) * 128
    return math.prod(shape[:-2]) * rows * lanes * size


def call(body, out, scalars, arrays, scratch=(), flops=0, own_copies=False):
    outs = jax.tree.leaves(out)
    bytes_ = sum(padded_bytes(a.shape, a.dtype) for a in (*arrays, *outs))
    held = sum(padded_bytes(shape, dtype) for shape, dtype in scratch)
    scratch = [pltpu.VMEM(shape, dtype) for shape, dtype in scratch]
    if own_copies:
        scratch += [pltpu.VMEM(a.shape, a.dtype) for a in arrays] + [pltpu.SemaphoreType.DMA((len(arrays),))]
    return pl.pallas_call(
        body,
        out_shape=out,
        in_specs=[SMEM] * len(scalars) + [HBM if own_copies else VMEM] * len(arrays),
        out_specs=jax.tree.map(lambda _: VMEM, out),
        scratch_shapes=scratch,
        compiler_params=pltpu.CompilerParams(
            vmem_limit_bytes=56 * 2**20 if own_copies else int(1.5 * (bytes_ + held)) + 4 * 2**20
        ),
        cost_estimate=pl.CostEstimate(flops=flops, bytes_accessed=bytes_, transcendentals=0),
    )(*scalars, *arrays)


def fetch(sources, targets, semaphores):
    copies = [
        pltpu.make_async_copy(source, target, semaphores.at[k])
        for k, (source, target) in enumerate(zip(sources, targets))
    ]
    for copy in copies:
        copy.start()
    for copy in copies:
        copy.wait()


def column_of(row, first, count, each=1):
    wide = row.shape[1]
    place = first + lax.broadcasted_iota(jnp.int32, (count, wide), 0)
    start = lax.broadcasted_iota(jnp.int32, (count, wide), 1) * each
    hit = jnp.logical_and(place >= start, place < start + each)
    return jnp.sum(jnp.where(hit, row, 0.0), axis=1, keepdims=True)


def upwind_change(state, sign):
    cells = state.shape[1]
    spot = lax.broadcasted_iota(jnp.int32, (1, cells), 1)
    after = jnp.where(spot == cells - 1, 0.0, pltpu.roll(state, cells - 1, 1))
    before = jnp.where(spot == 0, 0.0, pltpu.roll(state, 1, 1))
    return state - jnp.where(sign > 0, after, before)


def pack_kernel(adjoint_, labels_, conductance_, out, adjoint, labels, conductance, semaphores):
    fetch((adjoint_, labels_, conductance_), (adjoint, labels, conductance), semaphores)
    groups, rows, columns = out.shape
    part = adjoint.shape[1] // groups
    label = column_of(labels[...].astype(f32), 0, rows)
    kinds = lax.broadcasted_iota(jnp.int32, (rows, conductance.shape[1]), 1).astype(f32)
    kappa = jnp.sum(jnp.where(kinds == label, conductance[...], 0.0), axis=1, keepdims=True)
    first, _ = split(kappa)
    second, third = split(kappa - first.astype(f32))
    column = lax.broadcasted_iota(jnp.int32, (rows, columns - part), 1)
    scale = jnp.where(column == 0, first.astype(f32), 0.0) + jnp.where(column == 1, second.astype(f32), 0.0)
    scale = (scale + jnp.where(column == 2, third.astype(f32), 0.0)).astype(bf16)
    for group in range(groups):
        out[group, :, :part] = adjoint[:, group * part : (group + 1) * part].astype(bf16)
        out[group, :, part:] = scale


def flip_kernel(collision, adjoint, source, out):
    base = split(adjoint[...] + relax_factor * source[...])
    out[...] = jnp.concatenate([collision[...], *base], axis=0).T


def relayed(step, lines):
    return lines // 2 <= step < lines - 1


def pieces_of(lines):
    return [(step,) for step in range(lines - 1, -1, -1) if step == 0 or relayed(step, lines)]


def straight(lines):
    return [step for step in range(lines - 1, 0, -1) if not relayed(step, lines)]


def hand_out(index, blocks, outs, lines):
    outs = iter(outs)
    own, other = index[PAIR], 1 - index[PAIR]
    for piece in pieces_of(lines):
        for step in piece:
            next(outs)[...] = blocks[2 * index[TARGETS + step] + own]
        out = next(outs)
        for spot, step in enumerate(piece):
            out[spot] = blocks[2 * index[TARGETS + step] + other].astype(bf16)
    for step in straight(lines):
        for pair in (other, own):
            next(outs)[...] = blocks[2 * index[TARGETS + step] + pair].astype(bf16)


def handed_out(lines, block):
    shapes = []
    for piece in pieces_of(lines):
        shapes += [jax.ShapeDtypeStruct(block, f32)] * len(piece)
        shapes += [jax.ShapeDtypeStruct((len(piece), *block), bf16)]
    return shapes + [jax.ShapeDtypeStruct(block, bf16)] * (2 * len(straight(lines)))


def first_kernel(index, flipped, full, *refs):
    *outs, inputs, terms = refs
    groups, part, cells = terms.shape
    lines = groups // 2
    depth = full.shape[0]
    rows = cells // groups
    inputs[:depth, :] = full[...] * bf16(-relax_factor)
    row = lax.broadcasted_iota(jnp.int32, (rows, cells), 0)
    column = lax.broadcasted_iota(jnp.int32, (rows, cells), 1)
    place = (column == row + index[ME] * rows).astype(f32).astype(bf16)
    inputs[depth : depth + rows, :] = place
    inputs[depth + rows :, :] = place
    terms[...] = jnp.dot(flipped[...], inputs[...], preferred_element_type=f32).reshape(terms.shape)
    hand_out(index, terms, outs, lines)


def transport_kernel(index, start, kappa, speed, direction, out, rate_out, sign_out):
    part, _ = out.shape
    first = index[ME] * part
    rate_out[...] = relax_factor * column_of(speed[...], first, part) * kappa[:1, :]
    sign_out[...] = 2.0 * column_of(direction[...].astype(f32), first, part, BRANCH) - 1.0
    out[...] = rate_out[...] * upwind_change(start[...].astype(f32), sign_out[...])


def second_kernel(index, flipped, full, state, rate, sign, *refs):
    *outs, terms, blocks = refs
    groups, part, cells = terms.shape
    lines = groups // 2
    depth = full.shape[0]
    inputs = full[...] * bf16(-relax_factor)
    terms[...] = jnp.dot(flipped[:, :depth], inputs, preferred_element_type=f32).reshape(terms.shape)
    terms[index[ME]] += state[...] - rate[...] * upwind_change(state[...], sign[...])
    blocks[...] = terms[...].reshape(groups * part, cells).T.reshape(blocks.shape)
    hand_out(index, blocks, outs, lines)


def steps_of(count):
    if count & (count - 1):
        return [[(i, (i + step) % count) for i in range(count)] for step in range(count)]
    return [[(i, i ^ step) for i in range(count)] for step in range(count)]


def reduce_over_cells(blocks, steps):
    lines, blocks = len(steps), iter(blocks)
    swap = [(0, 1), (1, 0)]
    pieces = [(piece[0], next(blocks), next(blocks)) for piece in pieces_of(lines)]
    far = [step for step in straight(lines) if 2 * step >= lines]
    near = [step for step in straight(lines) if 2 * step < lines]
    far_blocks = [(next(blocks), next(blocks)) for _ in far]
    (_, own, late), near_blocks = pieces.pop(), [(next(blocks), next(blocks)) for _ in near]
    terms = []
    for step, kept, sent in pieces:
        block = (kept + lax.ppermute(sent, "pair", swap)[0].astype(f32)).astype(bf16)
        block, late, near_blocks = lax.optimization_barrier((block, late, near_blocks))
        terms.append(lax.ppermute(block, "line", steps[step]))
    straight_terms = []
    for step, (across, along) in zip(far + near, far_blocks + near_blocks):
        diagonal = [(2 * i + pair, 2 * j + 1 - pair) for i, j in steps[step] for pair in range(2)]
        straight_terms.append(lax.ppermute(along, "line", steps[step]))
        straight_terms.append(lax.ppermute(across, ("line", "pair"), diagonal))
    terms = straight_terms[:1] + terms + straight_terms[1:] + [lax.ppermute(late, "pair", swap)[0]]
    result = own
    for term in terms:
        result = result + term.astype(f32)
    return result


def shards(adjoint, source, collision, speed, direction, labels, conductance):
    rows, width = adjoint.shape
    lines, pairs, modes = lax.axis_size("line"), lax.axis_size("pair"), lax.axis_size("mode")
    groups = lines * pairs
    part = width // groups
    cells = rows * groups
    depth = modes * part
    line, pair = lax.axis_index("line"), lax.axis_index("pair")
    me = line * pairs + pair
    steps = steps_of(lines)
    targets = [line]
    for step in range(1, lines):
        targets.append(lax.rem(line + step, lines) if lines & (lines - 1) else line ^ step)
    index = jnp.stack([me, pair, *targets]).astype(jnp.int32)
    shape = jax.ShapeDtypeStruct

    columns = -(-(part + EXTRA) // 128) * 128
    sent = call(
        pack_kernel,
        shape((groups, rows, columns), bf16),
        [],
        [adjoint, labels[None, :], conductance[None, :]],
        own_copies=True,
    )
    got = lax.all_to_all(sent, ("line", "pair"), split_axis=0, concat_axis=0, tiled=True).reshape(cells, columns)

    collision, sent = lax.optimization_barrier((collision, sent))
    flipped = call(
        flip_kernel,
        shape((width, depth + 2 * rows), bf16),
        [],
        [collision.reshape(depth, width), adjoint, source],
    )

    start = got[:, :part].T
    full = lax.all_gather(start, "mode", axis=0, tiled=True)
    terms = call(
        first_kernel,
        handed_out(lines, (part, cells)),
        [index],
        [flipped, full],
        [((depth + 2 * rows, cells), bf16), ((groups, part, cells), f32)],
        flops=2 * width * depth * cells,
    )
    start, got, terms = lax.optimization_barrier((start, got, terms))
    transport, rate, sign = call(
        transport_kernel,
        [shape((part, cells), f32), shape((part, cells), f32), shape((part, 1), f32)],
        [index],
        [start, jnp.sum(got[:, part:].astype(f32), axis=1)[None, :], speed[None, :], direction[None, :]],
    )
    state = reduce_over_cells(terms, steps) - transport

    full = lax.all_gather(state.astype(bf16), "mode", axis=0, tiled=True)
    terms = call(
        second_kernel,
        handed_out(lines, (rows, width)),
        [index],
        [flipped, full, state, rate, sign],
        [((groups, part, cells), f32), ((groups, rows, width), f32)],
        flops=2 * width * depth * cells,
    )
    return reduce_over_cells(terms, steps) + relax_factor * source


def solution(mesh):
    modes, groups = mesh.shape["mode"], mesh.shape["cell"]
    mesh = Mesh(mesh.devices.reshape(modes, groups // 2, 2), ("mode", "line", "pair"))
    cell = ("line", "pair")
    in_specs = (
        P(cell, "mode"),
        P(cell, "mode"),
        P(None, cell, None, "mode"),
        P("mode"),
        P("mode"),
        P(cell),
        P(),
    )
    out_specs = P(cell, "mode")
    return jax.shard_map(shards, mesh=mesh, in_specs=in_specs, out_specs=out_specs, check_vma=False)
```

```python
import math

import jax
import jax.numpy as jnp
from jax import lax
from jax.experimental import pallas as pl
from jax.experimental.pallas import tpu as pltpu
from jax.sharding import Mesh, PartitionSpec as P

BRANCH = 48
ITERS = 2


relax_factor = 0.5
VMEM = pl.BlockSpec(memory_space=pltpu.VMEM)
SMEM = pl.BlockSpec(memory_space=pltpu.SMEM)
HBM = pl.BlockSpec(memory_space=pltpu.HBM)
bf16, f32 = jnp.bfloat16, jnp.float32
EXTRA = 16
ME, PAIR, TARGETS = 0, 1, 2


def split(array):
    head = array.astype(bf16)
    return head, (array - head.astype(f32)).astype(bf16)


def padded_bytes(shape, dtype):
    size = jnp.dtype(dtype).itemsize
    if len(shape) < 2:
        return 4096
    sublanes = 8 * 4 // size
    rows, lanes = -(-shape[-2] // sublanes) * sublanes, -(-shape[-1] // 128) * 128
    return math.prod(shape[:-2]) * rows * lanes * size


def call(body, out, scalars, arrays, scratch=(), flops=0, own_copies=False):
    outs = jax.tree.leaves(out)
    bytes_ = sum(padded_bytes(a.shape, a.dtype) for a in (*arrays, *outs))
    held = sum(padded_bytes(shape, dtype) for shape, dtype in scratch)
    scratch = [pltpu.VMEM(shape, dtype) for shape, dtype in scratch]
    if own_copies:
        scratch += [pltpu.VMEM(a.shape, a.dtype) for a in arrays] + [pltpu.SemaphoreType.DMA((len(arrays),))]
    return pl.pallas_call(
        body,
        out_shape=out,
        in_specs=[SMEM] * len(scalars) + [HBM if own_copies else VMEM] * len(arrays),
        out_specs=jax.tree.map(lambda _: VMEM, out),
        scratch_shapes=scratch,
        compiler_params=pltpu.CompilerParams(
            vmem_limit_bytes=56 * 2**20 if own_copies else int(1.5 * (bytes_ + held)) + 4 * 2**20
        ),
        cost_estimate=pl.CostEstimate(flops=flops, bytes_accessed=bytes_, transcendentals=0),
    )(*scalars, *arrays)


def fetch(sources, targets, semaphores):
    copies = [
        pltpu.make_async_copy(source, target, semaphores.at[k])
        for k, (source, target) in enumerate(zip(sources, targets))
    ]
    for copy in copies:
        copy.start()
    for copy in copies:
        copy.wait()


def column_of(row, first, count, each=1):
    wide = row.shape[1]
    place = first + lax.broadcasted_iota(jnp.int32, (count, wide), 0)
    start = lax.broadcasted_iota(jnp.int32, (count, wide), 1) * each
    hit = jnp.logical_and(place >= start, place < start + each)
    return jnp.sum(jnp.where(hit, row, 0.0), axis=1, keepdims=True)


def upwind_change(state, sign):
    cells = state.shape[1]
    spot = lax.broadcasted_iota(jnp.int32, (1, cells), 1)
    after = jnp.where(spot == cells - 1, 0.0, pltpu.roll(state, cells - 1, 1))
    before = jnp.where(spot == 0, 0.0, pltpu.roll(state, 1, 1))
    return state - jnp.where(sign > 0, after, before)


def pack_kernel(adjoint_, labels_, conductance_, out, adjoint, labels, conductance, semaphores):
    fetch((adjoint_, labels_, conductance_), (adjoint, labels, conductance), semaphores)
    groups, rows, columns = out.shape
    part = adjoint.shape[1] // groups
    label = column_of(labels[...].astype(f32), 0, rows)
    kinds = lax.broadcasted_iota(jnp.int32, (rows, conductance.shape[1]), 1).astype(f32)
    kappa = jnp.sum(jnp.where(kinds == label, conductance[...], 0.0), axis=1, keepdims=True)
    first, _ = split(kappa)
    second, third = split(kappa - first.astype(f32))
    column = lax.broadcasted_iota(jnp.int32, (rows, columns - part), 1)
    scale = jnp.where(column == 0, first.astype(f32), 0.0) + jnp.where(column == 1, second.astype(f32), 0.0)
    scale = (scale + jnp.where(column == 2, third.astype(f32), 0.0)).astype(bf16)
    for group in range(groups):
        out[group, :, :part] = adjoint[:, group * part : (group + 1) * part].astype(bf16)
        out[group, :, part:] = scale


def index_of(lines):
    line, pair = lax.axis_index("line"), lax.axis_index("pair")
    shifted = lines & (lines - 1)
    targets = [lax.rem(line + step, lines) if shifted else line ^ step for step in range(lines)]
    return [2 * line + pair, pair, *targets]


def flip_kernel(collision, adjoint, source, out, place):
    base = split(adjoint[...] + relax_factor * source[...])
    out[...] = jnp.concatenate([collision[...] * bf16(-relax_factor), *base], axis=0).T
    rows, cells = adjoint.shape[0], place.shape[1]
    index = index_of(cells // (2 * rows))
    row = lax.broadcasted_iota(jnp.int32, (rows, cells), 0)
    column = lax.broadcasted_iota(jnp.int32, (rows, cells), 1)
    mine = (column == row + index[ME] * rows).astype(f32).astype(bf16)
    place[:rows, :] = mine
    place[rows:, :] = mine


def relayed(step, lines):
    return lines // 2 <= step < lines - 1


def pieces_of(lines):
    return [(step,) for step in range(lines - 1, -1, -1) if step == 0 or relayed(step, lines)]


def straight(lines):
    return [step for step in range(lines - 1, 0, -1) if not relayed(step, lines)]


def hand_out(index, blocks, outs, lines):
    outs = iter(outs)
    own, other = index[PAIR], 1 - index[PAIR]
    for piece in pieces_of(lines):
        for step in piece:
            next(outs)[...] = blocks[2 * index[TARGETS + step] + own]
        out = next(outs)
        for spot, step in enumerate(piece):
            out[spot] = blocks[2 * index[TARGETS + step] + other].astype(bf16)
    for step in straight(lines):
        for pair in (other, own):
            next(outs)[...] = blocks[2 * index[TARGETS + step] + pair].astype(bf16)


def handed_out(lines, block):
    shapes = []
    for piece in pieces_of(lines):
        shapes += [jax.ShapeDtypeStruct(block, f32)] * len(piece)
        shapes += [jax.ShapeDtypeStruct((len(piece), *block), bf16)]
    return shapes + [jax.ShapeDtypeStruct(block, bf16)] * (2 * len(straight(lines)))


def first_kernel(flipped, place, full, *refs):
    *outs, terms = refs
    lines = terms.shape[0] // 2
    depth = full.shape[0]
    result = jnp.dot(flipped[:, :depth], full[...], preferred_element_type=f32)
    result += jnp.dot(flipped[:, depth:], place[...], preferred_element_type=f32)
    terms[...] = result.reshape(terms.shape)
    hand_out(index_of(lines), terms, outs, lines)


def transport_kernel(start, kappa, speed, direction, out, rate_out, sign_out):
    part, _ = out.shape
    lines = speed.shape[1] // (2 * part)
    first = index_of(lines)[ME] * part
    rate_out[...] = relax_factor * column_of(speed[...], first, part) * kappa[:1, :]
    sign_out[...] = 2.0 * column_of(direction[...].astype(f32), first, part, BRANCH) - 1.0
    out[...] = rate_out[...] * upwind_change(start[...].astype(f32), sign_out[...])


def second_kernel(flipped, full, state, rate, sign, *refs):
    *outs, terms, blocks = refs
    groups, part, cells = terms.shape
    lines = groups // 2
    depth = full.shape[0]
    index = index_of(lines)
    terms[...] = jnp.dot(flipped[:, :depth], full[...], preferred_element_type=f32).reshape(terms.shape)
    terms[index[ME]] += state[...] - rate[...] * upwind_change(state[...], sign[...])
    blocks[...] = terms[...].reshape(groups * part, cells).T.reshape(blocks.shape)
    hand_out(index, blocks, outs, lines)


def steps_of(count):
    if count & (count - 1):
        return [[(i, (i + step) % count) for i in range(count)] for step in range(count)]
    return [[(i, i ^ step) for i in range(count)] for step in range(count)]


def reduce_over_cells(blocks, steps):
    lines, blocks = len(steps), iter(blocks)
    swap = [(0, 1), (1, 0)]
    pieces = [(piece[0], next(blocks), next(blocks)) for piece in pieces_of(lines)]
    far = [step for step in straight(lines) if 2 * step >= lines]
    near = [step for step in straight(lines) if 2 * step < lines]
    far_blocks = [(next(blocks), next(blocks)) for _ in far]
    (_, own, late), near_blocks = pieces.pop(), [(next(blocks), next(blocks)) for _ in near]
    terms = []
    for step, kept, sent in pieces:
        block = (kept + lax.ppermute(sent, "pair", swap)[0].astype(f32)).astype(bf16)
        block, late, near_blocks = lax.optimization_barrier((block, late, near_blocks))
        terms.append(lax.ppermute(block, "line", steps[step]))
    straight_terms = []
    for step, (across, along) in zip(far + near, far_blocks + near_blocks):
        diagonal = [(2 * i + pair, 2 * j + 1 - pair) for i, j in steps[step] for pair in range(2)]
        straight_terms.append(lax.ppermute(along, "line", steps[step]))
        straight_terms.append(lax.ppermute(across, ("line", "pair"), diagonal))
    terms = straight_terms[:1] + terms + straight_terms[1:] + [lax.ppermute(late, "pair", swap)[0]]
    result = own
    for term in terms:
        result = result + term.astype(f32)
    return result


def shards(adjoint, source, collision, speed, direction, labels, conductance):
    rows, width = adjoint.shape
    lines, pairs, modes = lax.axis_size("line"), lax.axis_size("pair"), lax.axis_size("mode")
    groups = lines * pairs
    part = width // groups
    cells = rows * groups
    depth = modes * part
    steps = steps_of(lines)
    shape = jax.ShapeDtypeStruct

    columns = -(-(part + EXTRA) // 128) * 128
    sent = call(
        pack_kernel,
        shape((groups, rows, columns), bf16),
        [],
        [adjoint, labels[None, :], conductance[None, :]],
        own_copies=True,
    )
    got = lax.all_to_all(sent, ("line", "pair"), split_axis=0, concat_axis=0, tiled=True).reshape(cells, columns)

    collision, sent = lax.optimization_barrier((collision, sent))
    flipped, place = call(
        flip_kernel,
        [shape((width, depth + 2 * rows), bf16), shape((2 * rows, cells), bf16)],
        [],
        [collision.reshape(depth, width), adjoint, source],
    )

    start = got[:, :part].T
    full = lax.all_gather(start, "mode", axis=0, tiled=True)
    terms = call(
        first_kernel,
        handed_out(lines, (part, cells)),
        [],
        [flipped, place, full],
        [((groups, part, cells), f32)],
        flops=2 * width * depth * cells,
    )
    start, got, terms = lax.optimization_barrier((start, got, terms))
    transport, rate, sign = call(
        transport_kernel,
        [shape((part, cells), f32), shape((part, cells), f32), shape((part, 1), f32)],
        [],
        [start, jnp.sum(got[:, part:].astype(f32), axis=1)[None, :], speed[None, :], direction[None, :]],
    )
    state = reduce_over_cells(terms, steps) - transport

    full = lax.all_gather(state.astype(bf16), "mode", axis=0, tiled=True)
    terms = call(
        second_kernel,
        handed_out(lines, (rows, width)),
        [],
        [flipped, full, state, rate, sign],
        [((groups, part, cells), f32), ((groups, rows, width), f32)],
        flops=2 * width * depth * cells,
    )
    return reduce_over_cells(terms, steps) + relax_factor * source


def solution(mesh):
    modes, groups = mesh.shape["mode"], mesh.shape["cell"]
    mesh = Mesh(mesh.devices.reshape(modes, groups // 2, 2), ("mode", "line", "pair"))
    cell = ("line", "pair")
    in_specs = (
        P(cell, "mode"),
        P(cell, "mode"),
        P(None, cell, None, "mode"),
        P("mode"),
        P("mode"),
        P(cell),
        P(),
    )
    out_specs = P(cell, "mode")
    return jax.shard_map(shards, mesh=mesh, in_specs=in_specs, out_specs=out_specs, check_vma=False)
```

```python
import math

import jax
import jax.numpy as jnp
from jax import lax
from jax.experimental import pallas as pl
from jax.experimental.pallas import tpu as pltpu
from jax.sharding import Mesh, PartitionSpec as P

BRANCH = 48
ITERS = 2


relax_factor = 0.5
VMEM = pl.BlockSpec(memory_space=pltpu.VMEM)
SMEM = pl.BlockSpec(memory_space=pltpu.SMEM)
HBM = pl.BlockSpec(memory_space=pltpu.HBM)
bf16, f32 = jnp.bfloat16, jnp.float32
EXTRA = 16


def split(array):
    head = array.astype(bf16)
    return head, (array - head.astype(f32)).astype(bf16)


def padded_bytes(shape, dtype):
    size = jnp.dtype(dtype).itemsize
    if len(shape) < 2:
        return 4096
    sublanes = 8 * 4 // size
    rows, lanes = -(-shape[-2] // sublanes) * sublanes, -(-shape[-1] // 128) * 128
    return math.prod(shape[:-2]) * rows * lanes * size


def call(body, out, scalars, arrays, scratch=(), flops=0, own_copies=False):
    outs = jax.tree.leaves(out)
    bytes_ = sum(padded_bytes(a.shape, a.dtype) for a in (*arrays, *outs))
    held = sum(padded_bytes(shape, dtype) for shape, dtype in scratch)
    scratch = [pltpu.VMEM(shape, dtype) for shape, dtype in scratch]
    if own_copies:
        scratch += [pltpu.VMEM(a.shape, a.dtype) for a in arrays] + [pltpu.SemaphoreType.DMA((len(arrays),))]
    return pl.pallas_call(
        body,
        out_shape=out,
        in_specs=[SMEM] * len(scalars) + [HBM if own_copies else VMEM] * len(arrays),
        out_specs=jax.tree.map(lambda _: VMEM, out),
        scratch_shapes=scratch,
        compiler_params=pltpu.CompilerParams(
            vmem_limit_bytes=56 * 2**20 if own_copies else int(1.5 * (bytes_ + held)) + 4 * 2**20
        ),
        cost_estimate=pl.CostEstimate(flops=flops, bytes_accessed=bytes_, transcendentals=0),
    )(*scalars, *arrays)


def fetch(sources, targets, semaphores):
    copies = [
        pltpu.make_async_copy(source, target, semaphores.at[k])
        for k, (source, target) in enumerate(zip(sources, targets))
    ]
    for copy in copies:
        copy.start()
    for copy in copies:
        copy.wait()


def column_of(row, first, count, each=1):
    wide = row.shape[1]
    place = first + lax.broadcasted_iota(jnp.int32, (count, wide), 0)
    start = lax.broadcasted_iota(jnp.int32, (count, wide), 1) * each
    hit = jnp.logical_and(place >= start, place < start + each)
    return jnp.sum(jnp.where(hit, row, 0.0), axis=1, keepdims=True)


def upwind_change(state, sign):
    cells = state.shape[1]
    spot = lax.broadcasted_iota(jnp.int32, (1, cells), 1)
    after = jnp.where(spot == cells - 1, 0.0, pltpu.roll(state, cells - 1, 1))
    before = jnp.where(spot == 0, 0.0, pltpu.roll(state, 1, 1))
    return state - jnp.where(sign > 0, after, before)


def pack_kernel(adjoint_, labels_, conductance_, out, adjoint, labels, conductance, semaphores):
    fetch((adjoint_, labels_, conductance_), (adjoint, labels, conductance), semaphores)
    groups, rows, columns = out.shape
    part = adjoint.shape[1] // groups
    label = column_of(labels[...].astype(f32), 0, rows)
    kinds = lax.broadcasted_iota(jnp.int32, (rows, conductance.shape[1]), 1).astype(f32)
    kappa = jnp.sum(jnp.where(kinds == label, conductance[...], 0.0), axis=1, keepdims=True)
    first, _ = split(kappa)
    second, third = split(kappa - first.astype(f32))
    column = lax.broadcasted_iota(jnp.int32, (rows, columns - part), 1)
    scale = jnp.where(column == 0, first.astype(f32), 0.0) + jnp.where(column == 1, second.astype(f32), 0.0)
    scale = (scale + jnp.where(column == 2, third.astype(f32), 0.0)).astype(bf16)
    for group in range(groups):
        out[group, :, :part] = adjoint[:, group * part : (group + 1) * part].astype(bf16)
        out[group, :, part:] = scale


def index_of():
    line, pair = lax.axis_index("line"), lax.axis_index("pair")
    return line, pair, 2 * line + pair


def flip_kernel(collision, adjoint, source, out, place):
    base = split(adjoint[...] + relax_factor * source[...])
    out[...] = jnp.concatenate([collision[...] * bf16(-relax_factor), *base], axis=0).T
    rows, cells = adjoint.shape[0], place.shape[1]
    _, _, me = index_of()
    row = lax.broadcasted_iota(jnp.int32, (rows, cells), 0)
    column = lax.broadcasted_iota(jnp.int32, (rows, cells), 1)
    mine = (column == row + me * rows).astype(f32).astype(bf16)
    place[:rows, :] = mine
    place[rows:, :] = mine


def neighbours(lines):
    return [(0, 1)] + ([(1, 0), (1, 1)] if lines > 1 else [])


def fours(lines):
    return max(lines // 2, 1)


def hand_out(blocks, outs, lines):
    line, pair, _ = index_of()
    outs = iter(outs)
    for four in range(fours(lines)):
        next(outs)[...] = blocks[2 * (line ^ (2 * four)) + pair]
    if fours(lines) > 1:
        for bit, other in neighbours(lines):
            out = next(outs)
            for four in range(1, fours(lines)):
                out[four - 1] = blocks[2 * (line ^ (2 * four + bit)) + (pair ^ other)].astype(bf16)
    for bit, other in neighbours(lines):
        next(outs)[...] = blocks[2 * (line ^ bit) + (pair ^ other)].astype(bf16)


def handed_out(lines, block):
    count = fours(lines)
    kept = [jax.ShapeDtypeStruct(block, f32)] * count
    far = [jax.ShapeDtypeStruct((count - 1, *block), bf16)] * len(neighbours(lines)) if count > 1 else []
    return kept + far + [jax.ShapeDtypeStruct(block, bf16)] * len(neighbours(lines))


def first_kernel(flipped, place, full, *refs):
    *outs, terms = refs
    lines = terms.shape[0] // 2
    depth = full.shape[0]
    result = jnp.dot(flipped[:, :depth], full[...], preferred_element_type=f32)
    result += jnp.dot(flipped[:, depth:], place[...], preferred_element_type=f32)
    terms[...] = result.reshape(terms.shape)
    hand_out(terms, outs, lines)


def transport_kernel(start, kappa, speed, direction, out, rate_out, sign_out):
    part, _ = out.shape
    first = index_of()[2] * part
    rate_out[...] = relax_factor * column_of(speed[...], first, part) * kappa[:1, :]
    sign_out[...] = 2.0 * column_of(direction[...].astype(f32), first, part, BRANCH) - 1.0
    out[...] = rate_out[...] * upwind_change(start[...].astype(f32), sign_out[...])


def second_kernel(flipped, full, state, rate, sign, *refs):
    *outs, terms, blocks = refs
    groups, part, cells = terms.shape
    lines = groups // 2
    depth = full.shape[0]
    _, _, me = index_of()
    terms[...] = jnp.dot(flipped[:, :depth], full[...], preferred_element_type=f32).reshape(terms.shape)
    terms[me] += state[...] - rate[...] * upwind_change(state[...], sign[...])
    blocks[...] = terms[...].reshape(groups * part, cells).T.reshape(blocks.shape)
    hand_out(blocks, outs, lines)


def to_neighbour(block, lines, bit, other):
    pairs = [(2 * i + p, 2 * (i ^ bit) + (p ^ other)) for i in range(lines) for p in range(2)]
    return lax.ppermute(block, ("line", "pair"), pairs)


def reduce_over_cells(blocks, lines):
    blocks = list(blocks)
    count, ways = fours(lines), neighbours(lines)
    kept, blocks = blocks[:count], blocks[count:]
    terms = []
    if count > 1:
        far, blocks = blocks[: len(ways)], blocks[len(ways) :]
        arrived = [to_neighbour(block, lines, *way) for block, way in zip(far, ways)]
        for four in range(1, count):
            block = kept[four]
            for part in arrived:
                block = block + part[four - 1].astype(f32)
            block, blocks[-1] = lax.optimization_barrier((block.astype(bf16), blocks[-1]))
            terms.append(lax.ppermute(block, "line", [(i, i ^ (2 * four)) for i in range(lines)]))
    terms += [to_neighbour(block, lines, *way) for block, way in zip(blocks, ways)]
    result = kept[0]
    for term in terms:
        result = result + term.astype(f32)
    return result


def shards(adjoint, source, collision, speed, direction, labels, conductance):
    rows, width = adjoint.shape
    lines, pairs, modes = lax.axis_size("line"), lax.axis_size("pair"), lax.axis_size("mode")
    groups = lines * pairs
    part = width // groups
    cells = rows * groups
    depth = modes * part
    shape = jax.ShapeDtypeStruct

    columns = -(-(part + EXTRA) // 128) * 128
    sent = call(
        pack_kernel,
        shape((groups, rows, columns), bf16),
        [],
        [adjoint, labels[None, :], conductance[None, :]],
        own_copies=True,
    )
    got = lax.all_to_all(sent, ("line", "pair"), split_axis=0, concat_axis=0, tiled=True).reshape(cells, columns)

    collision, sent = lax.optimization_barrier((collision, sent))
    flipped, place = call(
        flip_kernel,
        [shape((width, depth + 2 * rows), bf16), shape((2 * rows, cells), bf16)],
        [],
        [collision.reshape(depth, width), adjoint, source],
    )

    start = got[:, :part].T
    full = lax.all_gather(start, "mode", axis=0, tiled=True)
    terms = call(
        first_kernel,
        handed_out(lines, (part, cells)),
        [],
        [flipped, place, full],
        [((groups, part, cells), f32)],
        flops=2 * width * depth * cells,
    )
    start, got, terms = lax.optimization_barrier((start, got, terms))
    transport, rate, sign = call(
        transport_kernel,
        [shape((part, cells), f32), shape((part, cells), f32), shape((part, 1), f32)],
        [],
        [start, jnp.sum(got[:, part:].astype(f32), axis=1)[None, :], speed[None, :], direction[None, :]],
    )
    state = reduce_over_cells(terms, lines) - transport

    full = lax.all_gather(state.astype(bf16), "mode", axis=0, tiled=True)
    terms = call(
        second_kernel,
        handed_out(lines, (rows, width)),
        [],
        [flipped, full, state, rate, sign],
        [((groups, part, cells), f32), ((groups, rows, width), f32)],
        flops=2 * width * depth * cells,
    )
    return reduce_over_cells(terms, lines) + relax_factor * source


def solution(mesh):
    modes, groups = mesh.shape["mode"], mesh.shape["cell"]
    mesh = Mesh(mesh.devices.reshape(modes, groups // 2, 2), ("mode", "line", "pair"))
    cell = ("line", "pair")
    in_specs = (
        P(cell, "mode"),
        P(cell, "mode"),
        P(None, cell, None, "mode"),
        P("mode"),
        P("mode"),
        P(cell),
        P(),
    )
    out_specs = P(cell, "mode")
    return jax.shard_map(shards, mesh=mesh, in_specs=in_specs, out_specs=out_specs, check_vma=False)
```

```python
import math

import jax
import jax.numpy as jnp
from jax import lax
from jax.experimental import pallas as pl
from jax.experimental.pallas import tpu as pltpu
from jax.sharding import Mesh, PartitionSpec as P

BRANCH = 48
ITERS = 2


relax_factor = 0.5
VMEM = pl.BlockSpec(memory_space=pltpu.VMEM)
SMEM = pl.BlockSpec(memory_space=pltpu.SMEM)
HBM = pl.BlockSpec(memory_space=pltpu.HBM)
bf16, f32 = jnp.bfloat16, jnp.float32
EXTRA = 16


def split(array):
    head = array.astype(bf16)
    return head, (array - head.astype(f32)).astype(bf16)


def padded_bytes(shape, dtype):
    size = jnp.dtype(dtype).itemsize
    if len(shape) < 2:
        return 4096
    sublanes = 8 * 4 // size
    rows, lanes = -(-shape[-2] // sublanes) * sublanes, -(-shape[-1] // 128) * 128
    return math.prod(shape[:-2]) * rows * lanes * size


def call(body, out, scalars, arrays, scratch=(), flops=0, own_copies=False):
    outs = jax.tree.leaves(out)
    bytes_ = sum(padded_bytes(a.shape, a.dtype) for a in (*arrays, *outs))
    held = sum(padded_bytes(shape, dtype) for shape, dtype in scratch)
    scratch = [pltpu.VMEM(shape, dtype) for shape, dtype in scratch]
    if own_copies:
        scratch += [pltpu.VMEM(a.shape, a.dtype) for a in arrays] + [pltpu.SemaphoreType.DMA((len(arrays),))]
    return pl.pallas_call(
        body,
        out_shape=out,
        in_specs=[SMEM] * len(scalars) + [HBM if own_copies else VMEM] * len(arrays),
        out_specs=jax.tree.map(lambda _: VMEM, out),
        scratch_shapes=scratch,
        compiler_params=pltpu.CompilerParams(
            vmem_limit_bytes=56 * 2**20 if own_copies else int(1.5 * (bytes_ + held)) + 4 * 2**20
        ),
        cost_estimate=pl.CostEstimate(flops=flops, bytes_accessed=bytes_, transcendentals=0),
    )(*scalars, *arrays)


def fetch(sources, targets, semaphores):
    copies = [
        pltpu.make_async_copy(source, target, semaphores.at[k])
        for k, (source, target) in enumerate(zip(sources, targets))
    ]
    for copy in copies:
        copy.start()
    for copy in copies:
        copy.wait()


def column_of(row, first, count, each=1):
    wide = row.shape[1]
    place = first + lax.broadcasted_iota(jnp.int32, (count, wide), 0)
    start = lax.broadcasted_iota(jnp.int32, (count, wide), 1) * each
    hit = jnp.logical_and(place >= start, place < start + each)
    return jnp.sum(jnp.where(hit, row, 0.0), axis=1, keepdims=True)


def upwind_change(state, sign):
    cells = state.shape[1]
    spot = lax.broadcasted_iota(jnp.int32, (1, cells), 1)
    after = jnp.where(spot == cells - 1, 0.0, pltpu.roll(state, cells - 1, 1))
    before = jnp.where(spot == 0, 0.0, pltpu.roll(state, 1, 1))
    return state - jnp.where(sign > 0, after, before)


def pack_kernel(adjoint_, labels_, conductance_, out, adjoint, labels, conductance, semaphores):
    fetch((adjoint_, labels_, conductance_), (adjoint, labels, conductance), semaphores)
    groups, rows, columns = out.shape
    part = adjoint.shape[1] // groups
    label = column_of(labels[...].astype(f32), 0, rows)
    kinds = lax.broadcasted_iota(jnp.int32, (rows, conductance.shape[1]), 1).astype(f32)
    kappa = jnp.sum(jnp.where(kinds == label, conductance[...], 0.0), axis=1, keepdims=True)
    first, _ = split(kappa)
    second, third = split(kappa - first.astype(f32))
    column = lax.broadcasted_iota(jnp.int32, (rows, columns - part), 1)
    scale = jnp.where(column == 0, first.astype(f32), 0.0) + jnp.where(column == 1, second.astype(f32), 0.0)
    scale = (scale + jnp.where(column == 2, third.astype(f32), 0.0)).astype(bf16)
    for group in range(groups):
        out[group, :, :part] = adjoint[:, group * part : (group + 1) * part].astype(bf16)
        out[group, :, part:] = scale


def index_of():
    line, pair = lax.axis_index("line"), lax.axis_index("pair")
    return line, pair, 2 * line + pair


def flip_kernel(collision, adjoint, source, out, place):
    base = split(adjoint[...] + relax_factor * source[...])
    out[...] = jnp.concatenate([collision[...] * bf16(-relax_factor), *base], axis=0).T
    rows, cells = adjoint.shape[0], place.shape[1]
    _, _, me = index_of()
    row = lax.broadcasted_iota(jnp.int32, (rows, cells), 0)
    column = lax.broadcasted_iota(jnp.int32, (rows, cells), 1)
    mine = (column == row + me * rows).astype(f32).astype(bf16)
    place[:rows, :] = mine
    place[rows:, :] = mine


def ways_of(lines):
    return [(0, 1), (1, 0), (1, 1)] if lines > 1 else [(0, 1)]


def fours(lines):
    return max(lines // 2, 1)


def hand_out(blocks, outs, lines):
    line, pair, _ = index_of()
    outs, count = iter(outs), fours(lines)
    for four in range(count):
        next(outs)[...] = blocks[2 * (line ^ (2 * four)) + pair]
    if count > 1:
        for bit, other in ways_of(lines)[:2]:
            out = next(outs)
            for four in range(1, count):
                out[four - 1] = blocks[2 * (line ^ (2 * four + bit)) + (pair ^ other)].astype(bf16)
    for four in range(1, count):
        next(outs)[...] = blocks[2 * (line ^ (2 * four + 1)) + (pair ^ 1)].astype(bf16)
    for bit, other in ways_of(lines):
        next(outs)[...] = blocks[2 * (line ^ bit) + (pair ^ other)].astype(bf16)


def handed_out(lines, block):
    count, sent = fours(lines), jax.ShapeDtypeStruct(block, bf16)
    kept = [jax.ShapeDtypeStruct(block, f32)] * count
    far = [jax.ShapeDtypeStruct((count - 1, *block), bf16)] * 2 if count > 1 else []
    return kept + far + [sent] * (count - 1) + [sent] * len(ways_of(lines))


def first_kernel(flipped, place, full, *refs):
    *outs, terms = refs
    lines = terms.shape[0] // 2
    depth = full.shape[0]
    result = jnp.dot(flipped[:, :depth], full[...], preferred_element_type=f32)
    result += jnp.dot(flipped[:, depth:], place[...], preferred_element_type=f32)
    terms[...] = result.reshape(terms.shape)
    hand_out(terms, outs, lines)


def transport_kernel(start, kappa, speed, direction, out, rate_out, sign_out):
    part, _ = out.shape
    first = index_of()[2] * part
    rate_out[...] = relax_factor * column_of(speed[...], first, part) * kappa[:1, :]
    sign_out[...] = 2.0 * column_of(direction[...].astype(f32), first, part, BRANCH) - 1.0
    out[...] = rate_out[...] * upwind_change(start[...].astype(f32), sign_out[...])


def second_kernel(flipped, full, state, rate, sign, *refs):
    *outs, terms, blocks = refs
    groups, part, cells = terms.shape
    lines = groups // 2
    depth = full.shape[0]
    _, _, me = index_of()
    terms[...] = jnp.dot(flipped[:, :depth], full[...], preferred_element_type=f32).reshape(terms.shape)
    terms[me] += state[...] - rate[...] * upwind_change(state[...], sign[...])
    blocks[...] = terms[...].reshape(groups * part, cells).T.reshape(blocks.shape)
    hand_out(blocks, outs, lines)


def swapped(block, lines, bits, other):
    pairs = [(2 * i + p, 2 * (i ^ bits) + (p ^ other)) for i in range(lines) for p in range(2)]
    return lax.ppermute(block, ("line", "pair"), pairs)


def reduce_over_cells(blocks, lines):
    count, ways, blocks = fours(lines), ways_of(lines), list(blocks)
    kept, blocks = blocks[:count], blocks[count:]
    near, blocks = blocks[-len(ways) :], blocks[: -len(ways)]
    terms = []
    if count > 1:
        arrived = [swapped(block, lines, *way) for block, way in zip(blocks[:2], ways)]
        for four in range(1, count):
            block = kept[four]
            for part in arrived:
                block = block + part[four - 1].astype(f32)
            block, near[:2] = lax.optimization_barrier((block.astype(bf16), near[:2]))
            terms.append(swapped(block, lines, 2 * four, 0))
        terms += [swapped(block, lines, 2 * four + 3, 1) for four, block in enumerate(blocks[2:])]
    for way, block in list(zip(ways, near))[::-1]:
        terms.append(swapped(block, lines, *way))
    result = kept[0]
    for term in terms:
        result = result + term.astype(f32)
    return result


def shards(adjoint, source, collision, speed, direction, labels, conductance):
    rows, width = adjoint.shape
    lines, pairs, modes = lax.axis_size("line"), lax.axis_size("pair"), lax.axis_size("mode")
    groups = lines * pairs
    part = width // groups
    cells = rows * groups
    depth = modes * part
    shape = jax.ShapeDtypeStruct

    columns = -(-(part + EXTRA) // 128) * 128
    sent = call(
        pack_kernel,
        shape((groups, rows, columns), bf16),
        [],
        [adjoint, labels[None, :], conductance[None, :]],
        own_copies=True,
    )
    got = lax.all_to_all(sent, ("line", "pair"), split_axis=0, concat_axis=0, tiled=True).reshape(cells, columns)

    collision, sent = lax.optimization_barrier((collision, sent))
    flipped, place = call(
        flip_kernel,
        [shape((width, depth + 2 * rows), bf16), shape((2 * rows, cells), bf16)],
        [],
        [collision.reshape(depth, width), adjoint, source],
    )

    start = got[:, :part].T
    full = lax.all_gather(start, "mode", axis=0, tiled=True)
    terms = call(
        first_kernel,
        handed_out(lines, (part, cells)),
        [],
        [flipped, place, full],
        [((groups, part, cells), f32)],
        flops=2 * width * depth * cells,
    )
    start, got, terms = lax.optimization_barrier((start, got, terms))
    transport, rate, sign = call(
        transport_kernel,
        [shape((part, cells), f32), shape((part, cells), f32), shape((part, 1), f32)],
        [],
        [start, jnp.sum(got[:, part:].astype(f32), axis=1)[None, :], speed[None, :], direction[None, :]],
    )
    state = reduce_over_cells(terms, lines) - transport

    full = lax.all_gather(state.astype(bf16), "mode", axis=0, tiled=True)
    terms = call(
        second_kernel,
        handed_out(lines, (rows, width)),
        [],
        [flipped, full, state, rate, sign],
        [((groups, part, cells), f32), ((groups, rows, width), f32)],
        flops=2 * width * depth * cells,
    )
    return reduce_over_cells(terms, lines) + relax_factor * source


def solution(mesh):
    modes, groups = mesh.shape["mode"], mesh.shape["cell"]
    mesh = Mesh(mesh.devices.reshape(modes, groups // 2, 2), ("mode", "line", "pair"))
    cell = ("line", "pair")
    in_specs = (
        P(cell, "mode"),
        P(cell, "mode"),
        P(None, cell, None, "mode"),
        P("mode"),
        P("mode"),
        P(cell),
        P(),
    )
    out_specs = P(cell, "mode")
    return jax.shard_map(shards, mesh=mesh, in_specs=in_specs, out_specs=out_specs, check_vma=False)
```

```python
import math

import jax
import jax.numpy as jnp
from jax import lax
from jax.experimental import pallas as pl
from jax.experimental.pallas import tpu as pltpu
from jax.sharding import Mesh, PartitionSpec as P

BRANCH = 48
ITERS = 2


relax_factor = 0.5
VMEM = pl.BlockSpec(memory_space=pltpu.VMEM)
SMEM = pl.BlockSpec(memory_space=pltpu.SMEM)
HBM = pl.BlockSpec(memory_space=pltpu.HBM)
bf16, f32 = jnp.bfloat16, jnp.float32
EXTRA = 16


def split(array):
    head = array.astype(bf16)
    return head, (array - head.astype(f32)).astype(bf16)


def padded_bytes(shape, dtype):
    size = jnp.dtype(dtype).itemsize
    if len(shape) < 2:
        return 4096
    sublanes = 8 * 4 // size
    rows, lanes = -(-shape[-2] // sublanes) * sublanes, -(-shape[-1] // 128) * 128
    return math.prod(shape[:-2]) * rows * lanes * size


def call(body, out, scalars, arrays, scratch=(), flops=0, own_copies=False):
    outs = jax.tree.leaves(out)
    bytes_ = sum(padded_bytes(a.shape, a.dtype) for a in (*arrays, *outs))
    held = sum(padded_bytes(shape, dtype) for shape, dtype in scratch)
    scratch = [pltpu.VMEM(shape, dtype) for shape, dtype in scratch]
    if own_copies:
        scratch += [pltpu.VMEM(a.shape, a.dtype) for a in arrays] + [pltpu.SemaphoreType.DMA((len(arrays),))]
    return pl.pallas_call(
        body,
        out_shape=out,
        in_specs=[SMEM] * len(scalars) + [HBM if own_copies else VMEM] * len(arrays),
        out_specs=jax.tree.map(lambda _: VMEM, out),
        scratch_shapes=scratch,
        compiler_params=pltpu.CompilerParams(
            vmem_limit_bytes=56 * 2**20 if own_copies else int(1.5 * (bytes_ + held)) + 4 * 2**20
        ),
        cost_estimate=pl.CostEstimate(flops=flops, bytes_accessed=bytes_, transcendentals=0),
    )(*scalars, *arrays)


def fetch(sources, targets, semaphores):
    copies = [
        pltpu.make_async_copy(source, target, semaphores.at[k])
        for k, (source, target) in enumerate(zip(sources, targets))
    ]
    for copy in copies:
        copy.start()
    for copy in copies:
        copy.wait()


def column_of(row, first, count, each=1):
    wide = row.shape[1]
    place = first + lax.broadcasted_iota(jnp.int32, (count, wide), 0)
    start = lax.broadcasted_iota(jnp.int32, (count, wide), 1) * each
    hit = jnp.logical_and(place >= start, place < start + each)
    return jnp.sum(jnp.where(hit, row, 0.0), axis=1, keepdims=True)


def upwind_change(state, sign):
    cells = state.shape[1]
    spot = lax.broadcasted_iota(jnp.int32, (1, cells), 1)
    after = jnp.where(spot == cells - 1, 0.0, pltpu.roll(state, cells - 1, 1))
    before = jnp.where(spot == 0, 0.0, pltpu.roll(state, 1, 1))
    return state - jnp.where(sign > 0, after, before)


def pack_kernel(adjoint_, labels_, conductance_, out, adjoint, labels, conductance, semaphores):
    fetch((adjoint_, labels_, conductance_), (adjoint, labels, conductance), semaphores)
    groups, rows, columns = out.shape
    part = adjoint.shape[1] // groups
    label = column_of(labels[...].astype(f32), 0, rows)
    kinds = lax.broadcasted_iota(jnp.int32, (rows, conductance.shape[1]), 1).astype(f32)
    kappa = jnp.sum(jnp.where(kinds == label, conductance[...], 0.0), axis=1, keepdims=True)
    first, _ = split(kappa)
    second, third = split(kappa - first.astype(f32))
    column = lax.broadcasted_iota(jnp.int32, (rows, columns - part), 1)
    scale = jnp.where(column == 0, first.astype(f32), 0.0) + jnp.where(column == 1, second.astype(f32), 0.0)
    scale = (scale + jnp.where(column == 2, third.astype(f32), 0.0)).astype(bf16)
    for group in range(groups):
        out[group, :, :part] = adjoint[:, group * part : (group + 1) * part].astype(bf16)
        out[group, :, part:] = scale


def index_of():
    line, pair = lax.axis_index("line"), lax.axis_index("pair")
    return line, pair, 2 * line + pair


def flip_kernel(collision, adjoint, source, out, place):
    base = split(adjoint[...] + relax_factor * source[...])
    out[...] = jnp.concatenate([collision[...] * bf16(-relax_factor), *base], axis=0).T
    rows, cells = adjoint.shape[0], place.shape[1]
    _, _, me = index_of()
    row = lax.broadcasted_iota(jnp.int32, (rows, cells), 0)
    column = lax.broadcasted_iota(jnp.int32, (rows, cells), 1)
    mine = (column == row + me * rows).astype(f32).astype(bf16)
    place[:rows, :] = mine
    place[rows:, :] = mine


def fours(lines):
    return max(lines // 2, 1)


def blocks_of(lines):
    others = range(2, lines, 2)
    kept = [(bits, 0) for bits in (0, *others)]
    over_pair = [(bits, 1) for bits in others]
    if lines > 1:
        kept, over_pair = kept + [(1, 0)], over_pair + [(1, 1)]
    return kept, over_pair, [(bits + 1, 0) for bits in others], [(bits + 1, 1) for bits in others], (0, 1)


def hand_out(blocks, outs, lines):
    line, pair, _ = index_of()

    def found(bits, other):
        return blocks[2 * (line ^ bits) + (pair ^ other)]

    outs = iter(outs)
    kept, over_pair, over_line, diagonal, near = blocks_of(lines)
    for way in kept:
        next(outs)[...] = found(*way)
    for group in (over_pair, over_line):
        if group:
            out = next(outs)
            for spot, way in enumerate(group):
                out[spot] = found(*way).astype(bf16)
    for way in (*diagonal, near):
        next(outs)[...] = found(*way).astype(bf16)


def handed_out(lines, block):
    kept, over_pair, over_line, diagonal, _ = blocks_of(lines)
    stacked = [jax.ShapeDtypeStruct((len(group), *block), bf16) for group in (over_pair, over_line) if group]
    single = [jax.ShapeDtypeStruct(block, bf16)] * (len(diagonal) + 1)
    return [jax.ShapeDtypeStruct(block, f32)] * len(kept) + stacked + single


def first_kernel(flipped, place, full, *refs):
    *outs, terms = refs
    lines = terms.shape[0] // 2
    depth = full.shape[0]
    result = jnp.dot(flipped[:, :depth], full[...], preferred_element_type=f32)
    result += jnp.dot(flipped[:, depth:], place[...], preferred_element_type=f32)
    terms[...] = result.reshape(terms.shape)
    hand_out(terms, outs, lines)


def transport_kernel(start, kappa, speed, direction, out, rate_out, sign_out):
    part, _ = out.shape
    first = index_of()[2] * part
    rate_out[...] = relax_factor * column_of(speed[...], first, part) * kappa[:1, :]
    sign_out[...] = 2.0 * column_of(direction[...].astype(f32), first, part, BRANCH) - 1.0
    out[...] = rate_out[...] * upwind_change(start[...].astype(f32), sign_out[...])


def second_kernel(flipped, full, state, rate, sign, *refs):
    *outs, terms, blocks = refs
    groups, part, cells = terms.shape
    lines = groups // 2
    depth = full.shape[0]
    _, _, me = index_of()
    terms[...] = jnp.dot(flipped[:, :depth], full[...], preferred_element_type=f32).reshape(terms.shape)
    terms[me] += state[...] - rate[...] * upwind_change(state[...], sign[...])
    blocks[...] = terms[...].reshape(groups * part, cells).T.reshape(blocks.shape)
    hand_out(blocks, outs, lines)


def swapped(block, lines, bits, other):
    pairs = [(2 * i + p, 2 * (i ^ bits) + (p ^ other)) for i in range(lines) for p in range(2)]
    return lax.ppermute(block, ("line", "pair"), pairs)


def reduce_over_cells(blocks, lines):
    kept, over_pair, over_line, diagonal, near = blocks_of(lines)
    outs = iter(blocks)
    sums = [next(outs) for _ in kept]
    across = swapped(next(outs), lines, 0, 1) if over_pair else []
    along = swapped(next(outs), lines, 1, 0) if over_line else []
    for spot in range(len(over_pair)):
        block = sums[spot + 1] + across[spot].astype(f32)
        if spot < len(over_line):
            block = block + along[spot].astype(f32)
        sums[spot + 1] = block.astype(bf16)
    if over_pair:
        sums[1:] = lax.optimization_barrier(sums[1:])
    terms = [swapped(block, lines, bits, 0) for block, (bits, _) in zip(sums[1:], kept[1:])]
    terms[len(over_line) : len(over_line)] = [swapped(next(outs), lines, *way) for way in (*diagonal, near)]
    result = sums[0]
    for term in terms:
        result = result + term.astype(f32)
    return result


def shards(adjoint, source, collision, speed, direction, labels, conductance):
    rows, width = adjoint.shape
    lines, pairs, modes = lax.axis_size("line"), lax.axis_size("pair"), lax.axis_size("mode")
    groups = lines * pairs
    part = width // groups
    cells = rows * groups
    depth = modes * part
    shape = jax.ShapeDtypeStruct

    columns = -(-(part + EXTRA) // 128) * 128
    sent = call(
        pack_kernel,
        shape((groups, rows, columns), bf16),
        [],
        [adjoint, labels[None, :], conductance[None, :]],
        own_copies=True,
    )
    got = lax.all_to_all(sent, ("line", "pair"), split_axis=0, concat_axis=0, tiled=True).reshape(cells, columns)

    collision, sent = lax.optimization_barrier((collision, sent))
    flipped, place = call(
        flip_kernel,
        [shape((width, depth + 2 * rows), bf16), shape((2 * rows, cells), bf16)],
        [],
        [collision.reshape(depth, width), adjoint, source],
    )

    start = got[:, :part].T
    full = lax.all_gather(start, "mode", axis=0, tiled=True)
    terms = call(
        first_kernel,
        handed_out(lines, (part, cells)),
        [],
        [flipped, place, full],
        [((groups, part, cells), f32)],
        flops=2 * width * depth * cells,
    )
    start, got, terms = lax.optimization_barrier((start, got, terms))
    transport, rate, sign = call(
        transport_kernel,
        [shape((part, cells), f32), shape((part, cells), f32), shape((part, 1), f32)],
        [],
        [start, jnp.sum(got[:, part:].astype(f32), axis=1)[None, :], speed[None, :], direction[None, :]],
    )
    state = reduce_over_cells(terms, lines) - transport

    full = lax.all_gather(state.astype(bf16), "mode", axis=0, tiled=True)
    terms = call(
        second_kernel,
        handed_out(lines, (rows, width)),
        [],
        [flipped, full, state, rate, sign],
        [((groups, part, cells), f32), ((groups, rows, width), f32)],
        flops=2 * width * depth * cells,
    )
    return reduce_over_cells(terms, lines) + relax_factor * source


def solution(mesh):
    modes, groups = mesh.shape["mode"], mesh.shape["cell"]
    mesh = Mesh(mesh.devices.reshape(modes, groups // 2, 2), ("mode", "line", "pair"))
    cell = ("line", "pair")
    in_specs = (
        P(cell, "mode"),
        P(cell, "mode"),
        P(None, cell, None, "mode"),
        P("mode"),
        P("mode"),
        P(cell),
        P(),
    )
    out_specs = P(cell, "mode")
    return jax.shard_map(shards, mesh=mesh, in_specs=in_specs, out_specs=out_specs, check_vma=False)
```

```python
import math

import jax
import jax.numpy as jnp
from jax import lax
from jax.experimental import pallas as pl
from jax.experimental.pallas import tpu as pltpu
from jax.sharding import Mesh, PartitionSpec as P

BRANCH = 48
ITERS = 2


relax_factor = 0.5
VMEM = pl.BlockSpec(memory_space=pltpu.VMEM)
SMEM = pl.BlockSpec(memory_space=pltpu.SMEM)
HBM = pl.BlockSpec(memory_space=pltpu.HBM)
bf16, f32 = jnp.bfloat16, jnp.float32
EXTRA = 16


def split(array):
    head = array.astype(bf16)
    return head, (array - head.astype(f32)).astype(bf16)


def padded_bytes(shape, dtype):
    size = jnp.dtype(dtype).itemsize
    if len(shape) < 2:
        return 4096
    sublanes = 8 * 4 // size
    rows, lanes = -(-shape[-2] // sublanes) * sublanes, -(-shape[-1] // 128) * 128
    return math.prod(shape[:-2]) * rows * lanes * size


def call(body, out, scalars, arrays, scratch=(), flops=0, own_copies=False):
    outs = jax.tree.leaves(out)
    bytes_ = sum(padded_bytes(a.shape, a.dtype) for a in (*arrays, *outs))
    held = sum(padded_bytes(shape, dtype) for shape, dtype in scratch)
    scratch = [pltpu.VMEM(shape, dtype) for shape, dtype in scratch]
    if own_copies:
        scratch += [pltpu.VMEM(a.shape, a.dtype) for a in arrays] + [pltpu.SemaphoreType.DMA((len(arrays),))]
    return pl.pallas_call(
        body,
        out_shape=out,
        in_specs=[SMEM] * len(scalars) + [HBM if own_copies else VMEM] * len(arrays),
        out_specs=jax.tree.map(lambda _: VMEM, out),
        scratch_shapes=scratch,
        compiler_params=pltpu.CompilerParams(
            vmem_limit_bytes=56 * 2**20 if own_copies else int(1.5 * (bytes_ + held)) + 4 * 2**20
        ),
        cost_estimate=pl.CostEstimate(flops=flops, bytes_accessed=bytes_, transcendentals=0),
    )(*scalars, *arrays)


def fetch(sources, targets, semaphores):
    copies = [
        pltpu.make_async_copy(source, target, semaphores.at[k])
        for k, (source, target) in enumerate(zip(sources, targets))
    ]
    for copy in copies:
        copy.start()
    return copies


def column_of(row, first, count, each=1):
    wide = row.shape[1]
    place = first + lax.broadcasted_iota(jnp.int32, (count, wide), 0)
    start = lax.broadcasted_iota(jnp.int32, (count, wide), 1) * each
    hit = jnp.logical_and(place >= start, place < start + each)
    return jnp.sum(jnp.where(hit, row, 0.0), axis=1, keepdims=True)


def upwind_change(state, sign):
    cells = state.shape[1]
    spot = lax.broadcasted_iota(jnp.int32, (1, cells), 1)
    after = jnp.where(spot == cells - 1, 0.0, pltpu.roll(state, cells - 1, 1))
    before = jnp.where(spot == 0, 0.0, pltpu.roll(state, 1, 1))
    return state - jnp.where(sign > 0, after, before)


def pack_kernel(adjoint_, labels_, conductance_, out, adjoint, labels, conductance, semaphores):
    copies = fetch((adjoint_, labels_, conductance_), (adjoint, labels, conductance), semaphores)
    for copy in copies[1:]:
        copy.wait()
    groups, rows, columns = out.shape
    part = adjoint.shape[1] // groups
    label = column_of(labels[...].astype(f32), 0, rows)
    kinds = lax.broadcasted_iota(jnp.int32, (rows, conductance.shape[1]), 1).astype(f32)
    kappa = jnp.sum(jnp.where(kinds == label, conductance[...], 0.0), axis=1, keepdims=True)
    first, _ = split(kappa)
    second, third = split(kappa - first.astype(f32))
    column = lax.broadcasted_iota(jnp.int32, (rows, columns - part), 1)
    scale = jnp.where(column == 0, first.astype(f32), 0.0) + jnp.where(column == 1, second.astype(f32), 0.0)
    scale = (scale + jnp.where(column == 2, third.astype(f32), 0.0)).astype(bf16)
    copies[0].wait()
    for group in range(groups):
        out[group, :, :part] = adjoint[:, group * part : (group + 1) * part].astype(bf16)
        out[group, :, part:] = scale


def index_of():
    line, pair = lax.axis_index("line"), lax.axis_index("pair")
    return line, pair, 2 * line + pair


def flip_kernel(collision, adjoint, source, out, place):
    base = split(adjoint[...] + relax_factor * source[...])
    out[...] = jnp.concatenate([collision[...] * bf16(-relax_factor), *base], axis=0).T
    rows, cells = adjoint.shape[0], place.shape[1]
    _, _, me = index_of()
    row = lax.broadcasted_iota(jnp.int32, (rows, cells), 0)
    column = lax.broadcasted_iota(jnp.int32, (rows, cells), 1)
    mine = (column == row + me * rows).astype(f32).astype(bf16)
    place[:rows, :] = mine
    place[rows:, :] = mine


def ways_of(lines):
    return [(0, 1), (1, 0), (1, 1)] if lines > 1 else [(0, 1)]


def fours(lines):
    return max(lines // 2, 1)


def hand_out(blocks, outs, lines):
    line, pair, _ = index_of()
    outs, count = iter(outs), fours(lines)
    for four in range(count):
        next(outs)[...] = blocks[2 * (line ^ (2 * four)) + pair]
    if count > 1:
        for bit, other in ways_of(lines)[:2]:
            out = next(outs)
            for four in range(1, count):
                out[four - 1] = blocks[2 * (line ^ (2 * four + bit)) + (pair ^ other)].astype(bf16)
    for four in range(1, count):
        next(outs)[...] = blocks[2 * (line ^ (2 * four + 1)) + (pair ^ 1)].astype(bf16)
    for bit, other in ways_of(lines):
        next(outs)[...] = blocks[2 * (line ^ bit) + (pair ^ other)].astype(bf16)


def handed_out(lines, block):
    count, sent = fours(lines), jax.ShapeDtypeStruct(block, bf16)
    kept = [jax.ShapeDtypeStruct(block, f32)] * count
    far = [jax.ShapeDtypeStruct((count - 1, *block), bf16)] * 2 if count > 1 else []
    return kept + far + [sent] * (count - 1) + [sent] * len(ways_of(lines))


def first_kernel(flipped, place, full, *refs):
    *outs, terms = refs
    lines = terms.shape[0] // 2
    depth = full.shape[0]
    result = jnp.dot(flipped[:, :depth], full[...], preferred_element_type=f32)
    result += jnp.dot(flipped[:, depth:], place[...], preferred_element_type=f32)
    terms[...] = result.reshape(terms.shape)
    hand_out(terms, outs, lines)


def transport_kernel(start, kappa, speed, direction, out, rate_out, sign_out):
    part, _ = out.shape
    first = index_of()[2] * part
    rate_out[...] = relax_factor * column_of(speed[...], first, part) * kappa[:1, :]
    sign_out[...] = 2.0 * column_of(direction[...].astype(f32), first, part, BRANCH) - 1.0
    out[...] = rate_out[...] * upwind_change(start[...].astype(f32), sign_out[...])


def second_kernel(flipped, full, state, rate, sign, *refs):
    *outs, terms, blocks = refs
    groups, part, cells = terms.shape
    lines = groups // 2
    depth = full.shape[0]
    _, _, me = index_of()
    terms[...] = jnp.dot(flipped[:, :depth], full[...], preferred_element_type=f32).reshape(terms.shape)
    terms[me] += state[...] - rate[...] * upwind_change(state[...], sign[...])
    blocks[...] = terms[...].reshape(groups * part, cells).T.reshape(blocks.shape)
    hand_out(blocks, outs, lines)


def swapped(block, lines, bits, other):
    pairs = [(2 * i + p, 2 * (i ^ bits) + (p ^ other)) for i in range(lines) for p in range(2)]
    return lax.ppermute(block, ("line", "pair"), pairs)


def reduce_over_cells(blocks, lines):
    count, ways, blocks = fours(lines), ways_of(lines), list(blocks)
    kept, blocks = blocks[:count], blocks[count:]
    near, blocks = blocks[-len(ways) :], blocks[: -len(ways)]
    terms = []
    if count > 1:
        arrived = [swapped(block, lines, *way) for block, way in zip(blocks[:2], ways)]
        for four in range(1, count):
            block = kept[four]
            for part in arrived:
                block = block + part[four - 1].astype(f32)
            block, near = lax.optimization_barrier((block.astype(bf16), near))
            terms.append(swapped(block, lines, 2 * four, 0))
        terms += [swapped(block, lines, 2 * four + 3, 1) for four, block in enumerate(blocks[2:])]
    for way, block in list(zip(ways, near))[::-1]:
        terms.append(swapped(block, lines, *way))
    result = kept[0]
    for term in terms:
        result = result + term.astype(f32)
    return result


def shards(adjoint, source, collision, speed, direction, labels, conductance):
    rows, width = adjoint.shape
    lines, pairs, modes = lax.axis_size("line"), lax.axis_size("pair"), lax.axis_size("mode")
    groups = lines * pairs
    part = width // groups
    cells = rows * groups
    depth = modes * part
    shape = jax.ShapeDtypeStruct

    columns = -(-(part + EXTRA) // 128) * 128
    sent = call(
        pack_kernel,
        shape((groups, rows, columns), bf16),
        [],
        [adjoint, labels[None, :], conductance[None, :]],
        own_copies=True,
    )
    got = lax.all_to_all(sent, ("line", "pair"), split_axis=0, concat_axis=0, tiled=True).reshape(cells, columns)

    collision, sent = lax.optimization_barrier((collision, sent))
    flipped, place = call(
        flip_kernel,
        [shape((width, depth + 2 * rows), bf16), shape((2 * rows, cells), bf16)],
        [],
        [collision.reshape(depth, width), adjoint, source],
    )

    start = got[:, :part].T
    full = lax.all_gather(start, "mode", axis=0, tiled=True)
    terms = call(
        first_kernel,
        handed_out(lines, (part, cells)),
        [],
        [flipped, place, full],
        [((groups, part, cells), f32)],
        flops=2 * width * depth * cells,
    )
    start, got, terms = lax.optimization_barrier((start, got, terms))
    transport, rate, sign = call(
        transport_kernel,
        [shape((part, cells), f32), shape((part, cells), f32), shape((part, 1), f32)],
        [],
        [start, jnp.sum(got[:, part:].astype(f32), axis=1)[None, :], speed[None, :], direction[None, :]],
    )
    state = reduce_over_cells(terms, lines) - transport

    full = lax.all_gather(state.astype(bf16), "mode", axis=0, tiled=True)
    terms = call(
        second_kernel,
        handed_out(lines, (rows, width)),
        [],
        [flipped, full, state, rate, sign],
        [((groups, part, cells), f32), ((groups, rows, width), f32)],
        flops=2 * width * depth * cells,
    )
    return reduce_over_cells(terms, lines) + relax_factor * source


def solution(mesh):
    modes, groups = mesh.shape["mode"], mesh.shape["cell"]
    mesh = Mesh(mesh.devices.reshape(modes, groups // 2, 2), ("mode", "line", "pair"))
    cell = ("line", "pair")
    in_specs = (
        P(cell, "mode"),
        P(cell, "mode"),
        P(None, cell, None, "mode"),
        P("mode"),
        P("mode"),
        P(cell),
        P(),
    )
    out_specs = P(cell, "mode")
    return jax.shard_map(shards, mesh=mesh, in_specs=in_specs, out_specs=out_specs, check_vma=False)
```

```python
import math

import jax
import jax.numpy as jnp
from jax import lax
from jax.experimental import pallas as pl
from jax.experimental.pallas import tpu as pltpu
from jax.sharding import Mesh, PartitionSpec as P

BRANCH = 48
ITERS = 2


relax_factor = 0.5
VMEM = pl.BlockSpec(memory_space=pltpu.VMEM)
SMEM = pl.BlockSpec(memory_space=pltpu.SMEM)
HBM = pl.BlockSpec(memory_space=pltpu.HBM)
bf16, f32 = jnp.bfloat16, jnp.float32
EXTRA = 16


def split(array):
    head = array.astype(bf16)
    return head, (array - head.astype(f32)).astype(bf16)


def padded_bytes(shape, dtype):
    size = jnp.dtype(dtype).itemsize
    if len(shape) < 2:
        return 4096
    sublanes = 8 * 4 // size
    rows, lanes = -(-shape[-2] // sublanes) * sublanes, -(-shape[-1] // 128) * 128
    return math.prod(shape[:-2]) * rows * lanes * size


def call(body, out, scalars, arrays, scratch=(), flops=0, own_copies=False):
    outs = jax.tree.leaves(out)
    bytes_ = sum(padded_bytes(a.shape, a.dtype) for a in (*arrays, *outs))
    held = sum(padded_bytes(shape, dtype) for shape, dtype in scratch)
    scratch = [pltpu.VMEM(shape, dtype) for shape, dtype in scratch]
    if own_copies:
        scratch += [pltpu.VMEM(a.shape, a.dtype) for a in arrays] + [pltpu.SemaphoreType.DMA((len(arrays),))]
    return pl.pallas_call(
        body,
        out_shape=out,
        in_specs=[SMEM] * len(scalars) + [HBM if own_copies else VMEM] * len(arrays),
        out_specs=jax.tree.map(lambda _: VMEM, out),
        scratch_shapes=scratch,
        compiler_params=pltpu.CompilerParams(
            vmem_limit_bytes=56 * 2**20 if own_copies else int(1.5 * (bytes_ + held)) + 4 * 2**20
        ),
        cost_estimate=pl.CostEstimate(flops=flops, bytes_accessed=bytes_, transcendentals=0),
    )(*scalars, *arrays)


def fetch(sources, targets, semaphores):
    copies = [
        pltpu.make_async_copy(source, target, semaphores.at[k])
        for k, (source, target) in enumerate(zip(sources, targets))
    ]
    for copy in copies:
        copy.start()
    return copies


def column_of(row, first, count, each=1):
    wide = row.shape[1]
    place = first + lax.broadcasted_iota(jnp.int32, (count, wide), 0)
    start = lax.broadcasted_iota(jnp.int32, (count, wide), 1) * each
    hit = jnp.logical_and(place >= start, place < start + each)
    return jnp.sum(jnp.where(hit, row, 0.0), axis=1, keepdims=True)


def upwind_change(state, sign):
    cells = state.shape[1]
    spot = lax.broadcasted_iota(jnp.int32, (1, cells), 1)
    after = jnp.where(spot == cells - 1, 0.0, pltpu.roll(state, cells - 1, 1))
    before = jnp.where(spot == 0, 0.0, pltpu.roll(state, 1, 1))
    return state - jnp.where(sign > 0, after, before)


def pack_kernel(adjoint_, labels_, conductance_, out, adjoint, labels, conductance, semaphores):
    copies = fetch((adjoint_, labels_, conductance_), (adjoint, labels, conductance), semaphores)
    for copy in copies[1:]:
        copy.wait()
    groups, rows, columns = out.shape
    part = adjoint.shape[1] // groups
    label = column_of(labels[...].astype(f32), 0, rows)
    kinds = lax.broadcasted_iota(jnp.int32, (rows, conductance.shape[1]), 1).astype(f32)
    kappa = jnp.sum(jnp.where(kinds == label, conductance[...], 0.0), axis=1, keepdims=True)
    first, _ = split(kappa)
    second, third = split(kappa - first.astype(f32))
    column = lax.broadcasted_iota(jnp.int32, (rows, columns - part), 1)
    scale = jnp.where(column == 0, first.astype(f32), 0.0) + jnp.where(column == 1, second.astype(f32), 0.0)
    scale = (scale + jnp.where(column == 2, third.astype(f32), 0.0)).astype(bf16)
    copies[0].wait()
    for group in range(groups):
        out[group, :, :part] = adjoint[:, group * part : (group + 1) * part].astype(bf16)
        out[group, :, part:] = scale


def index_of():
    line, pair = lax.axis_index("line"), lax.axis_index("pair")
    return line, pair, 2 * line + pair


def flip_kernel(collision, adjoint, source, out, place):
    base = split(adjoint[...] + relax_factor * source[...])
    out[...] = jnp.concatenate([collision[...] * bf16(-relax_factor), *base], axis=0).T
    rows, cells = adjoint.shape[0], place.shape[1]
    _, _, me = index_of()
    row = lax.broadcasted_iota(jnp.int32, (rows, cells), 0)
    column = lax.broadcasted_iota(jnp.int32, (rows, cells), 1)
    mine = (column == row + me * rows).astype(f32).astype(bf16)
    place[:rows, :] = mine
    place[rows:, :] = mine


def ways_of(lines):
    return [(0, 1), (1, 0), (1, 1)] if lines > 1 else [(0, 1)]


def fours(lines):
    return max(lines // 2, 1)


def hand_out(blocks, outs, lines):
    line, pair, _ = index_of()
    outs, count = iter(outs), fours(lines)
    for four in range(count):
        next(outs)[...] = blocks[2 * (line ^ (2 * four)) + pair]
    if count > 1:
        for bit, other in ways_of(lines)[:2]:
            out = next(outs)
            for four in range(1, count):
                out[four - 1] = blocks[2 * (line ^ (2 * four + bit)) + (pair ^ other)].astype(bf16)
    for four in range(1, count):
        next(outs)[...] = blocks[2 * (line ^ (2 * four + 1)) + (pair ^ 1)].astype(bf16)
    for bit, other in ways_of(lines):
        next(outs)[...] = blocks[2 * (line ^ bit) + (pair ^ other)].astype(bf16)


def handed_out(lines, block):
    count, sent = fours(lines), jax.ShapeDtypeStruct(block, bf16)
    kept = [jax.ShapeDtypeStruct(block, f32)] * count
    far = [jax.ShapeDtypeStruct((count - 1, *block), bf16)] * 2 if count > 1 else []
    return kept + far + [sent] * (count - 1) + [sent] * len(ways_of(lines))


def first_kernel(flipped, place, full, *refs):
    *outs, terms = refs
    lines = terms.shape[0] // 2
    depth = full.shape[0]
    result = jnp.dot(flipped[:, :depth], full[...], preferred_element_type=f32)
    result += jnp.dot(flipped[:, depth:], place[...], preferred_element_type=f32)
    terms[...] = result.reshape(terms.shape)
    hand_out(terms, outs, lines)


def transport_kernel(start, kappa, speed, direction, out, rate_out, sign_out):
    part, _ = out.shape
    first = index_of()[2] * part
    rate_out[...] = relax_factor * column_of(speed[...], first, part) * kappa[:1, :]
    sign_out[...] = 2.0 * column_of(direction[...].astype(f32), first, part, BRANCH) - 1.0
    out[...] = rate_out[...] * upwind_change(start[...].astype(f32), sign_out[...])


def second_kernel(flipped, full, state, rate, sign, *refs):
    *outs, terms, blocks = refs
    groups, part, cells = terms.shape
    lines = groups // 2
    depth = full.shape[0]
    _, _, me = index_of()
    terms[...] = jnp.dot(flipped[:, :depth], full[...], preferred_element_type=f32).reshape(terms.shape)
    terms[me] += state[...] - rate[...] * upwind_change(state[...], sign[...])
    blocks[...] = terms[...].reshape(groups * part, cells).T.reshape(blocks.shape)
    hand_out(blocks, outs, lines)


def swapped(block, lines, bits, other):
    pairs = [(2 * i + p, 2 * (i ^ bits) + (p ^ other)) for i in range(lines) for p in range(2)]
    return lax.ppermute(block, ("line", "pair"), pairs)


def reduce_over_cells(blocks, lines):
    count, ways, blocks = fours(lines), ways_of(lines), list(blocks)
    kept, blocks = blocks[:count], blocks[count:]
    near, blocks = blocks[-len(ways) :], blocks[: -len(ways)]
    terms = []
    if count > 1:
        arrived = [swapped(block, lines, *way) for block, way in zip(blocks[:2], ways)]
        for four in range(1, count):
            block = kept[four]
            for part in arrived:
                block = block + part[four - 1].astype(f32)
            block, near[0] = lax.optimization_barrier((block.astype(bf16), near[0]))
            terms.append(swapped(block, lines, 2 * four, 0))
        terms += [swapped(block, lines, 2 * four + 3, 1) for four, block in enumerate(blocks[2:])]
    for way, block in list(zip(ways, near))[::-1]:
        terms.append(swapped(block, lines, *way))
    result = kept[0]
    for term in terms:
        result = result + term.astype(f32)
    return result


def shards(adjoint, source, collision, speed, direction, labels, conductance):
    rows, width = adjoint.shape
    lines, pairs, modes = lax.axis_size("line"), lax.axis_size("pair"), lax.axis_size("mode")
    groups = lines * pairs
    part = width // groups
    cells = rows * groups
    depth = modes * part
    shape = jax.ShapeDtypeStruct

    columns = -(-(part + EXTRA) // 128) * 128
    sent = call(
        pack_kernel,
        shape((groups, rows, columns), bf16),
        [],
        [adjoint, labels[None, :], conductance[None, :]],
        own_copies=True,
    )
    got = lax.all_to_all(sent, ("line", "pair"), split_axis=0, concat_axis=0, tiled=True).reshape(cells, columns)

    collision, sent = lax.optimization_barrier((collision, sent))
    flipped, place = call(
        flip_kernel,
        [shape((width, depth + 2 * rows), bf16), shape((2 * rows, cells), bf16)],
        [],
        [collision.reshape(depth, width), adjoint, source],
    )

    start = got[:, :part].T
    full = lax.all_gather(start, "mode", axis=0, tiled=True)
    terms = call(
        first_kernel,
        handed_out(lines, (part, cells)),
        [],
        [flipped, place, full],
        [((groups, part, cells), f32)],
        flops=2 * width * depth * cells,
    )
    start, got, terms = lax.optimization_barrier((start, got, terms))
    transport, rate, sign = call(
        transport_kernel,
        [shape((part, cells), f32), shape((part, cells), f32), shape((part, 1), f32)],
        [],
        [start, jnp.sum(got[:, part:].astype(f32), axis=1)[None, :], speed[None, :], direction[None, :]],
    )
    state = reduce_over_cells(terms, lines) - transport

    full = lax.all_gather(state.astype(bf16), "mode", axis=0, tiled=True)
    terms = call(
        second_kernel,
        handed_out(lines, (rows, width)),
        [],
        [flipped, full, state, rate, sign],
        [((groups, part, cells), f32), ((groups, rows, width), f32)],
        flops=2 * width * depth * cells,
    )
    return reduce_over_cells(terms, lines) + relax_factor * source


def solution(mesh):
    modes, groups = mesh.shape["mode"], mesh.shape["cell"]
    mesh = Mesh(mesh.devices.reshape(modes, groups // 2, 2), ("mode", "line", "pair"))
    cell = ("line", "pair")
    in_specs = (
        P(cell, "mode"),
        P(cell, "mode"),
        P(None, cell, None, "mode"),
        P("mode"),
        P("mode"),
        P(cell),
        P(),
    )
    out_specs = P(cell, "mode")
    return jax.shard_map(shards, mesh=mesh, in_specs=in_specs, out_specs=out_specs, check_vma=False)
```

```python
import math

import jax
import jax.numpy as jnp
from jax import lax
from jax.experimental import pallas as pl
from jax.experimental.pallas import tpu as pltpu
from jax.sharding import Mesh, PartitionSpec as P

BRANCH = 48
ITERS = 2


relax_factor = 0.5
VMEM = pl.BlockSpec(memory_space=pltpu.VMEM)
SMEM = pl.BlockSpec(memory_space=pltpu.SMEM)
HBM = pl.BlockSpec(memory_space=pltpu.HBM)
bf16, f32 = jnp.bfloat16, jnp.float32
EXTRA = 16


def split(array):
    head = array.astype(bf16)
    return head, (array - head.astype(f32)).astype(bf16)


def padded_bytes(shape, dtype):
    size = jnp.dtype(dtype).itemsize
    if len(shape) < 2:
        return 4096
    sublanes = 8 * 4 // size
    rows, lanes = -(-shape[-2] // sublanes) * sublanes, -(-shape[-1] // 128) * 128
    return math.prod(shape[:-2]) * rows * lanes * size


def call(body, out, scalars, arrays, scratch=(), flops=0, own_copies=False):
    outs = jax.tree.leaves(out)
    bytes_ = sum(padded_bytes(a.shape, a.dtype) for a in (*arrays, *outs))
    held = sum(padded_bytes(shape, dtype) for shape, dtype in scratch)
    scratch = [pltpu.VMEM(shape, dtype) for shape, dtype in scratch]
    if own_copies:
        scratch += [pltpu.VMEM(a.shape, a.dtype) for a in arrays] + [pltpu.SemaphoreType.DMA((len(arrays),))]
    return pl.pallas_call(
        body,
        out_shape=out,
        in_specs=[SMEM] * len(scalars) + [HBM if own_copies else VMEM] * len(arrays),
        out_specs=jax.tree.map(lambda _: VMEM, out),
        scratch_shapes=scratch,
        compiler_params=pltpu.CompilerParams(
            vmem_limit_bytes=56 * 2**20 if own_copies else int(1.5 * (bytes_ + held)) + 4 * 2**20
        ),
        cost_estimate=pl.CostEstimate(flops=flops, bytes_accessed=bytes_, transcendentals=0),
    )(*scalars, *arrays)


def fetch(sources, targets, semaphores):
    copies = [
        pltpu.make_async_copy(source, target, semaphores.at[k])
        for k, (source, target) in enumerate(zip(sources, targets))
    ]
    for copy in copies:
        copy.start()
    return copies


def column_of(row, first, count, each=1):
    wide = row.shape[1]
    place = first + lax.broadcasted_iota(jnp.int32, (count, wide), 0)
    start = lax.broadcasted_iota(jnp.int32, (count, wide), 1) * each
    hit = jnp.logical_and(place >= start, place < start + each)
    return jnp.sum(jnp.where(hit, row, 0.0), axis=1, keepdims=True)


def upwind_change(state, sign):
    cells = state.shape[1]
    spot = lax.broadcasted_iota(jnp.int32, (1, cells), 1)
    after = jnp.where(spot == cells - 1, 0.0, pltpu.roll(state, cells - 1, 1))
    before = jnp.where(spot == 0, 0.0, pltpu.roll(state, 1, 1))
    return state - jnp.where(sign > 0, after, before)


def pack_kernel(adjoint_, labels_, conductance_, out, adjoint, labels, conductance, semaphores):
    copies = fetch((adjoint_, labels_, conductance_), (adjoint, labels, conductance), semaphores)
    for copy in copies[1:]:
        copy.wait()
    groups, rows, columns = out.shape
    part = adjoint.shape[1] // groups
    label = column_of(labels[...].astype(f32), 0, rows)
    kinds = lax.broadcasted_iota(jnp.int32, (rows, conductance.shape[1]), 1).astype(f32)
    kappa = jnp.sum(jnp.where(kinds == label, conductance[...], 0.0), axis=1, keepdims=True)
    first, _ = split(kappa)
    second, third = split(kappa - first.astype(f32))
    column = lax.broadcasted_iota(jnp.int32, (rows, columns - part), 1)
    scale = jnp.where(column == 0, first.astype(f32), 0.0) + jnp.where(column == 1, second.astype(f32), 0.0)
    scale = (scale + jnp.where(column == 2, third.astype(f32), 0.0)).astype(bf16)
    copies[0].wait()
    for group in range(groups):
        out[group, :, :part] = adjoint[:, group * part : (group + 1) * part].astype(bf16)
        out[group, :, part:] = scale


def index_of():
    line, pair = lax.axis_index("line"), lax.axis_index("pair")
    return line, pair, 2 * line + pair


def flip_kernel(collision, adjoint, source, out, place):
    base = split(adjoint[...] + relax_factor * source[...])
    out[...] = jnp.concatenate([collision[...] * bf16(-relax_factor), *base], axis=0).T
    rows, cells = adjoint.shape[0], place.shape[1]
    _, _, me = index_of()
    row = lax.broadcasted_iota(jnp.int32, (rows, cells), 0)
    column = lax.broadcasted_iota(jnp.int32, (rows, cells), 1)
    mine = (column == row + me * rows).astype(f32).astype(bf16)
    place[:rows, :] = mine
    place[rows:, :] = mine


def ways_of(lines):
    return [(0, 1), (1, 0), (1, 1)] if lines > 1 else [(0, 1)]


def fours(lines):
    return max(lines // 2, 1)


def hand_out(blocks, outs, lines):
    line, pair, _ = index_of()
    outs, count = iter(outs), fours(lines)
    for four in range(count):
        next(outs)[...] = blocks[2 * (line ^ (2 * four)) + pair]
    if count > 1:
        for bit, other in ways_of(lines)[:2]:
            out = next(outs)
            for four in range(1, count):
                out[four - 1] = blocks[2 * (line ^ (2 * four + bit)) + (pair ^ other)].astype(bf16)
    for four in range(1, count):
        next(outs)[...] = blocks[2 * (line ^ (2 * four + 1)) + (pair ^ 1)].astype(bf16)
    for bit, other in ways_of(lines):
        next(outs)[...] = blocks[2 * (line ^ bit) + (pair ^ other)].astype(bf16)


def handed_out(lines, block):
    count, sent = fours(lines), jax.ShapeDtypeStruct(block, bf16)
    kept = [jax.ShapeDtypeStruct(block, f32)] * count
    far = [jax.ShapeDtypeStruct((count - 1, *block), bf16)] * 2 if count > 1 else []
    return kept + far + [sent] * (count - 1) + [sent] * len(ways_of(lines))


def first_kernel(flipped, place, full, *refs):
    *outs, terms = refs
    lines = terms.shape[0] // 2
    depth = full.shape[0]
    result = jnp.dot(flipped[:, :depth], full[...], preferred_element_type=f32)
    result += jnp.dot(flipped[:, depth:], place[...], preferred_element_type=f32)
    terms[...] = result.reshape(terms.shape)
    hand_out(terms, outs, lines)


def transport_kernel(start, kappa, speed, direction, out, rate_out, sign_out):
    part, _ = out.shape
    first = index_of()[2] * part
    rate_out[...] = relax_factor * column_of(speed[...], first, part) * kappa[:1, :]
    sign_out[...] = 2.0 * column_of(direction[...].astype(f32), first, part, BRANCH) - 1.0
    out[...] = rate_out[...] * upwind_change(start[...].astype(f32), sign_out[...])


def second_kernel(flipped, full, state, rate, sign, *refs):
    *outs, terms, blocks = refs
    groups, part, cells = terms.shape
    lines = groups // 2
    depth = full.shape[0]
    _, _, me = index_of()
    terms[...] = jnp.dot(flipped[:, :depth], full[...], preferred_element_type=f32).reshape(terms.shape)
    terms[me] += state[...] - rate[...] * upwind_change(state[...], sign[...])
    blocks[...] = terms[...].reshape(groups * part, cells).T.reshape(blocks.shape)
    hand_out(blocks, outs, lines)


def swapped(block, lines, bits, other):
    pairs = [(2 * i + p, 2 * (i ^ bits) + (p ^ other)) for i in range(lines) for p in range(2)]
    return lax.ppermute(block, ("line", "pair"), pairs)


def reduce_over_cells(blocks, lines):
    count, ways, blocks = fours(lines), ways_of(lines), list(blocks)
    kept, blocks = blocks[:count], blocks[count:]
    near, blocks = blocks[-len(ways) :], blocks[: -len(ways)]
    terms = []
    if count > 1:
        arrived = [swapped(block, lines, *way) for block, way in zip(blocks[:2], ways)]
        for four in range(1, count):
            block = kept[four]
            for part in arrived:
                block = block + part[four - 1].astype(f32)
            terms.append(swapped(block.astype(bf16), lines, 2 * four, 0))
        terms += [swapped(block, lines, 2 * four + 3, 1) for four, block in enumerate(blocks[2:])]
    for way, block in list(zip(ways, near))[::-1]:
        terms.append(swapped(block, lines, *way))
    result = kept[0]
    for term in terms:
        result = result + term.astype(f32)
    return result


def shards(adjoint, source, collision, speed, direction, labels, conductance):
    rows, width = adjoint.shape
    lines, pairs, modes = lax.axis_size("line"), lax.axis_size("pair"), lax.axis_size("mode")
    groups = lines * pairs
    part = width // groups
    cells = rows * groups
    depth = modes * part
    shape = jax.ShapeDtypeStruct

    columns = -(-(part + EXTRA) // 128) * 128
    sent = call(
        pack_kernel,
        shape((groups, rows, columns), bf16),
        [],
        [adjoint, labels[None, :], conductance[None, :]],
        own_copies=True,
    )
    got = lax.all_to_all(sent, ("line", "pair"), split_axis=0, concat_axis=0, tiled=True).reshape(cells, columns)

    collision, sent = lax.optimization_barrier((collision, sent))
    flipped, place = call(
        flip_kernel,
        [shape((width, depth + 2 * rows), bf16), shape((2 * rows, cells), bf16)],
        [],
        [collision.reshape(depth, width), adjoint, source],
    )

    start = got[:, :part].T
    full = lax.all_gather(start, "mode", axis=0, tiled=True)
    terms = call(
        first_kernel,
        handed_out(lines, (part, cells)),
        [],
        [flipped, place, full],
        [((groups, part, cells), f32)],
        flops=2 * width * depth * cells,
    )
    start, got, terms = lax.optimization_barrier((start, got, terms))
    transport, rate, sign = call(
        transport_kernel,
        [shape((part, cells), f32), shape((part, cells), f32), shape((part, 1), f32)],
        [],
        [start, jnp.sum(got[:, part:].astype(f32), axis=1)[None, :], speed[None, :], direction[None, :]],
    )
    state = reduce_over_cells(terms, lines) - transport

    full = lax.all_gather(state.astype(bf16), "mode", axis=0, tiled=True)
    terms = call(
        second_kernel,
        handed_out(lines, (rows, width)),
        [],
        [flipped, full, state, rate, sign],
        [((groups, part, cells), f32), ((groups, rows, width), f32)],
        flops=2 * width * depth * cells,
    )
    return reduce_over_cells(terms, lines) + relax_factor * source


def solution(mesh):
    modes, groups = mesh.shape["mode"], mesh.shape["cell"]
    mesh = Mesh(mesh.devices.reshape(modes, groups // 2, 2), ("mode", "line", "pair"))
    cell = ("line", "pair")
    in_specs = (
        P(cell, "mode"),
        P(cell, "mode"),
        P(None, cell, None, "mode"),
        P("mode"),
        P("mode"),
        P(cell),
        P(),
    )
    out_specs = P(cell, "mode")
    return jax.shard_map(shards, mesh=mesh, in_specs=in_specs, out_specs=out_specs, check_vma=False)
```

```python
import math

import jax
import jax.numpy as jnp
from jax import lax
from jax.experimental import pallas as pl
from jax.experimental.pallas import tpu as pltpu
from jax.sharding import Mesh, PartitionSpec as P

BRANCH = 48
ITERS = 2


relax_factor = 0.5
VMEM = pl.BlockSpec(memory_space=pltpu.VMEM)
SMEM = pl.BlockSpec(memory_space=pltpu.SMEM)
HBM = pl.BlockSpec(memory_space=pltpu.HBM)
bf16, f32 = jnp.bfloat16, jnp.float32
EXTRA = 16


def split(array):
    head = array.astype(bf16)
    return head, (array - head.astype(f32)).astype(bf16)


def padded_bytes(shape, dtype):
    size = jnp.dtype(dtype).itemsize
    if len(shape) < 2:
        return 4096
    sublanes = 8 * 4 // size
    rows, lanes = -(-shape[-2] // sublanes) * sublanes, -(-shape[-1] // 128) * 128
    return math.prod(shape[:-2]) * rows * lanes * size


def call(body, out, scalars, arrays, scratch=(), flops=0, own_copies=False):
    outs = jax.tree.leaves(out)
    bytes_ = sum(padded_bytes(a.shape, a.dtype) for a in (*arrays, *outs))
    held = sum(padded_bytes(shape, dtype) for shape, dtype in scratch)
    scratch = [pltpu.VMEM(shape, dtype) for shape, dtype in scratch]
    if own_copies:
        scratch += [pltpu.VMEM(a.shape, a.dtype) for a in arrays] + [pltpu.SemaphoreType.DMA((len(arrays),))]
    return pl.pallas_call(
        body,
        out_shape=out,
        in_specs=[SMEM] * len(scalars) + [HBM if own_copies else VMEM] * len(arrays),
        out_specs=jax.tree.map(lambda _: VMEM, out),
        scratch_shapes=scratch,
        compiler_params=pltpu.CompilerParams(
            vmem_limit_bytes=56 * 2**20 if own_copies else int(1.5 * (bytes_ + held)) + 4 * 2**20
        ),
        cost_estimate=pl.CostEstimate(flops=flops, bytes_accessed=bytes_, transcendentals=0),
    )(*scalars, *arrays)


def fetch(sources, targets, semaphores):
    copies = [
        pltpu.make_async_copy(source, target, semaphores.at[k])
        for k, (source, target) in enumerate(zip(sources, targets))
    ]
    for copy in copies:
        copy.start()
    return copies


def column_of(row, first, count, each=1):
    wide = row.shape[1]
    place = first + lax.broadcasted_iota(jnp.int32, (count, wide), 0)
    start = lax.broadcasted_iota(jnp.int32, (count, wide), 1) * each
    hit = jnp.logical_and(place >= start, place < start + each)
    return jnp.sum(jnp.where(hit, row, 0.0), axis=1, keepdims=True)


def upwind_change(state, sign):
    cells = state.shape[1]
    spot = lax.broadcasted_iota(jnp.int32, (1, cells), 1)
    after = jnp.where(spot == cells - 1, 0.0, pltpu.roll(state, cells - 1, 1))
    before = jnp.where(spot == 0, 0.0, pltpu.roll(state, 1, 1))
    return state - jnp.where(sign > 0, after, before)


def pack_kernel(adjoint_, labels_, conductance_, out, adjoint, labels, conductance, semaphores):
    copies = fetch((adjoint_, labels_, conductance_), (adjoint, labels, conductance), semaphores)
    for copy in copies[1:]:
        copy.wait()
    groups, rows, columns = out.shape
    part = adjoint.shape[1] // groups
    label = column_of(labels[...].astype(f32), 0, rows)
    kinds = lax.broadcasted_iota(jnp.int32, (rows, conductance.shape[1]), 1).astype(f32)
    kappa = jnp.sum(jnp.where(kinds == label, conductance[...], 0.0), axis=1, keepdims=True)
    first, _ = split(kappa)
    second, third = split(kappa - first.astype(f32))
    column = lax.broadcasted_iota(jnp.int32, (rows, columns - part), 1)
    scale = jnp.where(column == 0, first.astype(f32), 0.0) + jnp.where(column == 1, second.astype(f32), 0.0)
    scale = (scale + jnp.where(column == 2, third.astype(f32), 0.0)).astype(bf16)
    copies[0].wait()
    for group in range(groups):
        out[group, :, :part] = adjoint[:, group * part : (group + 1) * part].astype(bf16)
        out[group, :, part:] = scale


def index_of():
    line, pair = lax.axis_index("line"), lax.axis_index("pair")
    return line, pair, 2 * line + pair


def flip_kernel(collision, adjoint, source, out, place):
    base = split(adjoint[...] + relax_factor * source[...])
    out[...] = jnp.concatenate([collision[...] * bf16(-relax_factor), *base], axis=0).T
    rows, cells = adjoint.shape[0], place.shape[1]
    _, _, me = index_of()
    row = lax.broadcasted_iota(jnp.int32, (rows, cells), 0)
    column = lax.broadcasted_iota(jnp.int32, (rows, cells), 1)
    mine = (column == row + me * rows).astype(f32).astype(bf16)
    place[:rows, :] = mine
    place[rows:, :] = mine


def ways_of(lines):
    return [(0, 1), (1, 0), (1, 1)] if lines > 1 else [(0, 1)]


def fours(lines):
    return max(lines // 2, 1)


def hand_out(blocks, outs, lines):
    line, pair, _ = index_of()
    outs, count = iter(outs), fours(lines)
    for four in range(count):
        next(outs)[...] = blocks[2 * (line ^ (2 * four)) + pair]
    if count > 1:
        for bit, other in ways_of(lines)[:2]:
            out = next(outs)
            for four in range(1, count):
                out[four - 1] = blocks[2 * (line ^ (2 * four + bit)) + (pair ^ other)].astype(bf16)
    for four in range(1, count):
        next(outs)[...] = blocks[2 * (line ^ (2 * four + 1)) + (pair ^ 1)].astype(bf16)
    for bit, other in ways_of(lines):
        next(outs)[...] = blocks[2 * (line ^ bit) + (pair ^ other)].astype(bf16)


def handed_out(lines, block):
    count, sent = fours(lines), jax.ShapeDtypeStruct(block, bf16)
    kept = [jax.ShapeDtypeStruct(block, f32)] * count
    far = [jax.ShapeDtypeStruct((count - 1, *block), bf16)] * 2 if count > 1 else []
    return kept + far + [sent] * (count - 1) + [sent] * len(ways_of(lines))


def first_kernel(flipped, place, full, *refs):
    *outs, terms = refs
    lines = terms.shape[0] // 2
    depth = full.shape[0]
    result = jnp.dot(flipped[:, :depth], full[...], preferred_element_type=f32)
    result += jnp.dot(flipped[:, depth:], place[...], preferred_element_type=f32)
    terms[...] = result.reshape(terms.shape)
    hand_out(terms, outs, lines)


def transport_kernel(start, kappa, speed, direction, out, rate_out, sign_out):
    part, _ = out.shape
    first = index_of()[2] * part
    rate_out[...] = relax_factor * column_of(speed[...], first, part) * kappa[:1, :]
    sign_out[...] = 2.0 * column_of(direction[...].astype(f32), first, part, BRANCH) - 1.0
    out[...] = rate_out[...] * upwind_change(start[...].astype(f32), sign_out[...])


def second_kernel(flipped, full, state, rate, sign, *refs):
    *outs, terms, blocks = refs
    groups, part, cells = terms.shape
    lines = groups // 2
    depth = full.shape[0]
    _, _, me = index_of()
    terms[...] = jnp.dot(flipped[:, :depth], full[...], preferred_element_type=f32).reshape(terms.shape)
    terms[me] += state[...] - rate[...] * upwind_change(state[...], sign[...])
    blocks[...] = terms[...].reshape(groups * part, cells).T.reshape(blocks.shape)
    hand_out(blocks, outs, lines)


def swapped(block, lines, bits, other):
    pairs = [(2 * i + p, 2 * (i ^ bits) + (p ^ other)) for i in range(lines) for p in range(2)]
    return lax.ppermute(block, ("line", "pair"), pairs)


def reduce_over_cells(blocks, lines):
    count, ways, blocks = fours(lines), ways_of(lines), list(blocks)
    kept, blocks = blocks[:count], blocks[count:]
    near, blocks = blocks[-len(ways) :], blocks[: -len(ways)]
    terms = []
    if count > 1:
        arrived = [swapped(block, lines, *way) for block, way in zip(blocks[:2], ways)]
        for four in range(1, count):
            block = kept[four]
            for part in arrived[::-1]:
                block = block + part[four - 1].astype(f32)
            block, near[0] = lax.optimization_barrier((block.astype(bf16), near[0]))
            terms.append(swapped(block, lines, 2 * four, 0))
        terms += [swapped(block, lines, 2 * four + 3, 1) for four, block in enumerate(blocks[2:])]
    for way, block in list(zip(ways, near))[::-1]:
        terms.append(swapped(block, lines, *way))
    result = kept[0]
    for term in terms:
        result = result + term.astype(f32)
    return result


def shards(adjoint, source, collision, speed, direction, labels, conductance):
    rows, width = adjoint.shape
    lines, pairs, modes = lax.axis_size("line"), lax.axis_size("pair"), lax.axis_size("mode")
    groups = lines * pairs
    part = width // groups
    cells = rows * groups
    depth = modes * part
    shape = jax.ShapeDtypeStruct

    columns = -(-(part + EXTRA) // 128) * 128
    sent = call(
        pack_kernel,
        shape((groups, rows, columns), bf16),
        [],
        [adjoint, labels[None, :], conductance[None, :]],
        own_copies=True,
    )
    got = lax.all_to_all(sent, ("line", "pair"), split_axis=0, concat_axis=0, tiled=True).reshape(cells, columns)

    collision, sent = lax.optimization_barrier((collision, sent))
    flipped, place = call(
        flip_kernel,
        [shape((width, depth + 2 * rows), bf16), shape((2 * rows, cells), bf16)],
        [],
        [collision.reshape(depth, width), adjoint, source],
    )

    start = got[:, :part].T
    full = lax.all_gather(start, "mode", axis=0, tiled=True)
    terms = call(
        first_kernel,
        handed_out(lines, (part, cells)),
        [],
        [flipped, place, full],
        [((groups, part, cells), f32)],
        flops=2 * width * depth * cells,
    )
    start, got, terms = lax.optimization_barrier((start, got, terms))
    transport, rate, sign = call(
        transport_kernel,
        [shape((part, cells), f32), shape((part, cells), f32), shape((part, 1), f32)],
        [],
        [start, jnp.sum(got[:, part:].astype(f32), axis=1)[None, :], speed[None, :], direction[None, :]],
    )
    state = reduce_over_cells(terms, lines) - transport

    full = lax.all_gather(state.astype(bf16), "mode", axis=0, tiled=True)
    terms = call(
        second_kernel,
        handed_out(lines, (rows, width)),
        [],
        [flipped, full, state, rate, sign],
        [((groups, part, cells), f32), ((groups, rows, width), f32)],
        flops=2 * width * depth * cells,
    )
    return reduce_over_cells(terms, lines) + relax_factor * source


def solution(mesh):
    modes, groups = mesh.shape["mode"], mesh.shape["cell"]
    mesh = Mesh(mesh.devices.reshape(modes, groups // 2, 2), ("mode", "line", "pair"))
    cell = ("line", "pair")
    in_specs = (
        P(cell, "mode"),
        P(cell, "mode"),
        P(None, cell, None, "mode"),
        P("mode"),
        P("mode"),
        P(cell),
        P(),
    )
    out_specs = P(cell, "mode")
    return jax.shard_map(shards, mesh=mesh, in_specs=in_specs, out_specs=out_specs, check_vma=False)
```

```python
import math

import jax
import jax.numpy as jnp
from jax import lax
from jax.experimental import pallas as pl
from jax.experimental.pallas import tpu as pltpu
from jax.sharding import Mesh, PartitionSpec as P

BRANCH = 48
ITERS = 2


relax_factor = 0.5
VMEM = pl.BlockSpec(memory_space=pltpu.VMEM)
SMEM = pl.BlockSpec(memory_space=pltpu.SMEM)
HBM = pl.BlockSpec(memory_space=pltpu.HBM)
bf16, f32 = jnp.bfloat16, jnp.float32
EXTRA = 16


def split(array):
    head = array.astype(bf16)
    return head, (array - head.astype(f32)).astype(bf16)


def padded_bytes(shape, dtype):
    size = jnp.dtype(dtype).itemsize
    if len(shape) < 2:
        return 4096
    sublanes = 8 * 4 // size
    rows, lanes = -(-shape[-2] // sublanes) * sublanes, -(-shape[-1] // 128) * 128
    return math.prod(shape[:-2]) * rows * lanes * size


def call(body, out, scalars, arrays, scratch=(), flops=0, own_copies=False):
    outs = jax.tree.leaves(out)
    bytes_ = sum(padded_bytes(a.shape, a.dtype) for a in (*arrays, *outs))
    held = sum(padded_bytes(shape, dtype) for shape, dtype in scratch)
    scratch = [pltpu.VMEM(shape, dtype) for shape, dtype in scratch]
    if own_copies:
        scratch += [pltpu.VMEM(a.shape, a.dtype) for a in arrays] + [pltpu.SemaphoreType.DMA((len(arrays),))]
    return pl.pallas_call(
        body,
        out_shape=out,
        in_specs=[SMEM] * len(scalars) + [HBM if own_copies else VMEM] * len(arrays),
        out_specs=jax.tree.map(lambda _: VMEM, out),
        scratch_shapes=scratch,
        compiler_params=pltpu.CompilerParams(
            vmem_limit_bytes=56 * 2**20 if own_copies else int(1.5 * (bytes_ + held)) + 4 * 2**20
        ),
        cost_estimate=pl.CostEstimate(flops=flops, bytes_accessed=bytes_, transcendentals=0),
    )(*scalars, *arrays)


def fetch(sources, targets, semaphores):
    copies = [
        pltpu.make_async_copy(source, target, semaphores.at[k])
        for k, (source, target) in enumerate(zip(sources, targets))
    ]
    for copy in copies:
        copy.start()
    return copies


def column_of(row, first, count, each=1):
    wide = row.shape[1]
    place = first + lax.broadcasted_iota(jnp.int32, (count, wide), 0)
    start = lax.broadcasted_iota(jnp.int32, (count, wide), 1) * each
    hit = jnp.logical_and(place >= start, place < start + each)
    return jnp.sum(jnp.where(hit, row, 0.0), axis=1, keepdims=True)


def upwind_change(state, sign):
    cells = state.shape[1]
    spot = lax.broadcasted_iota(jnp.int32, (1, cells), 1)
    after = jnp.where(spot == cells - 1, 0.0, pltpu.roll(state, cells - 1, 1))
    before = jnp.where(spot == 0, 0.0, pltpu.roll(state, 1, 1))
    return state - jnp.where(sign > 0, after, before)


def pack_kernel(adjoint_, labels_, conductance_, out, adjoint, labels, conductance, semaphores):
    copies = fetch((adjoint_, labels_, conductance_), (adjoint, labels, conductance), semaphores)
    for copy in copies[1:]:
        copy.wait()
    groups, rows, columns = out.shape
    part = adjoint.shape[1] // groups
    label = column_of(labels[...].astype(f32), 0, rows)
    kinds = lax.broadcasted_iota(jnp.int32, (rows, conductance.shape[1]), 1).astype(f32)
    kappa = jnp.sum(jnp.where(kinds == label, conductance[...], 0.0), axis=1, keepdims=True)
    first, _ = split(kappa)
    second, third = split(kappa - first.astype(f32))
    column = lax.broadcasted_iota(jnp.int32, (rows, columns - part), 1)
    scale = jnp.where(column == 0, first.astype(f32), 0.0) + jnp.where(column == 1, second.astype(f32), 0.0)
    scale = (scale + jnp.where(column == 2, third.astype(f32), 0.0)).astype(bf16)
    copies[0].wait()
    for group in range(groups):
        out[group, :, :part] = adjoint[:, group * part : (group + 1) * part].astype(bf16)
        out[group, :, part:] = scale


def index_of():
    line, pair = lax.axis_index("line"), lax.axis_index("pair")
    return line, pair, 2 * line + pair


def flip_kernel(collision, adjoint, source, out, place):
    base = split(adjoint[...] + relax_factor * source[...])
    out[...] = jnp.concatenate([collision[...] * bf16(-relax_factor), *base], axis=0).T
    rows, cells = adjoint.shape[0], place.shape[1]
    _, _, me = index_of()
    row = lax.broadcasted_iota(jnp.int32, (rows, cells), 0)
    column = lax.broadcasted_iota(jnp.int32, (rows, cells), 1)
    mine = (column == row + me * rows).astype(f32).astype(bf16)
    place[:rows, :] = mine
    place[rows:, :] = mine


def ways_of(lines):
    return [(0, 1), (1, 0), (1, 1)] if lines > 1 else [(0, 1)]


def fours(lines):
    return max(lines // 2, 1)


def hand_out(blocks, outs, lines):
    line, pair, _ = index_of()
    outs, count = iter(outs), fours(lines)
    for four in range(count):
        next(outs)[...] = blocks[2 * (line ^ (2 * four)) + pair]
    if count > 1:
        for bit, other in ways_of(lines)[:2]:
            out = next(outs)
            for four in range(1, count):
                out[four - 1] = blocks[2 * (line ^ (2 * four + bit)) + (pair ^ other)].astype(bf16)
    for four in range(1, count):
        next(outs)[...] = blocks[2 * (line ^ (2 * four + 1)) + (pair ^ 1)].astype(bf16)
    for bit, other in ways_of(lines):
        next(outs)[...] = blocks[2 * (line ^ bit) + (pair ^ other)].astype(bf16)


def handed_out(lines, block):
    count, sent = fours(lines), jax.ShapeDtypeStruct(block, bf16)
    kept = [jax.ShapeDtypeStruct(block, f32)] * count
    far = [jax.ShapeDtypeStruct((count - 1, *block), bf16)] * 2 if count > 1 else []
    return kept + far + [sent] * (count - 1) + [sent] * len(ways_of(lines))


def first_kernel(flipped, place, full, *refs):
    *outs, terms = refs
    lines = terms.shape[0] // 2
    depth = full.shape[0]
    result = jnp.dot(flipped[:, :depth], full[...], preferred_element_type=f32)
    result += jnp.dot(flipped[:, depth:], place[...], preferred_element_type=f32)
    terms[...] = result.reshape(terms.shape)
    hand_out(terms, outs, lines)


def transport_kernel(start, kappa, speed, direction, out, rate_out, sign_out):
    part, _ = out.shape
    first = index_of()[2] * part
    rate_out[...] = relax_factor * column_of(speed[...], first, part) * kappa[:1, :]
    sign_out[...] = 2.0 * column_of(direction[...].astype(f32), first, part, BRANCH) - 1.0
    out[...] = rate_out[...] * upwind_change(start[...].astype(f32), sign_out[...])


def second_kernel(flipped, full, state, rate, sign, *refs):
    *outs, terms, blocks = refs
    groups, part, cells = terms.shape
    lines = groups // 2
    depth = full.shape[0]
    _, _, me = index_of()
    terms[...] = jnp.dot(flipped[:, :depth], full[...], preferred_element_type=f32).reshape(terms.shape)
    terms[me] += state[...] - rate[...] * upwind_change(state[...], sign[...])
    blocks[...] = terms[...].reshape(groups * part, cells).T.reshape(blocks.shape)
    hand_out(blocks, outs, lines)


def swapped(block, lines, bits, other):
    pairs = [(2 * i + p, 2 * (i ^ bits) + (p ^ other)) for i in range(lines) for p in range(2)]
    return lax.ppermute(block, ("line", "pair"), pairs)


def reduce_over_cells(blocks, lines):
    count, ways, blocks = fours(lines), ways_of(lines), list(blocks)
    kept, blocks = blocks[:count], blocks[count:]
    near, blocks = blocks[-len(ways) :], blocks[: -len(ways)]
    terms = []
    if count > 1:
        arrived = [swapped(block, lines, *way) for block, way in zip(blocks[:2], ways)]
        for four in range(1, count):
            block = kept[four]
            for part in arrived:
                block = block + part[four - 1].astype(f32)
            block, near[0] = lax.optimization_barrier((block.astype(bf16), near[0]))
            terms.append(swapped(block, lines, 2 * four, 0))
        terms += [swapped(block, lines, 2 * four + 3, 1) for four, block in enumerate(blocks[2:])]
    for way, block in list(zip(ways, near))[1:] + list(zip(ways, near))[:1]:
        terms.append(swapped(block, lines, *way))
    result = kept[0]
    for term in terms:
        result = result + term.astype(f32)
    return result


def shards(adjoint, source, collision, speed, direction, labels, conductance):
    rows, width = adjoint.shape
    lines, pairs, modes = lax.axis_size("line"), lax.axis_size("pair"), lax.axis_size("mode")
    groups = lines * pairs
    part = width // groups
    cells = rows * groups
    depth = modes * part
    shape = jax.ShapeDtypeStruct

    columns = -(-(part + EXTRA) // 128) * 128
    sent = call(
        pack_kernel,
        shape((groups, rows, columns), bf16),
        [],
        [adjoint, labels[None, :], conductance[None, :]],
        own_copies=True,
    )
    got = lax.all_to_all(sent, ("line", "pair"), split_axis=0, concat_axis=0, tiled=True).reshape(cells, columns)

    collision, sent = lax.optimization_barrier((collision, sent))
    flipped, place = call(
        flip_kernel,
        [shape((width, depth + 2 * rows), bf16), shape((2 * rows, cells), bf16)],
        [],
        [collision.reshape(depth, width), adjoint, source],
    )

    start = got[:, :part].T
    full = lax.all_gather(start, "mode", axis=0, tiled=True)
    terms = call(
        first_kernel,
        handed_out(lines, (part, cells)),
        [],
        [flipped, place, full],
        [((groups, part, cells), f32)],
        flops=2 * width * depth * cells,
    )
    start, got, terms = lax.optimization_barrier((start, got, terms))
    transport, rate, sign = call(
        transport_kernel,
        [shape((part, cells), f32), shape((part, cells), f32), shape((part, 1), f32)],
        [],
        [start, jnp.sum(got[:, part:].astype(f32), axis=1)[None, :], speed[None, :], direction[None, :]],
    )
    state = reduce_over_cells(terms, lines) - transport

    full = lax.all_gather(state.astype(bf16), "mode", axis=0, tiled=True)
    terms = call(
        second_kernel,
        handed_out(lines, (rows, width)),
        [],
        [flipped, full, state, rate, sign],
        [((groups, part, cells), f32), ((groups, rows, width), f32)],
        flops=2 * width * depth * cells,
    )
    return reduce_over_cells(terms, lines) + relax_factor * source


def solution(mesh):
    modes, groups = mesh.shape["mode"], mesh.shape["cell"]
    mesh = Mesh(mesh.devices.reshape(modes, groups // 2, 2), ("mode", "line", "pair"))
    cell = ("line", "pair")
    in_specs = (
        P(cell, "mode"),
        P(cell, "mode"),
        P(None, cell, None, "mode"),
        P("mode"),
        P("mode"),
        P(cell),
        P(),
    )
    out_specs = P(cell, "mode")
    return jax.shard_map(shards, mesh=mesh, in_specs=in_specs, out_specs=out_specs, check_vma=False)
```

```python
import math

import jax
import jax.numpy as jnp
from jax import lax
from jax.experimental import pallas as pl
from jax.experimental.pallas import tpu as pltpu
from jax.sharding import Mesh, PartitionSpec as P

BRANCH = 48
ITERS = 2


relax_factor = 0.5
VMEM = pl.BlockSpec(memory_space=pltpu.VMEM)
SMEM = pl.BlockSpec(memory_space=pltpu.SMEM)
HBM = pl.BlockSpec(memory_space=pltpu.HBM)
bf16, f32 = jnp.bfloat16, jnp.float32
EXTRA = 16


def split(array):
    head = array.astype(bf16)
    return head, (array - head.astype(f32)).astype(bf16)


def padded_bytes(shape, dtype):
    size = jnp.dtype(dtype).itemsize
    if len(shape) < 2:
        return 4096
    sublanes = 8 * 4 // size
    rows, lanes = -(-shape[-2] // sublanes) * sublanes, -(-shape[-1] // 128) * 128
    return math.prod(shape[:-2]) * rows * lanes * size


def call(body, out, scalars, arrays, scratch=(), flops=0, own_copies=False):
    outs = jax.tree.leaves(out)
    bytes_ = sum(padded_bytes(a.shape, a.dtype) for a in (*arrays, *outs))
    held = sum(padded_bytes(shape, dtype) for shape, dtype in scratch)
    scratch = [pltpu.VMEM(shape, dtype) for shape, dtype in scratch]
    if own_copies:
        scratch += [pltpu.VMEM(a.shape, a.dtype) for a in arrays] + [pltpu.SemaphoreType.DMA((len(arrays),))]
    return pl.pallas_call(
        body,
        out_shape=out,
        in_specs=[SMEM] * len(scalars) + [HBM if own_copies else VMEM] * len(arrays),
        out_specs=jax.tree.map(lambda _: VMEM, out),
        scratch_shapes=scratch,
        compiler_params=pltpu.CompilerParams(
            vmem_limit_bytes=56 * 2**20 if own_copies else int(1.5 * (bytes_ + held)) + 4 * 2**20
        ),
        cost_estimate=pl.CostEstimate(flops=flops, bytes_accessed=bytes_, transcendentals=0),
    )(*scalars, *arrays)


def fetch(sources, targets, semaphores):
    copies = [
        pltpu.make_async_copy(source, target, semaphores.at[k])
        for k, (source, target) in enumerate(zip(sources, targets))
    ]
    for copy in copies:
        copy.start()
    return copies


def column_of(row, first, count, each=1):
    wide = row.shape[1]
    place = first + lax.broadcasted_iota(jnp.int32, (count, wide), 0)
    start = lax.broadcasted_iota(jnp.int32, (count, wide), 1) * each
    hit = jnp.logical_and(place >= start, place < start + each)
    return jnp.sum(jnp.where(hit, row, 0.0), axis=1, keepdims=True)


def upwind_change(state, sign):
    cells = state.shape[1]
    spot = lax.broadcasted_iota(jnp.int32, (1, cells), 1)
    after = jnp.where(spot == cells - 1, 0.0, pltpu.roll(state, cells - 1, 1))
    before = jnp.where(spot == 0, 0.0, pltpu.roll(state, 1, 1))
    return state - jnp.where(sign > 0, after, before)


def pack_kernel(adjoint_, labels_, conductance_, out, adjoint, labels, conductance, semaphores):
    copies = fetch((adjoint_, labels_, conductance_), (adjoint, labels, conductance), semaphores)
    for copy in copies[1:]:
        copy.wait()
    groups, rows, columns = out.shape
    part = adjoint.shape[1] // groups
    label = column_of(labels[...].astype(f32), 0, rows)
    kinds = lax.broadcasted_iota(jnp.int32, (rows, conductance.shape[1]), 1).astype(f32)
    kappa = jnp.sum(jnp.where(kinds == label, conductance[...], 0.0), axis=1, keepdims=True)
    first, _ = split(kappa)
    second, third = split(kappa - first.astype(f32))
    column = lax.broadcasted_iota(jnp.int32, (rows, columns - part), 1)
    scale = jnp.where(column == 0, first.astype(f32), 0.0) + jnp.where(column == 1, second.astype(f32), 0.0)
    scale = (scale + jnp.where(column == 2, third.astype(f32), 0.0)).astype(bf16)
    copies[0].wait()
    for group in range(groups):
        out[group, :, :part] = adjoint[:, group * part : (group + 1) * part].astype(bf16)
        out[group, :, part:] = scale


def index_of():
    line, pair = lax.axis_index("line"), lax.axis_index("pair")
    return line, pair, 2 * line + pair


def flip_kernel(collision, adjoint, source, out, place):
    base = split(adjoint[...] + relax_factor * source[...])
    out[...] = jnp.concatenate([collision[...] * bf16(-relax_factor), *base], axis=0).T
    rows, cells = adjoint.shape[0], place.shape[1]
    _, _, me = index_of()
    row = lax.broadcasted_iota(jnp.int32, (rows, cells), 0)
    column = lax.broadcasted_iota(jnp.int32, (rows, cells), 1)
    mine = (column == row + me * rows).astype(f32).astype(bf16)
    place[:rows, :] = mine
    place[rows:, :] = mine


def ways_of(lines):
    return [(0, 1), (1, 0), (1, 1)] if lines > 1 else [(0, 1)]


def fours(lines):
    return max(lines // 2, 1)


def hand_out(blocks, outs, lines):
    line, pair, _ = index_of()
    outs, count = iter(outs), fours(lines)
    for four in range(count):
        next(outs)[...] = blocks[2 * (line ^ (2 * four)) + pair]
    if count > 1:
        for bit, other in ways_of(lines)[:2]:
            out = next(outs)
            for four in range(1, count):
                out[four - 1] = blocks[2 * (line ^ (2 * four + bit)) + (pair ^ other)].astype(bf16)
    for four in range(1, count):
        next(outs)[...] = blocks[2 * (line ^ (2 * four + 1)) + (pair ^ 1)].astype(bf16)
    for bit, other in ways_of(lines):
        next(outs)[...] = blocks[2 * (line ^ bit) + (pair ^ other)].astype(bf16)


def handed_out(lines, block):
    count, sent = fours(lines), jax.ShapeDtypeStruct(block, bf16)
    kept = [jax.ShapeDtypeStruct(block, f32)] * count
    far = [jax.ShapeDtypeStruct((count - 1, *block), bf16)] * 2 if count > 1 else []
    return kept + far + [sent] * (count - 1) + [sent] * len(ways_of(lines))


def first_kernel(flipped, place, full, *refs):
    *outs, terms = refs
    lines = terms.shape[0] // 2
    depth = full.shape[0]
    result = jnp.dot(flipped[:, :depth], full[...], preferred_element_type=f32)
    result += jnp.dot(flipped[:, depth:], place[...], preferred_element_type=f32)
    terms[...] = result.reshape(terms.shape)
    hand_out(terms, outs, lines)


def transport_kernel(start, kappa, speed, direction, out, rate_out, sign_out):
    part, _ = out.shape
    first = index_of()[2] * part
    rate_out[...] = relax_factor * column_of(speed[...], first, part) * kappa[:1, :]
    sign_out[...] = 2.0 * column_of(direction[...].astype(f32), first, part, BRANCH) - 1.0
    out[...] = rate_out[...] * upwind_change(start[...].astype(f32), sign_out[...])


def second_kernel(flipped, full, state, rate, sign, *refs):
    *outs, terms, blocks = refs
    groups, part, cells = terms.shape
    lines = groups // 2
    depth = full.shape[0]
    _, _, me = index_of()
    terms[...] = jnp.dot(flipped[:, :depth], full[...], preferred_element_type=f32).reshape(terms.shape)
    terms[me] += state[...] - rate[...] * upwind_change(state[...], sign[...])
    blocks[...] = terms[...].reshape(groups * part, cells).T.reshape(blocks.shape)
    hand_out(blocks, outs, lines)


def swapped(block, lines, bits, other):
    pairs = [(2 * i + p, 2 * (i ^ bits) + (p ^ other)) for i in range(lines) for p in range(2)]
    return lax.ppermute(block, ("line", "pair"), pairs)


def reduce_over_cells(blocks, lines):
    count, ways, blocks = fours(lines), ways_of(lines), list(blocks)
    kept, blocks = blocks[:count], blocks[count:]
    near, blocks = blocks[-len(ways) :], blocks[: -len(ways)]
    terms = []
    if count > 1:
        arrived = [swapped(block, lines, *way) for block, way in zip(blocks[:2], ways)]
        for four in range(1, count):
            block = kept[four]
            for part in arrived:
                block = block + part[four - 1].astype(f32)
            block, near[1] = lax.optimization_barrier((block.astype(bf16), near[1]))
            terms.append(swapped(block, lines, 2 * four, 0))
        terms += [swapped(block, lines, 2 * four + 3, 1) for four, block in enumerate(blocks[2:])]
    for way, block in list(zip(ways, near))[2:] + list(zip(ways, near))[:2]:
        terms.append(swapped(block, lines, *way))
    result = kept[0]
    for term in terms:
        result = result + term.astype(f32)
    return result


def shards(adjoint, source, collision, speed, direction, labels, conductance):
    rows, width = adjoint.shape
    lines, pairs, modes = lax.axis_size("line"), lax.axis_size("pair"), lax.axis_size("mode")
    groups = lines * pairs
    part = width // groups
    cells = rows * groups
    depth = modes * part
    shape = jax.ShapeDtypeStruct

    columns = -(-(part + EXTRA) // 128) * 128
    sent = call(
        pack_kernel,
        shape((groups, rows, columns), bf16),
        [],
        [adjoint, labels[None, :], conductance[None, :]],
        own_copies=True,
    )
    got = lax.all_to_all(sent, ("line", "pair"), split_axis=0, concat_axis=0, tiled=True).reshape(cells, columns)

    collision, sent = lax.optimization_barrier((collision, sent))
    flipped, place = call(
        flip_kernel,
        [shape((width, depth + 2 * rows), bf16), shape((2 * rows, cells), bf16)],
        [],
        [collision.reshape(depth, width), adjoint, source],
    )

    start = got[:, :part].T
    full = lax.all_gather(start, "mode", axis=0, tiled=True)
    terms = call(
        first_kernel,
        handed_out(lines, (part, cells)),
        [],
        [flipped, place, full],
        [((groups, part, cells), f32)],
        flops=2 * width * depth * cells,
    )
    start, got, terms = lax.optimization_barrier((start, got, terms))
    transport, rate, sign = call(
        transport_kernel,
        [shape((part, cells), f32), shape((part, cells), f32), shape((part, 1), f32)],
        [],
        [start, jnp.sum(got[:, part:].astype(f32), axis=1)[None, :], speed[None, :], direction[None, :]],
    )
    state = reduce_over_cells(terms, lines) - transport

    full = lax.all_gather(state.astype(bf16), "mode", axis=0, tiled=True)
    terms = call(
        second_kernel,
        handed_out(lines, (rows, width)),
        [],
        [flipped, full, state, rate, sign],
        [((groups, part, cells), f32), ((groups, rows, width), f32)],
        flops=2 * width * depth * cells,
    )
    return reduce_over_cells(terms, lines) + relax_factor * source


def solution(mesh):
    modes, groups = mesh.shape["mode"], mesh.shape["cell"]
    mesh = Mesh(mesh.devices.reshape(modes, groups // 2, 2), ("mode", "line", "pair"))
    cell = ("line", "pair")
    in_specs = (
        P(cell, "mode"),
        P(cell, "mode"),
        P(None, cell, None, "mode"),
        P("mode"),
        P("mode"),
        P(cell),
        P(),
    )
    out_specs = P(cell, "mode")
    return jax.shard_map(shards, mesh=mesh, in_specs=in_specs, out_specs=out_specs, check_vma=False)
```

```python
import math

import jax
import jax.numpy as jnp
from jax import lax
from jax.experimental import pallas as pl
from jax.experimental.pallas import tpu as pltpu
from jax.sharding import Mesh, PartitionSpec as P

BRANCH = 48
ITERS = 2


relax_factor = 0.5
VMEM = pl.BlockSpec(memory_space=pltpu.VMEM)
SMEM = pl.BlockSpec(memory_space=pltpu.SMEM)
HBM = pl.BlockSpec(memory_space=pltpu.HBM)
bf16, f32 = jnp.bfloat16, jnp.float32
EXTRA = 16


def split(array):
    head = array.astype(bf16)
    return head, (array - head.astype(f32)).astype(bf16)


def padded_bytes(shape, dtype):
    size = jnp.dtype(dtype).itemsize
    if len(shape) < 2:
        return 4096
    sublanes = 8 * 4 // size
    rows, lanes = -(-shape[-2] // sublanes) * sublanes, -(-shape[-1] // 128) * 128
    return math.prod(shape[:-2]) * rows * lanes * size


def call(body, out, scalars, arrays, scratch=(), flops=0, own_copies=False):
    outs = jax.tree.leaves(out)
    bytes_ = sum(padded_bytes(a.shape, a.dtype) for a in (*arrays, *outs))
    held = sum(padded_bytes(shape, dtype) for shape, dtype in scratch)
    scratch = [pltpu.VMEM(shape, dtype) for shape, dtype in scratch]
    if own_copies:
        scratch += [pltpu.VMEM(a.shape, a.dtype) for a in arrays] + [pltpu.SemaphoreType.DMA((len(arrays) + out.shape[0],))]
    return pl.pallas_call(
        body,
        out_shape=out,
        in_specs=[SMEM] * len(scalars) + [HBM if own_copies else VMEM] * len(arrays),
        out_specs=jax.tree.map(lambda _: HBM if own_copies else VMEM, out),
        scratch_shapes=scratch,
        compiler_params=pltpu.CompilerParams(
            vmem_limit_bytes=56 * 2**20 if own_copies else int(1.5 * (bytes_ + held)) + 4 * 2**20
        ),
        cost_estimate=pl.CostEstimate(flops=flops, bytes_accessed=bytes_, transcendentals=0),
    )(*scalars, *arrays)


def fetch(sources, targets, semaphores):
    copies = [
        pltpu.make_async_copy(source, target, semaphores.at[k])
        for k, (source, target) in enumerate(zip(sources, targets))
    ]
    for copy in copies:
        copy.start()
    return copies


def column_of(row, first, count, each=1):
    wide = row.shape[1]
    place = first + lax.broadcasted_iota(jnp.int32, (count, wide), 0)
    start = lax.broadcasted_iota(jnp.int32, (count, wide), 1) * each
    hit = jnp.logical_and(place >= start, place < start + each)
    return jnp.sum(jnp.where(hit, row, 0.0), axis=1, keepdims=True)


def upwind_change(state, sign):
    cells = state.shape[1]
    spot = lax.broadcasted_iota(jnp.int32, (1, cells), 1)
    after = jnp.where(spot == cells - 1, 0.0, pltpu.roll(state, cells - 1, 1))
    before = jnp.where(spot == 0, 0.0, pltpu.roll(state, 1, 1))
    return state - jnp.where(sign > 0, after, before)


def pack_kernel(adjoint_, labels_, conductance_, out, blocks, adjoint, labels, conductance, semaphores):
    copies = fetch((adjoint_, labels_, conductance_), (adjoint, labels, conductance), semaphores)
    for copy in copies[1:]:
        copy.wait()
    groups, rows, columns = out.shape
    part = adjoint.shape[1] // groups
    label = column_of(labels[...].astype(f32), 0, rows)
    kinds = lax.broadcasted_iota(jnp.int32, (rows, conductance.shape[1]), 1).astype(f32)
    kappa = jnp.sum(jnp.where(kinds == label, conductance[...], 0.0), axis=1, keepdims=True)
    first, _ = split(kappa)
    second, third = split(kappa - first.astype(f32))
    column = lax.broadcasted_iota(jnp.int32, (rows, columns - part), 1)
    scale = jnp.where(column == 0, first.astype(f32), 0.0) + jnp.where(column == 1, second.astype(f32), 0.0)
    scale = (scale + jnp.where(column == 2, third.astype(f32), 0.0)).astype(bf16)
    copies[0].wait()
    sent = []
    for group in range(groups):
        blocks[group, :, :part] = adjoint[:, group * part : (group + 1) * part].astype(bf16)
        blocks[group, :, part:] = scale
        sent.append(pltpu.make_async_copy(blocks.at[group], out.at[group], semaphores.at[len(copies) + group]))
        sent[-1].start()
    for copy in sent:
        copy.wait()


def index_of():
    line, pair = lax.axis_index("line"), lax.axis_index("pair")
    return line, pair, 2 * line + pair


def flip_kernel(collision, adjoint, source, out, place):
    base = split(adjoint[...] + relax_factor * source[...])
    out[...] = jnp.concatenate([collision[...] * bf16(-relax_factor), *base], axis=0).T
    rows, cells = adjoint.shape[0], place.shape[1]
    _, _, me = index_of()
    row = lax.broadcasted_iota(jnp.int32, (rows, cells), 0)
    column = lax.broadcasted_iota(jnp.int32, (rows, cells), 1)
    mine = (column == row + me * rows).astype(f32).astype(bf16)
    place[:rows, :] = mine
    place[rows:, :] = mine


def ways_of(lines):
    return [(0, 1), (1, 0), (1, 1)] if lines > 1 else [(0, 1)]


def fours(lines):
    return max(lines // 2, 1)


def hand_out(blocks, outs, lines):
    line, pair, _ = index_of()
    outs, count = iter(outs), fours(lines)
    for four in range(count):
        next(outs)[...] = blocks[2 * (line ^ (2 * four)) + pair]
    if count > 1:
        for bit, other in ways_of(lines)[:2]:
            out = next(outs)
            for four in range(1, count):
                out[four - 1] = blocks[2 * (line ^ (2 * four + bit)) + (pair ^ other)].astype(bf16)
    for four in range(1, count):
        next(outs)[...] = blocks[2 * (line ^ (2 * four + 1)) + (pair ^ 1)].astype(bf16)
    for bit, other in ways_of(lines):
        next(outs)[...] = blocks[2 * (line ^ bit) + (pair ^ other)].astype(bf16)


def handed_out(lines, block):
    count, sent = fours(lines), jax.ShapeDtypeStruct(block, bf16)
    kept = [jax.ShapeDtypeStruct(block, f32)] * count
    far = [jax.ShapeDtypeStruct((count - 1, *block), bf16)] * 2 if count > 1 else []
    return kept + far + [sent] * (count - 1) + [sent] * len(ways_of(lines))


def first_kernel(flipped, place, full, *refs):
    *outs, terms = refs
    lines = terms.shape[0] // 2
    depth = full.shape[0]
    result = jnp.dot(flipped[:, :depth], full[...], preferred_element_type=f32)
    result += jnp.dot(flipped[:, depth:], place[...], preferred_element_type=f32)
    terms[...] = result.reshape(terms.shape)
    hand_out(terms, outs, lines)


def transport_kernel(start, kappa, speed, direction, out, rate_out, sign_out):
    part, _ = out.shape
    first = index_of()[2] * part
    rate_out[...] = relax_factor * column_of(speed[...], first, part) * kappa[:1, :]
    sign_out[...] = 2.0 * column_of(direction[...].astype(f32), first, part, BRANCH) - 1.0
    out[...] = rate_out[...] * upwind_change(start[...].astype(f32), sign_out[...])


def second_kernel(flipped, full, state, rate, sign, *refs):
    *outs, terms, blocks = refs
    groups, part, cells = terms.shape
    lines = groups // 2
    depth = full.shape[0]
    _, _, me = index_of()
    terms[...] = jnp.dot(flipped[:, :depth], full[...], preferred_element_type=f32).reshape(terms.shape)
    terms[me] += state[...] - rate[...] * upwind_change(state[...], sign[...])
    blocks[...] = terms[...].reshape(groups * part, cells).T.reshape(blocks.shape)
    hand_out(blocks, outs, lines)


def swapped(block, lines, bits, other):
    pairs = [(2 * i + p, 2 * (i ^ bits) + (p ^ other)) for i in range(lines) for p in range(2)]
    return lax.ppermute(block, ("line", "pair"), pairs)


def reduce_over_cells(blocks, lines):
    count, ways, blocks = fours(lines), ways_of(lines), list(blocks)
    kept, blocks = blocks[:count], blocks[count:]
    near, blocks = blocks[-len(ways) :], blocks[: -len(ways)]
    terms = []
    if count > 1:
        arrived = [swapped(block, lines, *way) for block, way in zip(blocks[:2], ways)]
        for four in range(1, count):
            block = kept[four]
            for part in arrived:
                block = block + part[four - 1].astype(f32)
            block, near[1] = lax.optimization_barrier((block.astype(bf16), near[1]))
            terms.append(swapped(block, lines, 2 * four, 0))
        terms += [swapped(block, lines, 2 * four + 3, 1) for four, block in enumerate(blocks[2:])]
    for way, block in list(zip(ways, near))[2:] + list(zip(ways, near))[:2]:
        terms.append(swapped(block, lines, *way))
    result = kept[0]
    for term in terms:
        result = result + term.astype(f32)
    return result


def shards(adjoint, source, collision, speed, direction, labels, conductance):
    rows, width = adjoint.shape
    lines, pairs, modes = lax.axis_size("line"), lax.axis_size("pair"), lax.axis_size("mode")
    groups = lines * pairs
    part = width // groups
    cells = rows * groups
    depth = modes * part
    shape = jax.ShapeDtypeStruct

    columns = -(-(part + EXTRA) // 128) * 128
    sent = call(
        pack_kernel,
        shape((groups, rows, columns), bf16),
        [],
        [adjoint, labels[None, :], conductance[None, :]],
        [((groups, rows, columns), bf16)],
        own_copies=True,
    )
    got = lax.all_to_all(sent, ("line", "pair"), split_axis=0, concat_axis=0, tiled=True).reshape(cells, columns)

    collision, sent = lax.optimization_barrier((collision, sent))
    flipped, place = call(
        flip_kernel,
        [shape((width, depth + 2 * rows), bf16), shape((2 * rows, cells), bf16)],
        [],
        [collision.reshape(depth, width), adjoint, source],
    )

    start = got[:, :part].T
    full = lax.all_gather(start, "mode", axis=0, tiled=True)
    terms = call(
        first_kernel,
        handed_out(lines, (part, cells)),
        [],
        [flipped, place, full],
        [((groups, part, cells), f32)],
        flops=2 * width * depth * cells,
    )
    start, got, terms = lax.optimization_barrier((start, got, terms))
    transport, rate, sign = call(
        transport_kernel,
        [shape((part, cells), f32), shape((part, cells), f32), shape((part, 1), f32)],
        [],
        [start, jnp.sum(got[:, part:].astype(f32), axis=1)[None, :], speed[None, :], direction[None, :]],
    )
    state = reduce_over_cells(terms, lines) - transport

    full = lax.all_gather(state.astype(bf16), "mode", axis=0, tiled=True)
    terms = call(
        second_kernel,
        handed_out(lines, (rows, width)),
        [],
        [flipped, full, state, rate, sign],
        [((groups, part, cells), f32), ((groups, rows, width), f32)],
        flops=2 * width * depth * cells,
    )
    return reduce_over_cells(terms, lines) + relax_factor * source


def solution(mesh):
    modes, groups = mesh.shape["mode"], mesh.shape["cell"]
    mesh = Mesh(mesh.devices.reshape(modes, groups // 2, 2), ("mode", "line", "pair"))
    cell = ("line", "pair")
    in_specs = (
        P(cell, "mode"),
        P(cell, "mode"),
        P(None, cell, None, "mode"),
        P("mode"),
        P("mode"),
        P(cell),
        P(),
    )
    out_specs = P(cell, "mode")
    return jax.shard_map(shards, mesh=mesh, in_specs=in_specs, out_specs=out_specs, check_vma=False)
```
